256 devices in a mesh: region: 2 (over z_lo), ax: 8 (over x, core), az: 16 (over z_hi, y).
Axes of the slice: x: 4, y: 4, z: 8 (z_hi: 4, z_lo: 2; z = z_hi * 2 + z_lo), core: 2. Of those that a mesh axis runs over, the one named last changes fastest.
Arguments:
- state: float32 [2, 3, 128, 128, 2048], P('region', None, None, 'az', 'ax'), may hold values from -6 to 6
- conduct: float32 [2, 128, 128, 2048], P('region', None, 'az', 'ax'), may hold values from 0.25 to 2
- zones: int32 [2048], P('ax'), may hold values from 0 to 2, never falling along the last dimension, each value on 1 to 1024 neighbouring positions
- placement: int32 [2048], P('ax'), may hold values from 0 to 127
Outputs:
- new_state: float32 [2, 3, 128, 128, 2048], P('region', None, None, 'az', 'ax')
The draws below stay inside these ranges and needn't reach their ends.
Inputs may be any that keep to these rules, and one draw needn't show every extreme that they name: `zones`: 0 evaporator, 1 adiabatic, 2 condenser, never falling along the axis; each zone has 1 to 1024 cells and one has exactly 1024.
All inputs are finite; a program needn't handle non-finite values.
Results may differ from the reference program's by a relative error of at most 0.00002.
Values sent between devices are 32-bit elements; how exact they have to be, the bound alone decides.
A program may use at most 64 MiB of HBM per device.

```python
import math
import jax
import jax.numpy as jnp
import numpy as np

R = 128
NAZ = 128
NX = 2048


def touch_ends(values, own_key, smallest, largest):
    place = [jax.random.randint(jax.random.fold_in(own_key, axis), (), 0, length) for axis, length in enumerate(values.shape)]
    longest = values.shape.index(max(values.shape))
    next_to = place[:longest] + [(place[longest] + 1) % values.shape[longest]] + place[longest + 1:]
    return values.at[tuple(place)].set(smallest).at[tuple(next_to)].set(largest)


def level_of(stream_key, shape, cuts, least, high):
    level = 1.0
    for dim, shards_of in cuts:
        draws = jax.random.uniform(jax.random.fold_in(jax.random.fold_in(stream_key, 6), dim), (shards_of,), jnp.float32, least / len(cuts), high / len(cuts))
        level = level * jnp.repeat(jnp.exp(draws), shape[dim] // shards_of).reshape((-1,) + (1,) * (len(shape) - 1 - dim))
    return level


def split_up(number_of, total, bound, lean):
    weights = [(1 << 20) // math.isqrt(grade ** lean) + 1 for grade in range(2, number_of + 1)]
    surplus, counts = total - bound - (number_of - 1), [1] * (number_of - 1)
    while surplus > 0:
        candidates = [i for i in range(number_of - 1) if counts[i] < bound]
        pool, left = sum([weights[i] for i in candidates]), surplus
        for i in candidates:
            extra = min(bound - counts[i], max(1, left * weights[i] // pool), surplus)
            counts[i] = counts[i] + extra
            surplus = surplus - extra
    return np.array([bound] + counts)


def uneven(rng, count, total, bound, skew):
    if count == 2:
        one = jax.random.randint(rng, (), max(1, total - bound), min(bound, total - 1) + 1)
        return jnp.stack([one, total - one])
    tallies = jnp.asarray(split_up(count, total, bound, skew), jnp.int32)
    couples = (count - 1) // 2
    giver, sink = tallies[1:1 + 2 * couples:2], tallies[2:2 + 2 * couples:2]
    slack = jnp.minimum(giver - 1, bound - sink)
    shifted = jax.random.randint(jax.random.fold_in(rng, 1), (couples,), 0, 1 << 20) % (slack + 1)
    tallies = tallies.at[1:1 + 2 * couples:2].set(giver - shifted).at[2:2 + 2 * couples:2].set(sink + shifted)
    return tallies[jax.random.permutation(jax.random.fold_in(rng, 2), count)]


def gaussian(own_key, shape, deviation, bound, split=(), held_as=jnp.bfloat16):
    loudness = level_of(own_key, shape, split, -0.22, 0.18) if split else 1.0
    result = jax.random.normal(own_key, shape, jnp.float32) * deviation * loudness
    return jnp.minimum(jnp.maximum(result, -bound), bound).astype(held_as)


def setup_inputs(seed: int = 0) -> dict:
    arg_keys = jax.random.split(jax.random.key(seed), 5)
    state = gaussian(arg_keys[0], (2, 3, R, NAZ, NX), 1.0, 6.0, ((0, 2), (3, 16), (4, 8)), jnp.float32)
    conduct = jnp.clip(jnp.exp(math.log(2.0) - 2.0794415 * jax.random.uniform(arg_keys[1], (2, R, NAZ, NX), jnp.float32) ** level_of(arg_keys[1], (2, R, NAZ, NX), ((0, 2), (2, 16), (3, 8)), -0.2, 0.2)), 0.25, 2.0)
    zones = jnp.searchsorted(jnp.cumsum(uneven(arg_keys[2], 3, NX, NX // 2, 0)), jnp.arange(NX), side="right").astype(jnp.int32)
    placement = touch_ends(jax.random.randint(arg_keys[3], (NX,), 0, NAZ), jax.random.fold_in(arg_keys[3], 1), 0, NAZ - 1).astype(jnp.int32)
    return {"state": state, "conduct": conduct, "zones": zones, "placement": placement}


time_step = 0.05
region_coeffs = ((1.0, 0.3, 0.1, 1.5, 0.2, 1.0), (0.6, 0.05, 2.0, 0.8, 0.4, 0.5))


def operators(fields):
    outward = jnp.concatenate([fields[:, 1:], fields[:, -1:]], axis=1)
    inward = jnp.concatenate([fields[:, :1], fields[:, :-1]], axis=1)
    az_plus = jnp.roll(fields, -1, axis=2)
    az_minus = jnp.roll(fields, 1, axis=2)
    zero_col = jnp.zeros_like(fields[..., :1])
    ax_plus = jnp.concatenate([fields[..., 1:], zero_col], axis=3)
    ax_minus = jnp.concatenate([zero_col, fields[..., :-1]], axis=3)
    laplace = outward + inward + az_plus + az_minus + ax_plus + ax_minus - 6.0 * fields
    gradient = 0.5 * (ax_plus - ax_minus)
    return laplace, gradient


def advance(fields, kappa, laplace, gradient, sources, coeffs):
    press_coef, visc_coef, fric_coef, sound_coef, pdiff_coef, advect_coef = coeffs
    temper, press, veloc = fields[0], fields[1], fields[2]
    new_t = temper + time_step * (kappa * laplace[0] - advect_coef * veloc * gradient[0] + sources[0])
    new_p = press + time_step * (-sound_coef * gradient[2] + pdiff_coef * laplace[1] + sources[1])
    new_u = veloc + time_step * (-press_coef * gradient[1] + visc_coef * laplace[2] - fric_coef * veloc + sources[2])
    return jnp.stack([new_t, new_p, new_u])


def facing(layer, shift):
    index = (jnp.arange(NAZ, dtype=jnp.int32)[:, None] + shift[None, :]) % NAZ
    index = jnp.broadcast_to(index[None], layer.shape).astype(jnp.int32)
    return jnp.take_along_axis(layer, index, axis=1)


def reference(state, conduct, zones, placement):
    vapor = state[0]
    wick = state[1]
    vapor_layer = vapor[:, R - 1]
    wick_layer = wick[:, 0]
    placement = placement.astype(jnp.int32)
    wick_seen = facing(wick_layer, placement)
    vapor_seen = facing(vapor_layer, (-placement) % NAZ)
    evap_v = 2.0 * (wick_seen[0] - 0.5 * vapor_layer[1])
    shear_v = 1.5 * (vapor_layer[2] - wick_seen[2])
    evap_w = 2.0 * (wick_layer[0] - 0.5 * vapor_seen[1])
    shear_w = 1.5 * (vapor_seen[2] - wick_layer[2])
    src_vapor = jnp.zeros_like(vapor)
    src_vapor = src_vapor.at[0, R - 1].add(0.5 * evap_v)
    src_vapor = src_vapor.at[1, R - 1].add(evap_v)
    src_vapor = src_vapor.at[2, R - 1].add(-shear_v)
    wall_temp = wick[0, R - 1]
    wall_heat = jnp.where(zones[None, :] == 0, jnp.float32(2.0),
                          jnp.where(zones[None, :] == 2, -1.5 * (wall_temp + 1.0), jnp.float32(0.0)))
    src_wick = jnp.zeros_like(wick)
    src_wick = src_wick.at[0, 0].add(-evap_w)
    src_wick = src_wick.at[1, 0].add(-0.5 * evap_w)
    src_wick = src_wick.at[2, 0].add(0.5 * shear_w)
    src_wick = src_wick.at[0, R - 1].add(wall_heat)
    lap_v, grad_v = operators(vapor)
    lap_w, grad_w = operators(wick)
    new_vapor = advance(vapor, conduct[0], lap_v, grad_v, src_vapor, region_coeffs[0])
    new_wick = advance(wick, conduct[1], lap_w, grad_w, src_wick, region_coeffs[1])
    return jnp.stack([new_vapor, new_wick])
```

```python
import functools
import jax
import jax.numpy as jnp
from jax import lax
from jax.experimental import pallas as pl
from jax.experimental.pallas import tpu as pltpu
from jax.sharding import PartitionSpec as P

MESH = pl.DeviceIdType.MESH
dt = 0.05
chunks = 8
unroll = 4


def step_kernel(
    state, conduct, zone_ref, place_ref, out,
    zones, placement, cells, kappa, below, above, packed, sides, strips, turned, facing,
    load_sem, edge_send, edge_recv, side_send, side_recv, strip_send, strip_recv,
    turn_send, turn_recv, ready,
):
    region = lax.axis_index("region")
    ax = lax.axis_index("ax")
    az = lax.axis_index("az")
    n_az = lax.axis_size("az")
    n_ax = lax.axis_size("ax")
    radial = state.shape[1]
    rows = radial // chunks
    is_vapor = region == 0
    nxt = lax.rem(az + 1, n_az)
    prv = lax.rem(az + n_az - 1, n_az)
    odd = lax.rem(ax, 2) == 1
    has_left = ax > 0
    has_right = ax < n_ax - 1
    is_worker = az < 4
    order = 2 * az + region
    iface = jnp.where(is_vapor, radial - 1, 0)
    next_later = jnp.logical_and(az != 11, az != 15)
    prev_later = jnp.logical_or(az == 0, az == 12)
    next_first = jnp.logical_not(next_later)
    prev_first = jnp.logical_not(prev_later)

    def signal(sem, **device):
        pl.semaphore_signal(sem, inc=1, device_id=device, device_id_type=MESH)

    def remote(src, dst, send, recv, **device):
        return pltpu.make_async_remote_copy(
            src_ref=src, dst_ref=dst, send_sem=send, recv_sem=recv,
            device_id=device, device_id_type=MESH,
        )

    barrier = pltpu.get_barrier_semaphore()
    pl.when(next_later)(lambda: signal(barrier, az=nxt))
    pl.when(prev_later)(lambda: signal(barrier, az=prv))
    pl.when(odd)(lambda: signal(barrier, ax=ax - 1))
    pl.when(jnp.logical_and(odd, has_right))(lambda: signal(barrier, ax=ax + 1))

    load_cells = pltpu.make_async_copy(state, cells, load_sem.at[0])
    load_kappa = pltpu.make_async_copy(conduct, kappa, load_sem.at[1])
    load_zones = pltpu.make_async_copy(zone_ref, zones, load_sem.at[2])
    load_place = pltpu.make_async_copy(place_ref, placement, load_sem.at[3])
    loads = [load_cells, load_kappa, load_zones, load_place]
    for c in loads:
        c.start()

    @pl.when(is_worker)
    def _():
        for other in range(8):
            pl.when(other > order)(
                functools.partial(signal, barrier, az=other // 2, region=other % 2)
            )

        @pl.loop(4, n_az)
        def _(j):
            signal(barrier, az=j, region=0)
            signal(barrier, az=j, region=1)

    count = (
        next_first.astype(jnp.int32)
        + prev_first.astype(jnp.int32)
        + jnp.where(odd, 0, 1 + has_left.astype(jnp.int32))
        + jnp.minimum(order, 8)
    )
    pl.when(count > 0)(lambda: pl.semaphore_wait(barrier, count))

    pl.when(next_first)(lambda: signal(ready.at[1], az=nxt))
    pl.when(prev_first)(lambda: signal(ready.at[0], az=prv))

    strip_copies = []
    for q in range(4):
        field = 1 - region if q < 2 else 2
        strip_copies.append(
            remote(
                state.at[field, iface, :, pl.ds(128 * (q % 2), 128)],
                strips.at[az],
                strip_send,
                strip_recv,
                az=q,
                region=1 - region,
            )
        )

    @pl.when(jnp.logical_not(is_worker))
    def _():
        for c in strip_copies:
            c.start()

    up, down = [], []
    for c in range(chunks):
        part = pl.ds(c * rows, rows)
        up.append(
            remote(
                state.at[:, part, pl.ds(7, 1), :], below.at[:, part],
                edge_send.at[0, c], edge_recv.at[0, c], az=nxt,
            )
        )
        down.append(
            remote(
                state.at[:, part, pl.ds(0, 1), :], above.at[:, part],
                edge_send.at[1, c], edge_recv.at[1, c], az=prv,
            )
        )

    def start_all(copies):
        for c in copies:
            c.start()

    @pl.when(next_first)
    def _():
        start_all(up)

    @pl.when(prev_first)
    def _():
        start_all(down)

    @pl.when(jnp.logical_not(odd))
    def _():
        signal(ready.at[2], ax=ax + 1)
        pl.when(has_left)(lambda: signal(ready.at[3], ax=ax - 1))

    @pl.when(jnp.logical_not(is_worker))
    def _():
        for q in range(4):
            signal(ready.at[4], az=q)

    @pl.when(is_worker)
    def _():
        for other in range(8):
            @pl.when(other < order)
            def _():
                same = region == other % 2
                pl.when(same)(functools.partial(signal, ready.at[4], az=other // 2))
                pl.when(jnp.logical_not(same))(
                    functools.partial(
                        signal, ready.at[5], az=other // 2, region=other % 2
                    )
                )

    @pl.when(next_later)
    def _():
        pl.semaphore_wait(ready.at[0], 1)
        start_all(up)

    @pl.when(is_worker)
    def _():
        later = jnp.where(is_vapor, 4 - az, 3 - az)
        pl.when(later > 0)(lambda: pl.semaphore_wait(ready.at[5], later))
        for c in strip_copies:
            c.start()

    for c in loads:
        c.wait()

    lane = lax.broadcasted_iota(jnp.int32, (8, 128), 1)
    first_lane = lane == 0
    last_lane = lane == 127
    sub = lax.broadcasted_iota(jnp.int32, (8, 128), 0)
    first_row = sub == 0
    last_row = sub == 7

    def pack(r, held):
        mine = lane == r
        got = []
        for f in range(3):
            left = pltpu.roll(cells[f, r, :, :128], r, 1)
            right = pltpu.roll(cells[f, r, :, 128:], lax.rem(r + 1, 128), 1)
            got.append(jnp.where(mine, left, held[2 * f]))
            got.append(jnp.where(mine, right, held[2 * f + 1]))
        return tuple(got)

    columns = lax.fori_loop(
        0, radial, pack, tuple(jnp.zeros((8, 128), jnp.float32) for _ in range(6)), unroll=4
    )
    for f in range(3):
        packed[0, f] = columns[2 * f]
        packed[1, f] = columns[2 * f + 1]

    to_left = remote(packed.at[0], sides.at[1], side_send.at[0], side_recv.at[1], ax=ax - 1)
    to_right = remote(packed.at[1], sides.at[0], side_send.at[1], side_recv.at[0], ax=ax + 1)

    @pl.when(has_left)
    def _():
        pl.when(odd)(lambda: pl.semaphore_wait(ready.at[2], 1))
        to_left.start()

    @pl.when(has_right)
    def _():
        pl.when(odd)(lambda: pl.semaphore_wait(ready.at[3], 1))
        to_right.start()

    @pl.when(prev_later)
    def _():
        pl.semaphore_wait(ready.at[1], 1)
        start_all(down)

    turn_copies = [
        remote(turned.at[j], facing.at[az], turn_send, turn_recv.at[az], az=j)
        for j in range(16)
    ]

    @pl.when(is_worker)
    def _():
        remote(strips, strips, strip_send, strip_recv, az=az).wait_recv()
        half = lax.rem(az, 2)
        shift = placement[pl.ds(half, 1), :]
        shift = jnp.where(is_vapor, shift, lax.rem(128 - shift, 128))
        circle = strips[...].reshape(128, 128)
        for bit in range(7):
            step = 1 << bit
            if step < 8:
                rolled = pltpu.roll(circle, 128 - step, 0)
            else:
                rolled = jnp.concatenate([circle[step:], circle[:step]], axis=0)
            circle = jnp.where(lax.rem(lax.div(shift, step), 2) == 1, rolled, circle)
        turned[...] = circle.reshape(16, 8, 128)
        facing[az] = turned[az]
        pl.semaphore_wait(ready.at[4], 15 - az)
        for j in range(16):
            pl.when(j != az)(turn_copies[j].start)

    @pl.when(has_left)
    def _():
        to_right.wait_recv()

    @pl.when(jnp.logical_not(has_left))
    def _():
        sides[0] = jnp.zeros((3, 8, 128), jnp.float32)

    @pl.when(has_right)
    def _():
        to_left.wait_recv()

    @pl.when(jnp.logical_not(has_right))
    def _():
        sides[1] = jnp.zeros((3, 8, 128), jnp.float32)

    def pick(vapor, wick):
        return jnp.where(is_vapor, jnp.float32(vapor), jnp.float32(wick))

    press = pick(1.0, 0.6)
    visc = pick(0.3, 0.05)
    fric = pick(0.1, 2.0)
    sound = pick(1.5, 0.8)
    pdiff = pick(0.2, 0.4)
    advect = pick(1.0, 0.5)

    def cell_row(r):
        inner = jnp.maximum(r - 1, 0)
        outer = jnp.minimum(r + 1, radial - 1)
        to_last = lax.rem(255 - r, 128)
        to_first = lax.rem(128 - r, 128)
        center, laplace, gradient = [], [], []
        for f in range(3):
            c = [cells[f, r, :, :128], cells[f, r, :, 128:]]
            plus = [pltpu.roll(c[0], 127, 1), pltpu.roll(c[1], 127, 1)]
            minus = [pltpu.roll(c[0], 1, 1), pltpu.roll(c[1], 1, 1)]
            from_right = pltpu.roll(sides[1, f], to_last, 1)
            from_left = pltpu.roll(sides[0, f], to_first, 1)
            ax_plus = [
                jnp.where(last_lane, plus[1], plus[0]),
                jnp.where(last_lane, from_right, plus[1]),
            ]
            ax_minus = [
                jnp.where(first_lane, from_left, minus[0]),
                jnp.where(first_lane, minus[0], minus[1]),
            ]
            laps, grads = [], []
            for h in range(2):
                lanes = pl.ds(128 * h, 128)
                az_plus = jnp.where(
                    last_row, above[f, r, :, lanes], pltpu.roll(c[h], 7, 0)
                )
                az_minus = jnp.where(
                    first_row, below[f, r, :, lanes], pltpu.roll(c[h], 1, 0)
                )
                laps.append(
                    cells[f, outer, :, lanes] + cells[f, inner, :, lanes]
                    + az_plus + az_minus + ax_plus[h] + ax_minus[h] - 6.0 * c[h]
                )
                grads.append(0.5 * (ax_plus[h] - ax_minus[h]))
            center.append(c)
            laplace.append(laps)
            gradient.append(grads)
        for h in range(2):
            lanes = pl.ds(128 * h, 128)
            t, p, u = center[0][h], center[1][h], center[2][h]
            out[0, r, :, lanes] = t + dt * (
                kappa[r, :, lanes] * laplace[0][h] - advect * u * gradient[0][h]
            )
            out[1, r, :, lanes] = p + dt * (
                -sound * gradient[2][h] + pdiff * laplace[1][h]
            )
            out[2, r, :, lanes] = u + dt * (
                -press * gradient[1][h] + visc * laplace[2][h] - fric * u
            )

    for c in range(chunks):
        up[c].wait_recv()
        down[c].wait_recv()

        @pl.loop(0, rows // unroll)
        def _(i):
            for k in range(unroll):
                cell_row(c * rows + i * unroll + k)

    for q in range(4):
        pl.when(az != q)(
            remote(facing.at[q], facing.at[q], turn_send, turn_recv.at[q], az=q).wait_recv
        )

    for h in range(2):
        lanes = pl.ds(128 * h, 128)
        own_t, own_p, own_u = [cells[f, iface, :, lanes] for f in range(3)]
        first, second = facing[h], facing[2 + h]
        t_wick = jnp.where(is_vapor, first, own_t)
        p_vapor = jnp.where(is_vapor, own_p, first)
        u_vapor = jnp.where(is_vapor, own_u, second)
        u_wick = jnp.where(is_vapor, second, own_u)
        evap = 2.0 * (t_wick - 0.5 * p_vapor)
        shear = 1.5 * (u_vapor - u_wick)
        out[0, iface, :, lanes] += dt * jnp.where(is_vapor, 0.5 * evap, -evap)
        out[1, iface, :, lanes] += dt * jnp.where(is_vapor, evap, -0.5 * evap)
        out[2, iface, :, lanes] += dt * jnp.where(is_vapor, -shear, 0.5 * shear)
        zone = jnp.broadcast_to(zones[pl.ds(h, 1), :], (8, 128))
        wall = cells[0, radial - 1, :, lanes]
        heat = jnp.where(
            zone == 0, jnp.float32(2.0), jnp.where(zone == 2, -1.5 * (wall + 1.0), 0.0)
        )
        out[0, radial - 1, :, lanes] += dt * jnp.where(is_vapor, 0.0, heat)

    for c in range(chunks):
        up[c].wait_send()
        down[c].wait_send()
    pl.when(has_left)(to_left.wait_send)
    pl.when(has_right)(to_right.wait_send)
    four = strips.at[pl.ds(0, 4)]
    remote(four, four, strip_send, strip_recv, az=az).wait_send()

    @pl.when(is_worker)
    def _():
        rest = turned.at[pl.ds(0, 15)]
        remote(rest, rest, turn_send, turn_recv.at[0], az=az).wait_send()


def store_kernel(new, out, sems):
    copies = [
        pltpu.make_async_copy(new.at[f], out.at[f], sems.at[f]) for f in range(3)
    ]
    for c in copies:
        c.start()
    for c in copies:
        c.wait()


def on_device(state, conduct, zones, placement):
    fields = state[0]
    f32 = jnp.float32
    shape = fields.shape
    radial, az_cells, ax_cells = shape[1:]
    hbm = pl.BlockSpec(memory_space=pltpu.HBM)
    vmem = pl.BlockSpec(memory_space=pltpu.VMEM)
    dma = pltpu.SemaphoreType.DMA
    new = pl.pallas_call(
        step_kernel,
        out_shape=jax.ShapeDtypeStruct(shape, f32),
        in_specs=[hbm] * 4,
        out_specs=vmem,
        scratch_shapes=[
            pltpu.VMEM((2, 128), jnp.int32),
            pltpu.VMEM((2, 128), jnp.int32),
            pltpu.VMEM(shape, f32),
            pltpu.VMEM(shape[1:], f32),
            pltpu.VMEM((3, radial, 1, ax_cells), f32),
            pltpu.VMEM((3, radial, 1, ax_cells), f32),
            pltpu.VMEM((2, 3, 8, 128), f32),
            pltpu.VMEM((2, 3, 8, 128), f32),
            pltpu.VMEM((16, 8, 128), f32),
            pltpu.VMEM((16, 8, 128), f32),
            pltpu.VMEM((4, 8, 128), f32),
            dma((4,)),
            dma((2, chunks)),
            dma((2, chunks)),
            dma((2,)),
            dma((2,)),
            dma,
            dma,
            dma,
            dma((4,)),
            pltpu.SemaphoreType.REGULAR((6,)),
        ],
        compiler_params=pltpu.CompilerParams(
            collective_id=0, has_side_effects=True, vmem_limit_bytes=60 << 20
        ),
        cost_estimate=pl.CostEstimate(
            flops=40 * fields.size, bytes_accessed=4 * 7 * conduct.size, transcendentals=0
        ),
    )(fields, conduct[0], zones.reshape(2, 128), placement.reshape(2, 128))
    result = pl.pallas_call(
        store_kernel,
        out_shape=jax.ShapeDtypeStruct(shape, f32),
        in_specs=[vmem],
        out_specs=hbm,
        scratch_shapes=[dma((3,))],
    )(new)
    return result[None]


def solution(mesh):
    return jax.shard_map(
        on_device,
        mesh=mesh,
        in_specs=(
            P("region", None, None, "az", "ax"),
            P("region", None, "az", "ax"),
            P("ax"),
            P("ax"),
        ),
        out_specs=P("region", None, None, "az", "ax"),
        check_vma=False,
    )
```

```python
import functools
import jax
import jax.numpy as jnp
from jax import lax
from jax.experimental import pallas as pl
from jax.experimental.pallas import tpu as pltpu
from jax.sharding import PartitionSpec as P

MESH = pl.DeviceIdType.MESH
dt = 0.05
chunks = 8
unroll = 4


def step_kernel(
    state, conduct, zone_ref, place_ref, out,
    zones, placement, cells, kappa, below, above, packed, sides, strips, turned, facing,
    load_sem, edge_send, edge_recv, side_send, side_recv, strip_send, strip_recv,
    turn_send, turn_recv, ready,
):
    region = lax.axis_index("region")
    ax = lax.axis_index("ax")
    az = lax.axis_index("az")
    n_az = lax.axis_size("az")
    n_ax = lax.axis_size("ax")
    radial = state.shape[1]
    rows = radial // chunks
    is_vapor = region == 0
    nxt = lax.rem(az + 1, n_az)
    prv = lax.rem(az + n_az - 1, n_az)
    odd = lax.rem(ax, 2) == 1
    has_left = ax > 0
    has_right = ax < n_ax - 1
    is_worker = az < 4
    order = 2 * az + region
    iface = jnp.where(is_vapor, radial - 1, 0)
    next_later = jnp.logical_and(az != 11, az != 15)
    prev_later = jnp.logical_or(az == 0, az == 12)
    next_first = jnp.logical_not(next_later)
    prev_first = jnp.logical_not(prev_later)

    def signal(sem, **device):
        pl.semaphore_signal(sem, inc=1, device_id=device, device_id_type=MESH)

    def remote(src, dst, send, recv, **device):
        return pltpu.make_async_remote_copy(
            src_ref=src, dst_ref=dst, send_sem=send, recv_sem=recv,
            device_id=device, device_id_type=MESH,
        )

    barrier = pltpu.get_barrier_semaphore()
    pl.when(next_later)(lambda: signal(barrier, az=nxt))
    pl.when(prev_later)(lambda: signal(barrier, az=prv))
    pl.when(odd)(lambda: signal(barrier, ax=ax - 1))
    pl.when(jnp.logical_and(odd, has_right))(lambda: signal(barrier, ax=ax + 1))

    load_cells = pltpu.make_async_copy(state, cells, load_sem.at[0])
    load_kappa = pltpu.make_async_copy(conduct, kappa, load_sem.at[1])
    load_zones = pltpu.make_async_copy(zone_ref, zones, load_sem.at[2])
    load_place = pltpu.make_async_copy(place_ref, placement, load_sem.at[3])
    loads = [load_cells, load_kappa, load_zones, load_place]
    for c in loads:
        c.start()

    @pl.when(is_worker)
    def _():
        for other in range(8):
            pl.when(other > order)(
                functools.partial(signal, barrier, az=other // 2, region=other % 2)
            )

        @pl.loop(4, n_az)
        def _(j):
            signal(barrier, az=j, region=0)
            signal(barrier, az=j, region=1)

    count = (
        next_first.astype(jnp.int32)
        + prev_first.astype(jnp.int32)
        + jnp.where(odd, 0, 1 + has_left.astype(jnp.int32))
        + jnp.minimum(order, 8)
    )
    pl.when(count > 0)(lambda: pl.semaphore_wait(barrier, count))

    pl.when(next_first)(lambda: signal(ready.at[1], az=nxt))
    pl.when(prev_first)(lambda: signal(ready.at[0], az=prv))

    strip_copies = []
    for q in range(4):
        field = 1 - region if q < 2 else 2
        strip_copies.append(
            remote(
                state.at[field, iface, :, pl.ds(128 * (q % 2), 128)],
                strips.at[az],
                strip_send,
                strip_recv,
                az=q,
                region=1 - region,
            )
        )

    @pl.when(jnp.logical_not(is_worker))
    def _():
        for c in strip_copies:
            c.start()

    up, down = [], []
    for c in range(chunks):
        part = pl.ds(c * rows, rows)
        up.append(
            remote(
                state.at[:, part, pl.ds(7, 1), :], below.at[:, part],
                edge_send.at[0, c], edge_recv.at[0, c], az=nxt,
            )
        )
        down.append(
            remote(
                state.at[:, part, pl.ds(0, 1), :], above.at[:, part],
                edge_send.at[1, c], edge_recv.at[1, c], az=prv,
            )
        )

    def start_all(copies):
        for c in copies:
            c.start()

    @pl.when(next_first)
    def _():
        start_all(up)

    @pl.when(prev_first)
    def _():
        start_all(down)

    @pl.when(jnp.logical_not(odd))
    def _():
        signal(ready.at[2], ax=ax + 1)
        pl.when(has_left)(lambda: signal(ready.at[3], ax=ax - 1))

    @pl.when(jnp.logical_not(is_worker))
    def _():
        for q in range(4):
            signal(ready.at[4], az=q)

    @pl.when(is_worker)
    def _():
        for other in range(8):
            @pl.when(other < order)
            def _():
                same = region == other % 2
                pl.when(same)(functools.partial(signal, ready.at[4], az=other // 2))
                pl.when(jnp.logical_not(same))(
                    functools.partial(
                        signal, ready.at[5], az=other // 2, region=other % 2
                    )
                )

    @pl.when(next_later)
    def _():
        pl.semaphore_wait(ready.at[0], 1)
        start_all(up)

    @pl.when(is_worker)
    def _():
        later = jnp.where(is_vapor, 4 - az, 3 - az)
        pl.when(later > 0)(lambda: pl.semaphore_wait(ready.at[5], later))
        for c in strip_copies:
            c.start()

    for c in loads:
        c.wait()

    lane = lax.broadcasted_iota(jnp.int32, (8, 128), 1)
    first_lane = lane == 0
    last_lane = lane == 127
    sub = lax.broadcasted_iota(jnp.int32, (8, 128), 0)
    first_row = sub == 0
    last_row = sub == 7

    def pack(r, held):
        mine = lane == r
        got = []
        for f in range(3):
            left = pltpu.roll(cells[f, r, :, :128], r, 1)
            right = pltpu.roll(cells[f, r, :, 128:], lax.rem(r + 1, 128), 1)
            got.append(jnp.where(mine, left, held[2 * f]))
            got.append(jnp.where(mine, right, held[2 * f + 1]))
        return tuple(got)

    columns = lax.fori_loop(
        0, radial, pack, tuple(jnp.zeros((8, 128), jnp.float32) for _ in range(6)), unroll=4
    )
    for f in range(3):
        packed[0, f] = columns[2 * f]
        packed[1, f] = columns[2 * f + 1]

    to_left = remote(packed.at[0], sides.at[1], side_send.at[0], side_recv.at[1], ax=ax - 1)
    to_right = remote(packed.at[1], sides.at[0], side_send.at[1], side_recv.at[0], ax=ax + 1)

    @pl.when(has_left)
    def _():
        pl.when(odd)(lambda: pl.semaphore_wait(ready.at[2], 1))
        to_left.start()

    @pl.when(has_right)
    def _():
        pl.when(odd)(lambda: pl.semaphore_wait(ready.at[3], 1))
        to_right.start()

    @pl.when(prev_later)
    def _():
        pl.semaphore_wait(ready.at[1], 1)
        start_all(down)

    turn_copies = [
        remote(turned.at[j], facing.at[az], turn_send, turn_recv.at[az], az=j)
        for j in range(16)
    ]

    @pl.when(is_worker)
    def _():
        remote(strips, strips, strip_send, strip_recv, az=az).wait_recv()
        half = lax.rem(az, 2)
        shift = placement[pl.ds(half, 1), :]
        shift = jnp.where(is_vapor, shift, lax.rem(128 - shift, 128))
        circle = strips[...].reshape(128, 128)
        for bit in range(7):
            step = 1 << bit
            if step < 8:
                rolled = pltpu.roll(circle, 128 - step, 0)
            else:
                rolled = jnp.concatenate([circle[step:], circle[:step]], axis=0)
            circle = jnp.where(lax.rem(lax.div(shift, step), 2) == 1, rolled, circle)
        turned[...] = circle.reshape(16, 8, 128)
        facing[az] = turned[az]
        pl.semaphore_wait(ready.at[4], 15 - az)
        for j in range(16):
            pl.when(j != az)(turn_copies[j].start)

    @pl.when(has_left)
    def _():
        to_right.wait_recv()

    @pl.when(jnp.logical_not(has_left))
    def _():
        sides[0] = jnp.zeros((3, 8, 128), jnp.float32)

    @pl.when(has_right)
    def _():
        to_left.wait_recv()

    @pl.when(jnp.logical_not(has_right))
    def _():
        sides[1] = jnp.zeros((3, 8, 128), jnp.float32)

    def pick(vapor, wick):
        return jnp.where(is_vapor, jnp.float32(vapor), jnp.float32(wick))

    press = pick(1.0, 0.6)
    visc = pick(0.3, 0.05)
    fric = pick(0.1, 2.0)
    sound = pick(1.5, 0.8)
    pdiff = pick(0.2, 0.4)
    advect = pick(1.0, 0.5)

    def cell_row(r):
        inner = jnp.maximum(r - 1, 0)
        outer = jnp.minimum(r + 1, radial - 1)
        to_last = lax.rem(255 - r, 128)
        to_first = lax.rem(128 - r, 128)
        center, laplace, gradient = [], [], []
        for f in range(3):
            c = [cells[f, r, :, :128], cells[f, r, :, 128:]]
            plus = [pltpu.roll(c[0], 127, 1), pltpu.roll(c[1], 127, 1)]
            minus = [pltpu.roll(c[0], 1, 1), pltpu.roll(c[1], 1, 1)]
            from_right = pltpu.roll(sides[1, f], to_last, 1)
            from_left = pltpu.roll(sides[0, f], to_first, 1)
            ax_plus = [
                jnp.where(last_lane, plus[1], plus[0]),
                jnp.where(last_lane, from_right, plus[1]),
            ]
            ax_minus = [
                jnp.where(first_lane, from_left, minus[0]),
                jnp.where(first_lane, minus[0], minus[1]),
            ]
            laps, grads = [], []
            for h in range(2):
                lanes = pl.ds(128 * h, 128)
                az_plus = jnp.where(
                    last_row, above[f, r, :, lanes], pltpu.roll(c[h], 7, 0)
                )
                az_minus = jnp.where(
                    first_row, below[f, r, :, lanes], pltpu.roll(c[h], 1, 0)
                )
                laps.append(
                    cells[f, outer, :, lanes] + cells[f, inner, :, lanes]
                    + az_plus + az_minus + ax_plus[h] + ax_minus[h] - 6.0 * c[h]
                )
                grads.append(0.5 * (ax_plus[h] - ax_minus[h]))
            center.append(c)
            laplace.append(laps)
            gradient.append(grads)
        for h in range(2):
            lanes = pl.ds(128 * h, 128)
            t, p, u = center[0][h], center[1][h], center[2][h]
            out[0, r, :, lanes] = t + dt * (
                kappa[r, :, lanes] * laplace[0][h] - advect * u * gradient[0][h]
            )
            out[1, r, :, lanes] = p + dt * (
                -sound * gradient[2][h] + pdiff * laplace[1][h]
            )
            out[2, r, :, lanes] = u + dt * (
                -press * gradient[1][h] + visc * laplace[2][h] - fric * u
            )

    for c in range(chunks):
        up[c].wait_recv()
        down[c].wait_recv()

        @pl.loop(0, rows // unroll)
        def _(i):
            for k in range(unroll):
                cell_row(c * rows + i * unroll + k)

    for q in range(4):
        pl.when(az != q)(
            remote(facing.at[q], facing.at[q], turn_send, turn_recv.at[q], az=q).wait_recv
        )

    for h in range(2):
        lanes = pl.ds(128 * h, 128)
        own_t, own_p, own_u = [cells[f, iface, :, lanes] for f in range(3)]
        first, second = facing[h], facing[2 + h]
        t_wick = jnp.where(is_vapor, first, own_t)
        p_vapor = jnp.where(is_vapor, own_p, first)
        u_vapor = jnp.where(is_vapor, own_u, second)
        u_wick = jnp.where(is_vapor, second, own_u)
        evap = 2.0 * (t_wick - 0.5 * p_vapor)
        shear = 1.5 * (u_vapor - u_wick)
        out[0, iface, :, lanes] += dt * jnp.where(is_vapor, 0.5 * evap, -evap)
        out[1, iface, :, lanes] += dt * jnp.where(is_vapor, evap, -0.5 * evap)
        out[2, iface, :, lanes] += dt * jnp.where(is_vapor, -shear, 0.5 * shear)
        zone = jnp.broadcast_to(zones[pl.ds(h, 1), :], (8, 128))
        wall = cells[0, radial - 1, :, lanes]
        heat = jnp.where(
            zone == 0, jnp.float32(2.0), jnp.where(zone == 2, -1.5 * (wall + 1.0), 0.0)
        )
        out[0, radial - 1, :, lanes] += dt * jnp.where(is_vapor, 0.0, heat)

    for c in range(chunks):
        up[c].wait_send()
        down[c].wait_send()
    pl.when(has_left)(to_left.wait_send)
    pl.when(has_right)(to_right.wait_send)
    four = strips.at[pl.ds(0, 4)]
    remote(four, four, strip_send, strip_recv, az=az).wait_send()

    @pl.when(is_worker)
    def _():
        rest = turned.at[pl.ds(0, 15)]
        remote(rest, rest, turn_send, turn_recv.at[0], az=az).wait_send()


def store_kernel(new, out, sems):
    copies = [
        pltpu.make_async_copy(new.at[f], out.at[f], sems.at[f]) for f in range(3)
    ]
    for c in copies:
        c.start()
    for c in copies:
        c.wait()


def on_device(state, conduct, zones, placement):
    fields = state[0]
    f32 = jnp.float32
    shape = fields.shape
    radial, az_cells, ax_cells = shape[1:]
    hbm = pl.BlockSpec(memory_space=pltpu.HBM)
    vmem = pl.BlockSpec(memory_space=pltpu.VMEM)
    dma = pltpu.SemaphoreType.DMA
    new = pl.pallas_call(
        step_kernel,
        out_shape=pltpu.VMEM(shape, f32),
        in_specs=[hbm] * 4,
        out_specs=vmem,
        scratch_shapes=[
            pltpu.VMEM((2, 128), jnp.int32),
            pltpu.VMEM((2, 128), jnp.int32),
            pltpu.VMEM(shape, f32),
            pltpu.VMEM(shape[1:], f32),
            pltpu.VMEM((3, radial, 1, ax_cells), f32),
            pltpu.VMEM((3, radial, 1, ax_cells), f32),
            pltpu.VMEM((2, 3, 8, 128), f32),
            pltpu.VMEM((2, 3, 8, 128), f32),
            pltpu.VMEM((16, 8, 128), f32),
            pltpu.VMEM((16, 8, 128), f32),
            pltpu.VMEM((4, 8, 128), f32),
            dma((4,)),
            dma((2, chunks)),
            dma((2, chunks)),
            dma((2,)),
            dma((2,)),
            dma,
            dma,
            dma,
            dma((4,)),
            pltpu.SemaphoreType.REGULAR((6,)),
        ],
        compiler_params=pltpu.CompilerParams(
            collective_id=0, has_side_effects=True, vmem_limit_bytes=24 << 20
        ),
        cost_estimate=pl.CostEstimate(
            flops=40 * fields.size, bytes_accessed=4 * 7 * conduct.size, transcendentals=0
        ),
    )(*(
        pltpu.with_memory_space_constraint(x, pltpu.HBM)
        for x in (fields, conduct[0], zones.reshape(2, 128), placement.reshape(2, 128))
    ))
    result = pl.pallas_call(
        store_kernel,
        out_shape=jax.ShapeDtypeStruct(shape, f32),
        in_specs=[vmem],
        out_specs=hbm,
        scratch_shapes=[dma((3,))],
        compiler_params=pltpu.CompilerParams(vmem_limit_bytes=1 << 20),
    )(pltpu.with_memory_space_constraint(new, pltpu.VMEM))
    return result[None]


def solution(mesh):
    return jax.shard_map(
        on_device,
        mesh=mesh,
        in_specs=(
            P("region", None, None, "az", "ax"),
            P("region", None, "az", "ax"),
            P("ax"),
            P("ax"),
        ),
        out_specs=P("region", None, None, "az", "ax"),
        check_vma=False,
    )
```

```python
import functools
import jax
import jax.numpy as jnp
from jax import lax
from jax.experimental import pallas as pl
from jax.experimental.pallas import tpu as pltpu
from jax.sharding import PartitionSpec as P

MESH = pl.DeviceIdType.MESH
dt = 0.05
chunks = 8
unroll = 8


def step_kernel(
    state, conduct, zone_ref, place_ref, out,
    zones, placement, cells, kappa, edges, hop, packed, sides, strips, turned, facing,
    load_sem, edge_send, edge_recv, hop_send, hop_recv, side_send, side_recv,
    strip_send, strip_recv, turn_send, turn_recv, ready,
):
    region = lax.axis_index("region")
    ax = lax.axis_index("ax")
    az = lax.axis_index("az")
    n_az = lax.axis_size("az")
    n_ax = lax.axis_size("ax")
    radial = state.shape[1]
    rows = radial // chunks
    is_vapor = region == 0
    y = lax.rem(az, 4)
    nxt = lax.rem(az + 1, n_az)
    prv = lax.rem(az + n_az - 1, n_az)
    odd = lax.rem(ax, 2) == 1
    has_left = ax > 0
    has_right = ax < n_ax - 1
    is_worker = jnp.logical_or(az == 1, az == 2)
    order = 2 * az + region
    iface = jnp.where(is_vapor, radial - 1, 0)
    next_later = jnp.logical_and(az != 11, az != 15)
    prev_later = jnp.logical_or(az == 0, az == 12)
    next_first = jnp.logical_not(next_later)
    prev_first = jnp.logical_not(prev_later)
    y_first = y == 0
    y_last = y == 3

    def signal(sem, **device):
        pl.semaphore_signal(sem, inc=1, device_id=device, device_id_type=MESH)

    def remote(src, dst, send, recv, **device):
        return pltpu.make_async_remote_copy(
            src_ref=src, dst_ref=dst, send_sem=send, recv_sem=recv,
            device_id=device, device_id_type=MESH,
        )

    barrier = pltpu.get_barrier_semaphore()
    pl.when(next_later)(lambda: signal(barrier, az=nxt))
    pl.when(prev_later)(lambda: signal(barrier, az=prv))
    pl.when(y_first)(lambda: signal(barrier, az=az + 3))
    pl.when(odd)(lambda: signal(barrier, ax=ax - 1))
    pl.when(jnp.logical_and(odd, has_right))(lambda: signal(barrier, ax=ax + 1))

    loads = [
        pltpu.make_async_copy(src, dst, load_sem.at[i])
        for i, (src, dst) in enumerate(
            ((state, cells), (conduct, kappa), (zone_ref, zones), (place_ref, placement))
        )
    ]
    for c in loads:
        c.start()

    @pl.when(az < 3)
    def _():
        for other in range(2, 6):
            pl.when(other > order)(
                functools.partial(signal, barrier, az=other // 2, region=other % 2)
            )

    @pl.when(is_worker)
    def _():
        @pl.loop(3, n_az)
        def _(j):
            signal(barrier, az=j, region=0)
            signal(barrier, az=j, region=1)

    count = (
        next_first.astype(jnp.int32)
        + prev_first.astype(jnp.int32)
        + y_last.astype(jnp.int32)
        + jnp.where(odd, 0, 1 + has_left.astype(jnp.int32))
        + jnp.where(az == 0, 0, jnp.where(is_worker, order, 4))
    )
    pl.when(count > 0)(lambda: pl.semaphore_wait(barrier, count))

    pl.when(next_first)(lambda: signal(ready.at[1], az=nxt))
    pl.when(prev_first)(lambda: signal(ready.at[0], az=prv))
    pl.when(y_last)(lambda: signal(ready.at[6], az=az - 3))

    strip_copies = [
        remote(
            state.at[1 - region if q == 0 else 2, iface],
            strips.at[az],
            strip_send,
            strip_recv,
            az=1 + q,
            region=1 - region,
        )
        for q in range(2)
    ]

    @pl.when(az > 2)
    def _():
        for c in strip_copies:
            c.start()

    far = (y_last, y_first)
    neighbour = (nxt, prv)
    other_end = (az - 3, az + 3)

    def edge_source(d, c):
        return state.at[:, pl.ds(c * rows, rows), pl.ds(7 - 7 * d, 1), :]

    def edge_copy(d, c):
        return remote(
            edge_source(d, c), edges.at[d, :, pl.ds(c * rows, rows)],
            edge_send.at[d, c], edge_recv.at[d, c], az=neighbour[d],
        )

    def detour_copy(d, i):
        c = 2 * i + 1
        return remote(
            edge_source(d, c), hop.at[i], edge_send.at[d, c], hop_recv.at[i], az=other_end[d]
        )

    def onward_copy(d, i):
        c = 2 * i + 1
        return remote(
            hop.at[i], edges.at[d, :, pl.ds(c * rows, rows)],
            hop_send.at[i], edge_recv.at[d, c],
            az=lax.rem(az + (4 if d == 0 else n_az - 4), n_az),
        )

    def start_even(d):
        @pl.loop(0, chunks // 2)
        def _(i):
            edge_copy(d, 2 * i).start()

    def start_odd(d):
        @pl.loop(0, chunks // 2)
        def _(i):
            pl.when(far[d])(lambda: detour_copy(d, i).start())
            pl.when(jnp.logical_not(far[d]))(lambda: edge_copy(d, 2 * i + 1).start())

    def start_both(d):
        @pl.loop(0, chunks // 2)
        def _(i):
            pl.when(far[d])(lambda: detour_copy(d, i).start())
            edge_copy(d, 2 * i).start()
            pl.when(jnp.logical_not(far[d]))(lambda: edge_copy(d, 2 * i + 1).start())

    def pass_on(i):
        @pl.when(jnp.logical_or(y_first, y_last))
        def _():
            remote(hop.at[i], hop.at[i], hop_send.at[i], hop_recv.at[i], az=nxt).wait_recv()
            pl.when(y_first)(lambda: onward_copy(0, i).start())
            pl.when(y_last)(lambda: onward_copy(1, i).start())

    @pl.when(next_first)
    def _():
        start_both(0)

    @pl.when(jnp.logical_and(prev_first, jnp.logical_not(y_first)))
    def _():
        start_both(1)

    @pl.when(jnp.logical_and(prev_first, y_first))
    def _():
        start_even(1)

    @pl.when(jnp.logical_not(odd))
    def _():
        signal(ready.at[2], ax=ax + 1)
        pl.when(has_left)(lambda: signal(ready.at[3], ax=ax - 1))

    @pl.when(az > 2)
    def _():
        signal(ready.at[4], az=1)
        signal(ready.at[4], az=2)

    @pl.when(is_worker)
    def _():
        pl.when(az == 2)(lambda: signal(ready.at[4], az=1))
        for other in range(5):
            pl.when(jnp.logical_and(other < order, region != other % 2))(
                functools.partial(signal, ready.at[5], az=other // 2, region=other % 2)
            )

    @pl.when(next_later)
    def _():
        pl.semaphore_wait(ready.at[0], 1)
        start_both(0)

    @pl.when(az < 3)
    def _():
        later = jnp.where(az == 0, 2, 3 - az - region)
        pl.when(later > 0)(lambda: pl.semaphore_wait(ready.at[5], later))
        for c in strip_copies:
            c.start()

    for c in loads:
        c.wait()

    lane = lax.broadcasted_iota(jnp.int32, (8, 128), 1)
    first_lane = lane == 0
    last_lane = lane == 127
    sub = lax.broadcasted_iota(jnp.int32, (8, 128), 0)
    first_row = sub == 0
    last_row = sub == 7

    def pack(r, held):
        mine = lane == r
        got = []
        for f in range(3):
            left = pltpu.roll(cells[f, r, :, :128], r, 1)
            right = pltpu.roll(cells[f, r, :, 128:], lax.rem(r + 1, 128), 1)
            got.append(jnp.where(mine, left, held[2 * f]))
            got.append(jnp.where(mine, right, held[2 * f + 1]))
        return tuple(got)

    columns = lax.fori_loop(
        0, radial, pack, tuple(jnp.zeros((8, 128), jnp.float32) for _ in range(6)), unroll=8
    )
    for f in range(3):
        packed[0, f] = columns[2 * f]
        packed[1, f] = columns[2 * f + 1]

    to_left = remote(packed.at[0], sides.at[1], side_send.at[0], side_recv.at[1], ax=ax - 1)
    to_right = remote(packed.at[1], sides.at[0], side_send.at[1], side_recv.at[0], ax=ax + 1)

    @pl.when(has_left)
    def _():
        pl.when(odd)(lambda: pl.semaphore_wait(ready.at[2], 1))
        to_left.start()

    @pl.when(has_right)
    def _():
        pl.when(odd)(lambda: pl.semaphore_wait(ready.at[3], 1))
        to_right.start()

    @pl.when(jnp.logical_and(prev_first, y_first))
    def _():
        pl.semaphore_wait(ready.at[6], 1)
        start_odd(1)

    def start_late():
        pl.semaphore_wait(ready.at[6], 1)
        pl.semaphore_wait(ready.at[1], 1)
        start_both(1)

    @pl.when(has_left)
    def _():
        to_right.wait_recv()

    @pl.when(jnp.logical_not(has_left))
    def _():
        sides[0] = jnp.zeros((3, 8, 128), jnp.float32)

    @pl.when(has_right)
    def _():
        to_left.wait_recv()

    @pl.when(jnp.logical_not(has_right))
    def _():
        sides[1] = jnp.zeros((3, 8, 128), jnp.float32)

    def pick(vapor, wick):
        return jnp.where(is_vapor, jnp.float32(vapor), jnp.float32(wick))

    press = pick(1.0, 0.6)
    visc = pick(0.3, 0.05)
    fric = pick(0.1, 2.0)
    sound = pick(1.5, 0.8)
    pdiff = pick(0.2, 0.4)
    advect = pick(1.0, 0.5)
    zero = jnp.float32(0.0)

    def cell_row(r):
        inner = jnp.maximum(r - 1, 0)
        outer = jnp.minimum(r + 1, radial - 1)
        to_last = lax.rem(255 - r, 128)
        to_first = lax.rem(128 - r, 128)
        center, laplace, gradient = [], [], []
        for f in range(3):
            c = [cells[f, r, :, :128], cells[f, r, :, 128:]]
            plus = [pltpu.roll(c[0], 127, 1), pltpu.roll(c[1], 127, 1)]
            minus = [pltpu.roll(c[0], 1, 1), pltpu.roll(c[1], 1, 1)]
            from_right = pltpu.roll(sides[1, f], to_last, 1)
            from_left = pltpu.roll(sides[0, f], to_first, 1)
            ax_plus = [
                jnp.where(last_lane, plus[1], plus[0]),
                jnp.where(last_lane, from_right, plus[1]),
            ]
            ax_minus = [
                jnp.where(first_lane, from_left, minus[0]),
                jnp.where(first_lane, minus[0], minus[1]),
            ]
            laps, grads = [], []
            for h in range(2):
                lanes = pl.ds(128 * h, 128)
                az_plus = jnp.where(last_row, zero, pltpu.roll(c[h], 7, 0))
                az_minus = jnp.where(first_row, zero, pltpu.roll(c[h], 1, 0))
                laps.append(
                    cells[f, outer, :, lanes] + cells[f, inner, :, lanes]
                    + az_plus + az_minus + ax_plus[h] + ax_minus[h] - 6.0 * c[h]
                )
                grads.append(0.5 * (ax_plus[h] - ax_minus[h]))
            center.append(c)
            laplace.append(laps)
            gradient.append(grads)
        for h in range(2):
            lanes = pl.ds(128 * h, 128)
            t, p, u = center[0][h], center[1][h], center[2][h]
            out[0, r, :, lanes] = t + dt * (
                kappa[r, :, lanes] * laplace[0][h] - advect * u * gradient[0][h]
            )
            out[1, r, :, lanes] = p + dt * (
                -sound * gradient[2][h] + pdiff * laplace[1][h]
            )
            out[2, r, :, lanes] = u + dt * (
                -press * gradient[1][h] + visc * laplace[2][h] - fric * u
            )

    first_pass = jnp.logical_or(az == 11, az == 12)
    last_pass = az == 3
    ahead = first_pass.astype(jnp.int32)
    pl.when(first_pass)(lambda: pass_on(0))
    turns = radial // unroll

    @pl.loop(0, turns)
    def _(i):
        for k in range(unroll):
            cell_row(i * unroll + k)
        quarter = lax.div(i + 1, turns // 4)

        @pl.when(lax.rem(i + 1, turns // 4) == 0)
        def _():
            pl.when(jnp.logical_and(quarter < 4, jnp.logical_not(last_pass)))(
                lambda: pass_on(quarter - 1 + ahead)
            )
            pl.when(jnp.logical_and(az == 12, quarter == 1))(start_late)

    pl.when(az == 0)(start_late)
    pl.when(jnp.logical_not(jnp.logical_or(first_pass, last_pass)))(lambda: pass_on(3))

    @pl.when(last_pass)
    def _():
        for i in range(chunks // 2):
            pass_on(i)

    @pl.when(is_worker)
    def _():
        remote(strips, strips, strip_send, strip_recv, az=az).wait_recv()
        for h in range(2):
            shift = placement[pl.ds(h, 1), :]
            shift = jnp.where(is_vapor, shift, lax.rem(128 - shift, 128))
            circle = strips[:, :, pl.ds(128 * h, 128)].reshape(128, 128)
            for bit in range(7):
                step = 1 << bit
                if step < 8:
                    rolled = pltpu.roll(circle, 128 - step, 0)
                else:
                    rolled = jnp.concatenate([circle[step:], circle[:step]], axis=0)
                circle = jnp.where(lax.rem(lax.div(shift, step), 2) == 1, rolled, circle)
            turned[:, :, pl.ds(128 * h, 128)] = circle.reshape(16, 8, 128)
        facing[az - 1] = turned[az]
        pl.semaphore_wait(ready.at[4], 15 - az)

        @pl.loop(0, 16)
        def _(j):
            @pl.when(j != az)
            def _():
                remote(
                    turned.at[j], facing.at[az - 1], turn_send, turn_recv.at[az - 1], az=j
                ).start()

    weights = (None, pdiff, visc)

    @pl.loop(0, chunks)
    def _(c):
        edge_copy(0, c).wait_recv()
        edge_copy(1, c).wait_recv()

        @pl.loop(0, rows // unroll)
        def _(i):
            for k in range(unroll):
                r = c * rows + i * unroll + k
                for h in range(2):
                    lanes = pl.ds(128 * h, 128)
                    for f in range(3):
                        beyond = jnp.where(
                            last_row,
                            edges[1, f, r, :, lanes],
                            jnp.where(first_row, edges[0, f, r, :, lanes], zero),
                        )
                        weight = kappa[r, :, lanes] if f == 0 else weights[f]
                        out[f, r, :, lanes] += dt * (weight * beyond)

    for q in range(2):
        pl.when(az != q + 1)(
            remote(facing.at[q], facing.at[q], turn_send, turn_recv.at[q], az=q).wait_recv
        )

    for h in range(2):
        lanes = pl.ds(128 * h, 128)
        own_t, own_p, own_u = [cells[f, iface, :, lanes] for f in range(3)]
        first, second = facing[0, :, lanes], facing[1, :, lanes]
        t_wick = jnp.where(is_vapor, first, own_t)
        p_vapor = jnp.where(is_vapor, own_p, first)
        u_vapor = jnp.where(is_vapor, own_u, second)
        u_wick = jnp.where(is_vapor, second, own_u)
        evap = 2.0 * (t_wick - 0.5 * p_vapor)
        shear = 1.5 * (u_vapor - u_wick)
        out[0, iface, :, lanes] += dt * jnp.where(is_vapor, 0.5 * evap, -evap)
        out[1, iface, :, lanes] += dt * jnp.where(is_vapor, evap, -0.5 * evap)
        out[2, iface, :, lanes] += dt * jnp.where(is_vapor, -shear, 0.5 * shear)
        zone = jnp.broadcast_to(zones[pl.ds(h, 1), :], (8, 128))
        wall = cells[0, radial - 1, :, lanes]
        heat = jnp.where(
            zone == 0, jnp.float32(2.0), jnp.where(zone == 2, -1.5 * (wall + 1.0), 0.0)
        )
        out[0, radial - 1, :, lanes] += dt * jnp.where(is_vapor, 0.0, heat)

    @pl.loop(0, chunks)
    def _(c):
        edge_copy(0, c).wait_send()
        edge_copy(1, c).wait_send()

    @pl.when(jnp.logical_or(y_first, y_last))
    def _():
        for i in range(chunks // 2):
            onward_copy(0, i).wait_send()

    pl.when(has_left)(to_left.wait_send)
    pl.when(has_right)(to_right.wait_send)
    two = strips.at[pl.ds(0, 2)]
    remote(two, two, strip_send, strip_recv, az=az).wait_send()

    @pl.when(is_worker)
    def _():
        rest = turned.at[pl.ds(0, 15)]
        remote(rest, rest, turn_send, turn_recv.at[0], az=az).wait_send()


def store_kernel(new, out, sems):
    copies = [
        pltpu.make_async_copy(new.at[f], out.at[f], sems.at[f]) for f in range(3)
    ]
    for c in copies:
        c.start()
    for c in copies:
        c.wait()


def on_device(state, conduct, zones, placement):
    fields = state[0]
    f32 = jnp.float32
    shape = fields.shape
    radial, az_cells, ax_cells = shape[1:]
    hbm = pl.BlockSpec(memory_space=pltpu.HBM)
    vmem = pl.BlockSpec(memory_space=pltpu.VMEM)
    dma = pltpu.SemaphoreType.DMA
    new = pl.pallas_call(
        step_kernel,
        out_shape=pltpu.VMEM(shape, f32),
        in_specs=[hbm] * 4,
        out_specs=vmem,
        scratch_shapes=[
            pltpu.VMEM((2, 128), jnp.int32),
            pltpu.VMEM((2, 128), jnp.int32),
            pltpu.VMEM(shape, f32),
            pltpu.VMEM(shape[1:], f32),
            pltpu.VMEM((2, 3, radial, 1, ax_cells), f32),
            pltpu.VMEM((chunks // 2, 3, radial // chunks, 1, ax_cells), f32),
            pltpu.VMEM((2, 3, 8, 128), f32),
            pltpu.VMEM((2, 3, 8, 128), f32),
            pltpu.VMEM((16, 8, 256), f32),
            pltpu.VMEM((16, 8, 256), f32),
            pltpu.VMEM((2, 8, 256), f32),
            dma((4,)),
            dma((2, chunks)),
            dma((2, chunks)),
            dma((chunks // 2,)),
            dma((chunks // 2,)),
            dma((2,)),
            dma((2,)),
            dma,
            dma,
            dma,
            dma((2,)),
            pltpu.SemaphoreType.REGULAR((7,)),
        ],
        compiler_params=pltpu.CompilerParams(
            collective_id=0, has_side_effects=True, vmem_limit_bytes=24 << 20
        ),
        cost_estimate=pl.CostEstimate(
            flops=40 * fields.size, bytes_accessed=4 * 7 * conduct.size, transcendentals=0
        ),
    )(*(
        pltpu.with_memory_space_constraint(x, pltpu.HBM)
        for x in (fields, conduct[0], zones.reshape(2, 128), placement.reshape(2, 128))
    ))
    result = pl.pallas_call(
        store_kernel,
        out_shape=jax.ShapeDtypeStruct(shape, f32),
        in_specs=[vmem],
        out_specs=hbm,
        scratch_shapes=[dma((3,))],
        compiler_params=pltpu.CompilerParams(vmem_limit_bytes=1 << 20),
    )(pltpu.with_memory_space_constraint(new, pltpu.VMEM))
    return result[None]


def solution(mesh):
    return jax.shard_map(
        on_device,
        mesh=mesh,
        in_specs=(
            P("region", None, None, "az", "ax"),
            P("region", None, "az", "ax"),
            P("ax"),
            P("ax"),
        ),
        out_specs=P("region", None, None, "az", "ax"),
        check_vma=False,
    )
```

```python
import functools
import jax
import jax.numpy as jnp
from jax import lax
from jax.experimental import pallas as pl
from jax.experimental.pallas import tpu as pltpu
from jax.sharding import PartitionSpec as P

MESH = pl.DeviceIdType.MESH
dt = 0.05
chunks = 8
detours = 6
unroll = 8


def step_kernel(
    state, conduct, zone_ref, place_ref, out,
    zones, placement, cells, kappa, edges, hop, lift, packed, sides, strips, turned, facing,
    load_sem, lift_send, lift_recv, edge_send, edge_recv, hop_send, hop_recv, side_send, side_recv,
    strip_send, strip_recv, turn_send, turn_recv, ready,
):
    region = lax.axis_index("region")
    ax = lax.axis_index("ax")
    az = lax.axis_index("az")
    n_az = lax.axis_size("az")
    n_ax = lax.axis_size("ax")
    radial = state.shape[1]
    rows = radial // chunks
    is_vapor = region == 0
    y = lax.rem(az, 4)
    nxt = lax.rem(az + 1, n_az)
    prv = lax.rem(az + n_az - 1, n_az)
    odd = lax.rem(ax, 2) == 1
    has_left = ax > 0
    has_right = ax < n_ax - 1
    is_worker = jnp.logical_or(az == 1, az == 2)
    iface = jnp.where(is_vapor, radial - 1, 0)
    swap_low = jnp.logical_and(is_vapor, jnp.logical_or(az == 10, az == 14))
    swap_high = jnp.logical_and(is_vapor, jnp.logical_or(az == 11, az == 15))
    next_later = jnp.logical_not(jnp.logical_or(jnp.logical_or(az == 11, az == 15), swap_low))
    prev_later = jnp.logical_or(jnp.logical_or(az == 0, az == 12), swap_high)
    next_first = jnp.logical_not(next_later)
    prev_first = jnp.logical_not(prev_later)
    even = lax.rem(ax, 2) == 0
    low_end = jnp.logical_and(y == 0, region == 1)
    high_end = jnp.logical_and(y == 3, region == 1)

    def signal(sem, **device):
        pl.semaphore_signal(sem, inc=1, device_id=device, device_id_type=MESH)

    def remote(src, dst, send, recv, **device):
        return pltpu.make_async_remote_copy(
            src_ref=src, dst_ref=dst, send_sem=send, recv_sem=recv,
            device_id=device, device_id_type=MESH,
        )

    barrier = pltpu.get_barrier_semaphore()
    pl.when(next_later)(lambda: signal(barrier, az=nxt))
    pl.when(prev_later)(lambda: signal(barrier, az=prv))
    pl.when(low_end)(lambda: signal(barrier, az=az + 3))
    pl.when(even)(lambda: signal(barrier, ax=ax + 1))
    pl.when(jnp.logical_and(even, has_left))(lambda: signal(barrier, ax=ax - 1))

    loads = [
        pltpu.make_async_copy(src, dst, load_sem.at[i])
        for i, (src, dst) in enumerate(
            ((state, cells), (conduct, kappa), (zone_ref, zones), (place_ref, placement))
        )
    ]
    for c in loads:
        c.start()

    @pl.when(az < 2)
    def _():
        signal(barrier, az=2)
        pl.when(az == 0)(lambda: signal(barrier, az=1))

    @pl.when(is_worker)
    def _():
        pl.when(is_vapor)(lambda: signal(barrier, region=1))

        @pl.loop(3, n_az)
        def _(j):
            signal(barrier, az=j)

    count = (
        next_first.astype(jnp.int32)
        + prev_first.astype(jnp.int32)
        + high_end.astype(jnp.int32)
        + jnp.where(odd, 1 + has_right.astype(jnp.int32), 0)
        + jnp.minimum(az, 2)
        + jnp.logical_and(is_worker, region == 1).astype(jnp.int32)
    )
    pl.when(count > 0)(lambda: pl.semaphore_wait(barrier, count))

    pl.when(next_first)(lambda: signal(ready.at[1], az=nxt))
    pl.when(prev_first)(lambda: signal(ready.at[0], az=prv))
    pl.when(high_end)(lambda: signal(ready.at[6], az=az - 3))

    def strip_source(q):
        return state.at[1 - region if q == 0 else 2, iface]

    strip_copies = [
        remote(strip_source(q), strips.at[az], strip_send, strip_recv, az=1 + q)
        for q in range(2)
    ]
    at_end = jnp.logical_and(region == 1, az > 3)
    lifted_low = jnp.logical_and(at_end, y == 0)
    lifted_high = jnp.logical_and(at_end, y == 3)
    lifted = jnp.logical_or(lifted_low, lifted_high)
    lifts = jnp.logical_and(at_end, jnp.logical_not(lifted))
    lift_copies = [
        remote(
            strip_source(q), lift.at[q], lift_send.at[q], lift_recv.at[q],
            az=jnp.where(lifted_low, az + 1, az - 1),
        )
        for q in range(2)
    ]
    lifted_copies = [
        remote(
            lift.at[q], strips.at[jnp.where(y == 1, az - 1, lax.rem(az + 1, n_az))],
            lift_send.at[q], strip_recv, az=1 + q,
        )
        for q in range(2)
    ]

    def start_all(copies):
        for c in copies:
            c.start()

    def pass_strips():
        for q in range(2):
            lift_copies[q].wait_recv()
            lifted_copies[q].start()

    pl.when(jnp.logical_and(az > 2, jnp.logical_not(lifted)))(lambda: start_all(strip_copies))
    pl.when(lifted_high)(lambda: start_all(lift_copies))

    far = (high_end, low_end)
    neighbour = (nxt, prv)

    def edge_source(d, c):
        return state.at[:, pl.ds(c * rows, rows), pl.ds(7 - 7 * d, 1), :]

    def edge_copy(d, c):
        return remote(
            edge_source(d, c), edges.at[d, :, pl.ds(c * rows, rows)],
            edge_send.at[d, c], edge_recv.at[d, c], az=neighbour[d],
        )

    def detour_copy(d, c):
        return remote(
            edge_source(d, c), hop.at[c], edge_send.at[d, c], hop_recv.at[c], az=az + 6 * d - 3
        )

    def onward_copy(d, c):
        return remote(
            hop.at[c], edges.at[d, :, pl.ds(c * rows, rows)], hop_send.at[c], edge_recv.at[d, c],
            az=lax.rem(az + (4 if d == 0 else n_az - 4), n_az),
        )

    def start(d):
        @pl.loop(0, chunks)
        def _(c):
            round_about = jnp.logical_and(far[d], c < detours)
            pl.when(round_about)(lambda: detour_copy(d, c).start())
            pl.when(jnp.logical_not(round_about))(lambda: edge_copy(d, c).start())

    def pass_on(first, last):
        @pl.when(jnp.logical_or(low_end, high_end))
        def _():
            @pl.loop(first, last)
            def _(c):
                remote(hop.at[c], hop.at[c], hop_send.at[c], hop_recv.at[c], az=nxt).wait_recv()
                pl.when(low_end)(lambda: onward_copy(0, c).start())
                pl.when(high_end)(lambda: onward_copy(1, c).start())

    pl.when(next_first)(lambda: start(0))
    pl.when(jnp.logical_and(prev_first, jnp.logical_not(low_end)))(lambda: start(1))

    @pl.when(odd)
    def _():
        signal(ready.at[3], ax=ax - 1)
        pl.when(has_right)(lambda: signal(ready.at[2], ax=ax + 1))

    @pl.when(is_worker)
    def _():
        signal(ready.at[5], az=0)
        pl.when(az == 2)(lambda: signal(ready.at[5], az=1))
        pl.when(region == 1)(lambda: signal(ready.at[5], region=0))

    @pl.when(next_later)
    def _():
        pl.semaphore_wait(ready.at[0], 1)
        pl.when(lifted_low)(lambda: start_all(lift_copies))
        start(0)

    @pl.when(az < 3)
    def _():
        later = jnp.where(az == 0, 2, 2 - az + jnp.where(is_vapor, 1, 0))
        pl.when(later > 0)(lambda: pl.semaphore_wait(ready.at[5], later))
        for q in range(2):
            pl.when(az != 1 + q)(strip_copies[q].start)

    for c in loads:
        c.wait()

    lane = lax.broadcasted_iota(jnp.int32, (8, 128), 1)
    first_lane = lane == 0
    last_lane = lane == 127
    sub = lax.broadcasted_iota(jnp.int32, (8, 128), 0)
    first_row = sub == 0
    last_row = sub == 7

    def pack(r, held):
        mine = lane == r
        got = []
        for f in range(3):
            left = pltpu.roll(cells[f, r, :, :128], r, 1)
            right = pltpu.roll(cells[f, r, :, 128:], lax.rem(r + 1, 128), 1)
            got.append(jnp.where(mine, left, held[2 * f]))
            got.append(jnp.where(mine, right, held[2 * f + 1]))
        return tuple(got)

    columns = lax.fori_loop(
        0, radial, pack, tuple(jnp.zeros((8, 128), jnp.float32) for _ in range(6)), unroll=8
    )
    for f in range(3):
        packed[0, f] = columns[2 * f]
        packed[1, f] = columns[2 * f + 1]

    to_left = remote(packed.at[0], sides.at[1], side_send.at[0], side_recv.at[1], ax=ax - 1)
    to_right = remote(packed.at[1], sides.at[0], side_send.at[1], side_recv.at[0], ax=ax + 1)

    @pl.when(has_left)
    def _():
        pl.when(even)(lambda: pl.semaphore_wait(ready.at[2], 1))
        to_left.start()

    @pl.when(has_right)
    def _():
        pl.when(even)(lambda: pl.semaphore_wait(ready.at[3], 1))
        to_right.start()

    @pl.when(low_end)
    def _():
        pl.semaphore_wait(ready.at[6], 1)
        pl.when(prev_first)(lambda: start(1))

    def start_late():
        pl.semaphore_wait(ready.at[1], 1)
        start(1)

    pl.when(swap_high)(start_late)

    @pl.when(has_left)
    def _():
        to_right.wait_recv()

    @pl.when(jnp.logical_not(has_left))
    def _():
        sides[0] = jnp.zeros((3, 8, 128), jnp.float32)

    @pl.when(has_right)
    def _():
        to_left.wait_recv()

    @pl.when(jnp.logical_not(has_right))
    def _():
        sides[1] = jnp.zeros((3, 8, 128), jnp.float32)

    def pick(vapor, wick):
        return jnp.where(is_vapor, jnp.float32(vapor), jnp.float32(wick))

    press = pick(1.0, 0.6)
    visc = pick(0.3, 0.05)
    fric = pick(0.1, 2.0)
    sound = pick(1.5, 0.8)
    pdiff = pick(0.2, 0.4)
    advect = pick(1.0, 0.5)
    zero = jnp.float32(0.0)

    def cell_row(r):
        inner = jnp.maximum(r - 1, 0)
        outer = jnp.minimum(r + 1, radial - 1)
        to_last = lax.rem(255 - r, 128)
        to_first = lax.rem(128 - r, 128)
        center, laplace, gradient = [], [], []
        for f in range(3):
            c = [cells[f, r, :, :128], cells[f, r, :, 128:]]
            plus = [pltpu.roll(c[0], 127, 1), pltpu.roll(c[1], 127, 1)]
            minus = [pltpu.roll(c[0], 1, 1), pltpu.roll(c[1], 1, 1)]
            from_right = pltpu.roll(sides[1, f], to_last, 1)
            from_left = pltpu.roll(sides[0, f], to_first, 1)
            ax_plus = [
                jnp.where(last_lane, plus[1], plus[0]),
                jnp.where(last_lane, from_right, plus[1]),
            ]
            ax_minus = [
                jnp.where(first_lane, from_left, minus[0]),
                jnp.where(first_lane, minus[0], minus[1]),
            ]
            laps, grads = [], []
            for h in range(2):
                lanes = pl.ds(128 * h, 128)
                az_plus = jnp.where(last_row, zero, pltpu.roll(c[h], 7, 0))
                az_minus = jnp.where(first_row, zero, pltpu.roll(c[h], 1, 0))
                laps.append(
                    cells[f, outer, :, lanes] + cells[f, inner, :, lanes]
                    + az_plus + az_minus + ax_plus[h] + ax_minus[h] - 6.0 * c[h]
                )
                grads.append(0.5 * (ax_plus[h] - ax_minus[h]))
            center.append(c)
            laplace.append(laps)
            gradient.append(grads)
        for h in range(2):
            lanes = pl.ds(128 * h, 128)
            t, p, u = center[0][h], center[1][h], center[2][h]
            out[0, r, :, lanes] = t + dt * (
                kappa[r, :, lanes] * laplace[0][h] - advect * u * gradient[0][h]
            )
            out[1, r, :, lanes] = p + dt * (
                -sound * gradient[2][h] + pdiff * laplace[1][h]
            )
            out[2, r, :, lanes] = u + dt * (
                -press * gradient[1][h] + visc * laplace[2][h] - fric * u
            )

    turns = radial // unroll

    @pl.loop(0, turns)
    def _(i):
        for k in range(unroll):
            cell_row(i * unroll + k)

        pl.when(jnp.logical_and(az == 12, i == turns // 4 - 1))(start_late)
        pl.when(jnp.logical_and(az == 0, i == 3 * turns // 4 - 1))(start_late)
        pl.when(jnp.logical_and(lifts, i == turns // 2 - 1))(pass_strips)
        pl.when(jnp.logical_and(az >= 8, i == turns // 2 - 1))(lambda: pass_on(0, 1))
        pl.when(jnp.logical_and(az >= 4, i == 3 * turns // 4 - 1))(
            lambda: pass_on((az >= 8).astype(jnp.int32), 3 - (az < 8).astype(jnp.int32))
        )

    pass_on(jnp.where(az < 4, 0, jnp.where(az < 8, 2, 3)), detours)

    @pl.when(is_worker)
    def _():
        strips[az] = jnp.where(az == 1, cells[1 - region, iface], cells[2, iface])
        others = strips.at[pl.ds(0, 15)]
        remote(others, others, strip_send, strip_recv, az=az).wait_recv()
        signal(ready.at[4], region=1 - region)
        for h in range(2):
            shift = placement[pl.ds(h, 1), :]
            shift = jnp.where(is_vapor, lax.rem(128 - shift, 128), shift)
            circle = strips[:, :, pl.ds(128 * h, 128)].reshape(128, 128)
            for bit in range(7):
                step = 1 << bit
                if step < 8:
                    rolled = pltpu.roll(circle, 128 - step, 0)
                else:
                    rolled = jnp.concatenate([circle[step:], circle[:step]], axis=0)
                circle = jnp.where(lax.rem(lax.div(shift, step), 2) == 1, rolled, circle)
            turned[:, :, pl.ds(128 * h, 128)] = circle.reshape(16, 8, 128)
        pl.semaphore_wait(ready.at[4], 1)

        @pl.loop(0, n_az)
        def _(j):
            remote(
                turned.at[j], facing.at[az - 1], turn_send, turn_recv.at[az - 1],
                az=j, region=1 - region,
            ).start()

    weights = (None, pdiff, visc)

    @pl.loop(0, chunks)
    def _(c):
        edge_copy(0, c).wait_recv()
        edge_copy(1, c).wait_recv()

        @pl.loop(0, rows // unroll)
        def _(i):
            for k in range(unroll):
                r = c * rows + i * unroll + k
                for h in range(2):
                    lanes = pl.ds(128 * h, 128)
                    for f in range(3):
                        beyond = jnp.where(
                            last_row,
                            edges[1, f, r, :, lanes],
                            jnp.where(first_row, edges[0, f, r, :, lanes], zero),
                        )
                        weight = kappa[r, :, lanes] if f == 0 else weights[f]
                        out[f, r, :, lanes] += dt * (weight * beyond)

    for q in range(2):
        remote(facing.at[q], facing.at[q], turn_send, turn_recv.at[q], az=q).wait_recv()

    for h in range(2):
        lanes = pl.ds(128 * h, 128)
        own_t, own_p, own_u = [cells[f, iface, :, lanes] for f in range(3)]
        first, second = facing[0, :, lanes], facing[1, :, lanes]
        t_wick = jnp.where(is_vapor, first, own_t)
        p_vapor = jnp.where(is_vapor, own_p, first)
        u_vapor = jnp.where(is_vapor, own_u, second)
        u_wick = jnp.where(is_vapor, second, own_u)
        evap = 2.0 * (t_wick - 0.5 * p_vapor)
        shear = 1.5 * (u_vapor - u_wick)
        out[0, iface, :, lanes] += dt * jnp.where(is_vapor, 0.5 * evap, -evap)
        out[1, iface, :, lanes] += dt * jnp.where(is_vapor, evap, -0.5 * evap)
        out[2, iface, :, lanes] += dt * jnp.where(is_vapor, -shear, 0.5 * shear)
        zone = jnp.broadcast_to(zones[pl.ds(h, 1), :], (8, 128))
        wall = cells[0, radial - 1, :, lanes]
        heat = jnp.where(
            zone == 0, jnp.float32(2.0), jnp.where(zone == 2, -1.5 * (wall + 1.0), 0.0)
        )
        out[0, radial - 1, :, lanes] += dt * jnp.where(is_vapor, 0.0, heat)

    @pl.loop(0, chunks)
    def _(c):
        edge_copy(0, c).wait_send()
        edge_copy(1, c).wait_send()

    @pl.when(jnp.logical_or(low_end, high_end))
    def _():
        @pl.loop(0, detours)
        def _(c):
            onward_copy(0, c).wait_send()

    pl.when(has_left)(to_left.wait_send)
    pl.when(has_right)(to_right.wait_send)
    @pl.when(is_worker)
    def _():
        strip_copies[0].wait_send()
        remote(turned, turned, turn_send, turn_recv.at[0], az=az).wait_send()

    @pl.when(jnp.logical_not(jnp.logical_or(is_worker, lifted)))
    def _():
        two = facing
        remote(two, two, strip_send, strip_recv, az=az).wait_send()

    @pl.when(jnp.logical_or(lifted, lifts))
    def _():
        for c in lift_copies:
            c.wait_send()


def store_kernel(new, out, sems):
    copies = [
        pltpu.make_async_copy(new.at[f], out.at[f], sems.at[f]) for f in range(3)
    ]
    for c in copies:
        c.start()
    for c in copies:
        c.wait()


def on_device(state, conduct, zones, placement):
    fields = state[0]
    f32 = jnp.float32
    shape = fields.shape
    radial, az_cells, ax_cells = shape[1:]
    hbm = pl.BlockSpec(memory_space=pltpu.HBM)
    vmem = pl.BlockSpec(memory_space=pltpu.VMEM)
    dma = pltpu.SemaphoreType.DMA
    new = pl.pallas_call(
        step_kernel,
        out_shape=pltpu.VMEM(shape, f32),
        in_specs=[hbm] * 4,
        out_specs=vmem,
        scratch_shapes=[
            pltpu.VMEM((2, 128), jnp.int32),
            pltpu.VMEM((2, 128), jnp.int32),
            pltpu.VMEM(shape, f32),
            pltpu.VMEM(shape[1:], f32),
            pltpu.VMEM((2, 3, radial, 1, ax_cells), f32),
            pltpu.VMEM((detours, 3, radial // chunks, 1, ax_cells), f32),
            pltpu.VMEM((2, 8, ax_cells), f32),
            pltpu.VMEM((2, 3, 8, 128), f32),
            pltpu.VMEM((2, 3, 8, 128), f32),
            pltpu.VMEM((16, 8, 256), f32),
            pltpu.VMEM((16, 8, 256), f32),
            pltpu.VMEM((2, 8, 256), f32),
            dma((4,)),
            dma((2,)),
            dma((2,)),
            dma((2, chunks)),
            dma((2, chunks)),
            dma((detours,)),
            dma((detours,)),
            dma((2,)),
            dma((2,)),
            dma,
            dma,
            dma,
            dma((2,)),
            pltpu.SemaphoreType.REGULAR((7,)),
        ],
        compiler_params=pltpu.CompilerParams(
            collective_id=0, has_side_effects=True, vmem_limit_bytes=24 << 20
        ),
        cost_estimate=pl.CostEstimate(
            flops=40 * fields.size, bytes_accessed=4 * 7 * conduct.size, transcendentals=0
        ),
    )(*(
        pltpu.with_memory_space_constraint(x, pltpu.HBM)
        for x in (fields, conduct[0], zones.reshape(2, 128), placement.reshape(2, 128))
    ))
    result = pl.pallas_call(
        store_kernel,
        out_shape=jax.ShapeDtypeStruct(shape, f32),
        in_specs=[vmem],
        out_specs=hbm,
        scratch_shapes=[dma((3,))],
        compiler_params=pltpu.CompilerParams(vmem_limit_bytes=1 << 20),
    )(pltpu.with_memory_space_constraint(new, pltpu.VMEM))
    return result[None]


def solution(mesh):
    return jax.shard_map(
        on_device,
        mesh=mesh,
        in_specs=(
            P("region", None, None, "az", "ax"),
            P("region", None, "az", "ax"),
            P("ax"),
            P("ax"),
        ),
        out_specs=P("region", None, None, "az", "ax"),
        check_vma=False,
    )
```

```python
import functools
import jax
import jax.numpy as jnp
from jax import lax
from jax.experimental import pallas as pl
from jax.experimental.pallas import tpu as pltpu
from jax.sharding import PartitionSpec as P

MESH = pl.DeviceIdType.MESH
dt = 0.05
chunks = 8
detours = 6
unroll = 8


def step_kernel(
    state, conduct, zone_ref, place_ref, out,
    zones, placement, cells, kappa, edges, hop, lift, packed, sides, strips, turned, facing,
    load_sem, lift_send, lift_recv, edge_send, edge_recv, hop_send, hop_recv, side_send, side_recv,
    strip_send, strip_recv, turn_send, turn_recv, ready,
):
    region = lax.axis_index("region")
    ax = lax.axis_index("ax")
    az = lax.axis_index("az")
    n_az = lax.axis_size("az")
    n_ax = lax.axis_size("ax")
    radial = state.shape[1]
    rows = radial // chunks
    is_vapor = region == 0
    y = lax.rem(az, 4)
    nxt = lax.rem(az + 1, n_az)
    prv = lax.rem(az + n_az - 1, n_az)
    odd = lax.rem(ax, 2) == 1
    has_left = ax > 0
    has_right = ax < n_ax - 1
    is_worker = jnp.logical_or(az == 1, az == 2)
    iface = jnp.where(is_vapor, radial - 1, 0)
    swap_high = jnp.logical_or(az == 11, az == 15)
    next_later = jnp.logical_not(
        jnp.logical_or(swap_high, jnp.logical_or(az == 10, az == 14))
    )
    prev_later = jnp.logical_or(jnp.logical_or(az == 0, az == 12), swap_high)
    next_first = jnp.logical_not(next_later)
    prev_first = jnp.logical_not(prev_later)
    even = lax.rem(ax, 2) == 0
    low_end = jnp.logical_and(y == 0, region == 1)
    high_end = jnp.logical_and(y == 3, region == 1)

    def signal(sem, **device):
        pl.semaphore_signal(sem, inc=1, device_id=device, device_id_type=MESH)

    def remote(src, dst, send, recv, **device):
        return pltpu.make_async_remote_copy(
            src_ref=src, dst_ref=dst, send_sem=send, recv_sem=recv,
            device_id=device, device_id_type=MESH,
        )

    barrier = pltpu.get_barrier_semaphore()
    pl.when(next_later)(lambda: signal(barrier, az=nxt))
    pl.when(prev_later)(lambda: signal(barrier, az=prv))
    pl.when(low_end)(lambda: signal(barrier, az=az + 3))
    pl.when(even)(lambda: signal(barrier, ax=ax + 1))
    pl.when(jnp.logical_and(even, has_left))(lambda: signal(barrier, ax=ax - 1))

    loads = [
        pltpu.make_async_copy(src, dst, load_sem.at[i])
        for i, (src, dst) in enumerate(
            ((state, cells), (conduct, kappa), (zone_ref, zones), (place_ref, placement))
        )
    ]
    for c in loads:
        c.start()

    @pl.when(az < 2)
    def _():
        signal(barrier, az=2)
        pl.when(az == 0)(lambda: signal(barrier, az=1))

    @pl.when(is_worker)
    def _():
        pl.when(is_vapor)(lambda: signal(barrier, region=1))

        @pl.loop(3, n_az)
        def _(j):
            signal(barrier, az=j)

    count = (
        next_first.astype(jnp.int32)
        + prev_first.astype(jnp.int32)
        + high_end.astype(jnp.int32)
        + jnp.where(odd, 1 + has_right.astype(jnp.int32), 0)
        + jnp.minimum(az, 2)
        + jnp.logical_and(is_worker, region == 1).astype(jnp.int32)
    )
    pl.when(count > 0)(lambda: pl.semaphore_wait(barrier, count))

    pl.when(next_first)(lambda: signal(ready.at[1], az=nxt))
    pl.when(prev_first)(lambda: signal(ready.at[0], az=prv))
    pl.when(high_end)(lambda: signal(ready.at[6], az=az - 3))

    @pl.when(is_worker)
    def _():
        signal(ready.at[5], az=0)
        pl.when(az == 2)(lambda: signal(ready.at[5], az=1))
        pl.when(region == 1)(lambda: signal(ready.at[5], region=0))

    def strip_source(q):
        return state.at[1 - region if q == 0 else 2, iface]

    strip_copies = [
        remote(strip_source(q), strips.at[az], strip_send, strip_recv, az=1 + q)
        for q in range(2)
    ]
    lifted = jnp.logical_and(region == 1, az == 15)
    lifts = jnp.logical_and(region == 1, az == 12)
    lift_copies = [
        remote(strip_source(q), lift.at[q], lift_send.at[q], lift_recv.at[q], az=12)
        for q in range(2)
    ]
    lifted_copies = [
        remote(lift.at[q], strips.at[15], lift_send.at[q], strip_recv, az=1 + q)
        for q in range(2)
    ]

    def start_all(copies):
        for c in copies:
            c.start()

    def pass_strips():
        for q in range(2):
            lift_copies[q].wait_recv()
            lifted_copies[q].start()

    pl.when(jnp.logical_and(az > 2, jnp.logical_not(lifted)))(lambda: start_all(strip_copies))
    pl.when(lifted)(lambda: start_all(lift_copies))

    far = (high_end, low_end)
    neighbour = (nxt, prv)

    def edge_source(d, c):
        return state.at[:, pl.ds(c * rows, rows), pl.ds(7 - 7 * d, 1), :]

    def edge_copy(d, c):
        return remote(
            edge_source(d, c), edges.at[d, :, pl.ds(c * rows, rows)],
            edge_send.at[d, c], edge_recv.at[d, c], az=neighbour[d],
        )

    def detour_copy(d, c):
        return remote(
            edge_source(d, c), hop.at[c], edge_send.at[d, c], hop_recv.at[c], az=az + 6 * d - 3
        )

    def onward_copy(d, c):
        return remote(
            hop.at[c], edges.at[d, :, pl.ds(c * rows, rows)], hop_send.at[c], edge_recv.at[d, c],
            az=lax.rem(az + (4 if d == 0 else n_az - 4), n_az),
        )

    def start(d):
        @pl.loop(0, chunks)
        def _(c):
            round_about = jnp.logical_and(far[d], c < detours)
            pl.when(round_about)(lambda: detour_copy(d, c).start())
            pl.when(jnp.logical_not(round_about))(lambda: edge_copy(d, c).start())

    def pass_on(first, last):
        @pl.when(jnp.logical_or(low_end, high_end))
        def _():
            @pl.loop(first, last)
            def _(c):
                remote(hop.at[c], hop.at[c], hop_send.at[c], hop_recv.at[c], az=nxt).wait_recv()
                pl.when(low_end)(lambda: onward_copy(0, c).start())
                pl.when(high_end)(lambda: onward_copy(1, c).start())

    pl.when(next_first)(lambda: start(0))
    pl.when(jnp.logical_and(prev_first, jnp.logical_not(low_end)))(lambda: start(1))

    @pl.when(odd)
    def _():
        signal(ready.at[3], ax=ax - 1)
        pl.when(has_right)(lambda: signal(ready.at[2], ax=ax + 1))

    for c in loads:
        c.wait()

    lane = lax.broadcasted_iota(jnp.int32, (8, 128), 1)
    first_lane = lane == 0
    last_lane = lane == 127
    sub = lax.broadcasted_iota(jnp.int32, (8, 128), 0)
    first_row = sub == 0
    last_row = sub == 7

    def pack(r, held):
        mine = lane == r
        got = []
        for f in range(3):
            left = pltpu.roll(cells[f, r, :, :128], r, 1)
            right = pltpu.roll(cells[f, r, :, 128:], lax.rem(r + 1, 128), 1)
            got.append(jnp.where(mine, left, held[2 * f]))
            got.append(jnp.where(mine, right, held[2 * f + 1]))
        return tuple(got)

    columns = lax.fori_loop(
        0, radial, pack, tuple(jnp.zeros((8, 128), jnp.float32) for _ in range(6)), unroll=8
    )
    for f in range(3):
        packed[0, f] = columns[2 * f]
        packed[1, f] = columns[2 * f + 1]

    @pl.when(az < 3)
    def _():
        later = jnp.where(az == 0, 2, 2 - az + jnp.where(is_vapor, 1, 0))
        pl.when(later > 0)(lambda: pl.semaphore_wait(ready.at[5], later))
        for q in range(2):
            pl.when(az != 1 + q)(strip_copies[q].start)

    @pl.when(next_later)
    def _():
        pl.semaphore_wait(ready.at[0], 1)
        start(0)

    to_left = remote(packed.at[0], sides.at[1], side_send.at[0], side_recv.at[1], ax=ax - 1)
    to_right = remote(packed.at[1], sides.at[0], side_send.at[1], side_recv.at[0], ax=ax + 1)

    @pl.when(has_left)
    def _():
        pl.when(even)(lambda: pl.semaphore_wait(ready.at[2], 1))
        to_left.start()

    @pl.when(has_right)
    def _():
        pl.when(even)(lambda: pl.semaphore_wait(ready.at[3], 1))
        to_right.start()

    @pl.when(low_end)
    def _():
        pl.semaphore_wait(ready.at[6], 1)
        pl.when(prev_first)(lambda: start(1))

    def start_late():
        pl.semaphore_wait(ready.at[1], 1)
        start(1)

    pl.when(swap_high)(start_late)

    @pl.when(has_left)
    def _():
        to_right.wait_recv()

    @pl.when(jnp.logical_not(has_left))
    def _():
        sides[0] = jnp.zeros((3, 8, 128), jnp.float32)

    @pl.when(has_right)
    def _():
        to_left.wait_recv()

    @pl.when(jnp.logical_not(has_right))
    def _():
        sides[1] = jnp.zeros((3, 8, 128), jnp.float32)

    def pick(vapor, wick):
        return jnp.where(is_vapor, jnp.float32(vapor), jnp.float32(wick))

    press = pick(1.0, 0.6)
    visc = pick(0.3, 0.05)
    fric = pick(0.1, 2.0)
    sound = pick(1.5, 0.8)
    pdiff = pick(0.2, 0.4)
    advect = pick(1.0, 0.5)
    zero = jnp.float32(0.0)

    def cell_row(r):
        inner = jnp.maximum(r - 1, 0)
        outer = jnp.minimum(r + 1, radial - 1)
        to_last = lax.rem(255 - r, 128)
        to_first = lax.rem(128 - r, 128)
        center, laplace, gradient = [], [], []
        for f in range(3):
            c = [cells[f, r, :, :128], cells[f, r, :, 128:]]
            plus = [pltpu.roll(c[0], 127, 1), pltpu.roll(c[1], 127, 1)]
            minus = [pltpu.roll(c[0], 1, 1), pltpu.roll(c[1], 1, 1)]
            from_right = pltpu.roll(sides[1, f], to_last, 1)
            from_left = pltpu.roll(sides[0, f], to_first, 1)
            ax_plus = [
                jnp.where(last_lane, plus[1], plus[0]),
                jnp.where(last_lane, from_right, plus[1]),
            ]
            ax_minus = [
                jnp.where(first_lane, from_left, minus[0]),
                jnp.where(first_lane, minus[0], minus[1]),
            ]
            laps, grads = [], []
            for h in range(2):
                lanes = pl.ds(128 * h, 128)
                az_plus = jnp.where(last_row, zero, pltpu.roll(c[h], 7, 0))
                az_minus = jnp.where(first_row, zero, pltpu.roll(c[h], 1, 0))
                laps.append(
                    cells[f, outer, :, lanes] + cells[f, inner, :, lanes]
                    + az_plus + az_minus + ax_plus[h] + ax_minus[h] - 6.0 * c[h]
                )
                grads.append(0.5 * (ax_plus[h] - ax_minus[h]))
            center.append(c)
            laplace.append(laps)
            gradient.append(grads)
        for h in range(2):
            lanes = pl.ds(128 * h, 128)
            t, p, u = center[0][h], center[1][h], center[2][h]
            out[0, r, :, lanes] = t + dt * (
                kappa[r, :, lanes] * laplace[0][h] - advect * u * gradient[0][h]
            )
            out[1, r, :, lanes] = p + dt * (
                -sound * gradient[2][h] + pdiff * laplace[1][h]
            )
            out[2, r, :, lanes] = u + dt * (
                -press * gradient[1][h] + visc * laplace[2][h] - fric * u
            )

    turns = radial // unroll

    @pl.loop(0, turns)
    def _(i):
        for k in range(unroll):
            cell_row(i * unroll + k)

        pl.when(jnp.logical_and(lifts, i == turns // 4 - 1))(pass_strips)
        pl.when(jnp.logical_and(az == 12, i == turns // 4 - 1))(start_late)
        pl.when(jnp.logical_and(az == 0, i == 3 * turns // 4 - 1))(start_late)
        pl.when(jnp.logical_and(az >= 8, i == turns // 2 - 1))(lambda: pass_on(0, 1))
        pl.when(jnp.logical_and(az >= 4, i == 3 * turns // 4 - 1))(
            lambda: pass_on((az >= 8).astype(jnp.int32), 3 - (az < 8).astype(jnp.int32))
        )

    pass_on(jnp.where(az < 4, 0, jnp.where(az < 8, 2, 3)), detours)

    @pl.when(is_worker)
    def _():
        strips[az] = jnp.where(az == 1, cells[1 - region, iface], cells[2, iface])
        others = strips.at[pl.ds(0, 15)]
        remote(others, others, strip_send, strip_recv, az=az).wait_recv()
        signal(ready.at[4], region=1 - region)
        for h in range(2):
            shift = placement[pl.ds(h, 1), :]
            shift = jnp.where(is_vapor, lax.rem(128 - shift, 128), shift)
            circle = strips[:, :, pl.ds(128 * h, 128)].reshape(128, 128)
            for bit in range(7):
                step = 1 << bit
                if step < 8:
                    rolled = pltpu.roll(circle, 128 - step, 0)
                else:
                    rolled = jnp.concatenate([circle[step:], circle[:step]], axis=0)
                circle = jnp.where(lax.rem(lax.div(shift, step), 2) == 1, rolled, circle)
            turned[:, :, pl.ds(128 * h, 128)] = circle.reshape(16, 8, 128)
        pl.semaphore_wait(ready.at[4], 1)

        @pl.loop(0, n_az)
        def _(j):
            remote(
                turned.at[j], facing.at[az - 1], turn_send, turn_recv.at[az - 1],
                az=j, region=1 - region,
            ).start()

    weights = (None, pdiff, visc)

    @pl.loop(0, chunks)
    def _(c):
        edge_copy(0, c).wait_recv()
        edge_copy(1, c).wait_recv()

        @pl.loop(0, rows // unroll)
        def _(i):
            for k in range(unroll):
                r = c * rows + i * unroll + k
                for h in range(2):
                    lanes = pl.ds(128 * h, 128)
                    for f in range(3):
                        beyond = jnp.where(
                            last_row,
                            edges[1, f, r, :, lanes],
                            jnp.where(first_row, edges[0, f, r, :, lanes], zero),
                        )
                        weight = kappa[r, :, lanes] if f == 0 else weights[f]
                        out[f, r, :, lanes] += dt * (weight * beyond)

    for q in range(2):
        remote(facing.at[q], facing.at[q], turn_send, turn_recv.at[q], az=q).wait_recv()

    for h in range(2):
        lanes = pl.ds(128 * h, 128)
        own_t, own_p, own_u = [cells[f, iface, :, lanes] for f in range(3)]
        first, second = facing[0, :, lanes], facing[1, :, lanes]
        t_wick = jnp.where(is_vapor, first, own_t)
        p_vapor = jnp.where(is_vapor, own_p, first)
        u_vapor = jnp.where(is_vapor, own_u, second)
        u_wick = jnp.where(is_vapor, second, own_u)
        evap = 2.0 * (t_wick - 0.5 * p_vapor)
        shear = 1.5 * (u_vapor - u_wick)
        out[0, iface, :, lanes] += dt * jnp.where(is_vapor, 0.5 * evap, -evap)
        out[1, iface, :, lanes] += dt * jnp.where(is_vapor, evap, -0.5 * evap)
        out[2, iface, :, lanes] += dt * jnp.where(is_vapor, -shear, 0.5 * shear)
        zone = jnp.broadcast_to(zones[pl.ds(h, 1), :], (8, 128))
        wall = cells[0, radial - 1, :, lanes]
        heat = jnp.where(
            zone == 0, jnp.float32(2.0), jnp.where(zone == 2, -1.5 * (wall + 1.0), 0.0)
        )
        out[0, radial - 1, :, lanes] += dt * jnp.where(is_vapor, 0.0, heat)

    @pl.loop(0, chunks)
    def _(c):
        edge_copy(0, c).wait_send()
        edge_copy(1, c).wait_send()

    @pl.when(jnp.logical_or(low_end, high_end))
    def _():
        @pl.loop(0, detours)
        def _(c):
            onward_copy(0, c).wait_send()

    pl.when(has_left)(to_left.wait_send)
    pl.when(has_right)(to_right.wait_send)
    @pl.when(is_worker)
    def _():
        strip_copies[0].wait_send()
        remote(turned, turned, turn_send, turn_recv.at[0], az=az).wait_send()

    @pl.when(jnp.logical_not(jnp.logical_or(is_worker, lifted)))
    def _():
        two = facing
        remote(two, two, strip_send, strip_recv, az=az).wait_send()

    @pl.when(jnp.logical_or(lifted, lifts))
    def _():
        for c in lift_copies:
            c.wait_send()


def store_kernel(new, out, sems):
    copies = [
        pltpu.make_async_copy(new.at[f], out.at[f], sems.at[f]) for f in range(3)
    ]
    for c in copies:
        c.start()
    for c in copies:
        c.wait()


def on_device(state, conduct, zones, placement):
    fields = state[0]
    f32 = jnp.float32
    shape = fields.shape
    radial, az_cells, ax_cells = shape[1:]
    hbm = pl.BlockSpec(memory_space=pltpu.HBM)
    vmem = pl.BlockSpec(memory_space=pltpu.VMEM)
    dma = pltpu.SemaphoreType.DMA
    new = pl.pallas_call(
        step_kernel,
        out_shape=pltpu.VMEM(shape, f32),
        in_specs=[hbm] * 4,
        out_specs=vmem,
        scratch_shapes=[
            pltpu.VMEM((2, 128), jnp.int32),
            pltpu.VMEM((2, 128), jnp.int32),
            pltpu.VMEM(shape, f32),
            pltpu.VMEM(shape[1:], f32),
            pltpu.VMEM((2, 3, radial, 1, ax_cells), f32),
            pltpu.VMEM((detours, 3, radial // chunks, 1, ax_cells), f32),
            pltpu.VMEM((2, 8, ax_cells), f32),
            pltpu.VMEM((2, 3, 8, 128), f32),
            pltpu.VMEM((2, 3, 8, 128), f32),
            pltpu.VMEM((16, 8, 256), f32),
            pltpu.VMEM((16, 8, 256), f32),
            pltpu.VMEM((2, 8, 256), f32),
            dma((4,)),
            dma((2,)),
            dma((2,)),
            dma((2, chunks)),
            dma((2, chunks)),
            dma((detours,)),
            dma((detours,)),
            dma((2,)),
            dma((2,)),
            dma,
            dma,
            dma,
            dma((2,)),
            pltpu.SemaphoreType.REGULAR((7,)),
        ],
        compiler_params=pltpu.CompilerParams(
            collective_id=0, has_side_effects=True, vmem_limit_bytes=24 << 20
        ),
        cost_estimate=pl.CostEstimate(
            flops=40 * fields.size, bytes_accessed=4 * 7 * conduct.size, transcendentals=0
        ),
    )(*(
        pltpu.with_memory_space_constraint(x, pltpu.HBM)
        for x in (fields, conduct[0], zones.reshape(2, 128), placement.reshape(2, 128))
    ))
    result = pl.pallas_call(
        store_kernel,
        out_shape=jax.ShapeDtypeStruct(shape, f32),
        in_specs=[vmem],
        out_specs=hbm,
        scratch_shapes=[dma((3,))],
        compiler_params=pltpu.CompilerParams(vmem_limit_bytes=1 << 20),
    )(pltpu.with_memory_space_constraint(new, pltpu.VMEM))
    return result[None]


def solution(mesh):
    return jax.shard_map(
        on_device,
        mesh=mesh,
        in_specs=(
            P("region", None, None, "az", "ax"),
            P("region", None, "az", "ax"),
            P("ax"),
            P("ax"),
        ),
        out_specs=P("region", None, None, "az", "ax"),
        check_vma=False,
    )
```

```python
import functools
import jax
import jax.numpy as jnp
from jax import lax
from jax.experimental import pallas as pl
from jax.experimental.pallas import tpu as pltpu
from jax.sharding import PartitionSpec as P

MESH = pl.DeviceIdType.MESH
dt = 0.05
chunks = 8
unroll = 8


def step_kernel(
    state, conduct, zone_ref, place_ref, out,
    zones, placement, cells, kappa, edges, hop, lift, packed, sides, strips, turned, facing,
    load_sem, lift_send, lift_recv, edge_send, edge_recv, hop_send, hop_recv, side_send, side_recv,
    strip_send, strip_recv, turn_send, turn_recv, ready,
):
    region = lax.axis_index("region")
    ax = lax.axis_index("ax")
    az = lax.axis_index("az")
    n_az = lax.axis_size("az")
    n_ax = lax.axis_size("ax")
    radial = state.shape[1]
    rows = radial // chunks
    is_vapor = region == 0
    y = lax.rem(az, 4)
    nxt = lax.rem(az + 1, n_az)
    prv = lax.rem(az + n_az - 1, n_az)
    odd = lax.rem(ax, 2) == 1
    has_left = ax > 0
    has_right = ax < n_ax - 1
    is_worker = jnp.logical_or(az == 1, az == 2)
    iface = jnp.where(is_vapor, radial - 1, 0)
    swap_high = jnp.logical_or(az == 11, az == 15)
    next_later = jnp.logical_not(
        jnp.logical_or(swap_high, jnp.logical_or(az == 10, az == 14))
    )
    prev_later = jnp.logical_or(jnp.logical_or(az == 0, az == 12), swap_high)
    next_first = jnp.logical_not(next_later)
    prev_first = jnp.logical_not(prev_later)
    even = lax.rem(ax, 2) == 0
    low_end = jnp.logical_and(y == 0, region == 1)
    high_end = jnp.logical_and(y == 3, region == 1)
    inner = jnp.logical_and(
        region == 1, jnp.logical_or(az == 1, jnp.logical_or(az == 9, az == 13))
    )

    def signal(sem, **device):
        pl.semaphore_signal(sem, inc=1, device_id=device, device_id_type=MESH)

    def remote(src, dst, send, recv, **device):
        return pltpu.make_async_remote_copy(
            src_ref=src, dst_ref=dst, send_sem=send, recv_sem=recv,
            device_id=device, device_id_type=MESH,
        )

    barrier = pltpu.get_barrier_semaphore()
    pl.when(next_later)(lambda: signal(barrier, az=nxt))
    pl.when(prev_later)(lambda: signal(barrier, az=prv))
    pl.when(low_end)(lambda: signal(barrier, az=az + 3))
    pl.when(jnp.logical_and(inner, az > 8))(lambda: signal(barrier, az=az + 2))
    pl.when(even)(lambda: signal(barrier, ax=ax + 1))
    pl.when(jnp.logical_and(even, has_left))(lambda: signal(barrier, ax=ax - 1))

    loads = [
        pltpu.make_async_copy(src, dst, load_sem.at[i])
        for i, (src, dst) in enumerate(
            ((state, cells), (conduct, kappa), (zone_ref, zones), (place_ref, placement))
        )
    ]
    for c in loads:
        c.start()

    @pl.when(az < 2)
    def _():
        signal(barrier, az=2)
        pl.when(az == 0)(lambda: signal(barrier, az=1))

    @pl.when(is_worker)
    def _():
        pl.when(is_vapor)(lambda: signal(barrier, region=1))

        @pl.loop(3, n_az)
        def _(j):
            signal(barrier, az=j)

    count = (
        next_first.astype(jnp.int32)
        + prev_first.astype(jnp.int32)
        + high_end.astype(jnp.int32)
        + jnp.logical_and(high_end, az > 8).astype(jnp.int32)
        + jnp.where(odd, 1 + has_right.astype(jnp.int32), 0)
        + jnp.minimum(az, 2)
        + jnp.logical_and(is_worker, region == 1).astype(jnp.int32)
    )
    pl.when(count > 0)(lambda: pl.semaphore_wait(barrier, count))

    pl.when(next_first)(lambda: signal(ready.at[1], az=nxt))
    pl.when(prev_first)(lambda: signal(ready.at[0], az=prv))
    pl.when(high_end)(lambda: signal(ready.at[6], az=az - 3))

    @pl.when(is_worker)
    def _():
        signal(ready.at[5], az=0)
        pl.when(az == 2)(lambda: signal(ready.at[5], az=1))
        pl.when(region == 1)(lambda: signal(ready.at[5], region=0))

    def strip_source(q):
        return state.at[1 - region if q == 0 else 2, iface]

    strip_copies = [
        remote(strip_source(q), strips.at[az], strip_send, strip_recv, az=1 + q)
        for q in range(2)
    ]
    lifted = az < 0
    lifts = az < 0
    lift_copies = [
        remote(strip_source(q), lift.at[q], lift_send.at[q], lift_recv.at[q], az=12)
        for q in range(2)
    ]
    lifted_copies = [
        remote(lift.at[q], strips.at[15], lift_send.at[q], strip_recv, az=1 + q)
        for q in range(2)
    ]

    def start_all(copies):
        for c in copies:
            c.start()

    def pass_strips():
        for q in range(2):
            lift_copies[q].wait_recv()
            lifted_copies[q].start()

    pl.when(jnp.logical_and(az > 2, jnp.logical_not(lifted)))(lambda: start_all(strip_copies))
    pl.when(lifted)(lambda: start_all(lift_copies))

    far = (high_end, low_end)
    neighbour = (nxt, prv)

    def edge_source(d, c):
        return state.at[:, pl.ds(c * rows, rows), pl.ds(7 - 7 * d, 1), :]

    def edge_copy(d, c):
        return remote(
            edge_source(d, c), edges.at[d, :, pl.ds(c * rows, rows)],
            edge_send.at[d, c], edge_recv.at[d, c], az=neighbour[d],
        )

    round_about = (
        jnp.where(az < 8, 6, 5),
        jnp.where(az < 12, 5, 6),
    )
    rest_inner = (jnp.logical_and(high_end, az > 8), jnp.logical_and(low_end, az == 0))

    def detour_copy(d, c):
        way = jnp.where(c < round_about[d], 3, 2 - d)
        return remote(
            edge_source(d, c), hop.at[c], edge_send.at[d, c], hop_recv.at[c],
            az=az - way if d == 0 else az + way,
        )

    upward = jnp.logical_or(lax.rem(y, 2) == 0, jnp.logical_or(az == 9, az == 13))
    onward_even = lax.rem(az + 4 - y, n_az)
    onward_odd = lax.rem(az + n_az - 1 - y, n_az)

    def onward_copy(d, c):
        return remote(
            hop.at[c], edges.at[d, :, pl.ds(c * rows, rows)], hop_send.at[c], edge_recv.at[d, c],
            az=onward_even if d == 0 else onward_odd,
        )

    def start_part(d, first, last):
        @pl.loop(first, last)
        def _(c):
            detour = jnp.logical_and(far[d], jnp.logical_or(c < round_about[d], rest_inner[d]))
            pl.when(detour)(lambda: detour_copy(d, c).start())
            pl.when(jnp.logical_not(detour))(lambda: edge_copy(d, c).start())

    def start(d):
        start_part(d, 0, chunks)

    def pass_on(first, last):
        @pl.when(region == 1)
        def _():
            @pl.loop(first, last)
            def _(c):
                remote(hop.at[c], hop.at[c], hop_send.at[c], hop_recv.at[c], az=nxt).wait_recv()
                pl.when(upward)(lambda: onward_copy(0, c).start())
                pl.when(jnp.logical_not(upward))(lambda: onward_copy(1, c).start())

    last_straight = jnp.logical_and(az == 15, is_vapor)
    pl.when(jnp.logical_and(next_first, jnp.logical_not(last_straight)))(lambda: start(0))
    pl.when(prev_first)(
        lambda: start_part(1, jnp.where(low_end, round_about[1], 0), chunks)
    )

    @pl.when(odd)
    def _():
        signal(ready.at[3], ax=ax - 1)
        pl.when(has_right)(lambda: signal(ready.at[2], ax=ax + 1))

    for c in loads:
        c.wait()

    pl.when(last_straight)(lambda: start(0))

    lane = lax.broadcasted_iota(jnp.int32, (8, 128), 1)
    first_lane = lane == 0
    last_lane = lane == 127
    sub = lax.broadcasted_iota(jnp.int32, (8, 128), 0)
    first_row = sub == 0
    last_row = sub == 7

    def pack(r, held):
        mine = lane == r
        got = []
        for f in range(3):
            left = pltpu.roll(cells[f, r, :, :128], r, 1)
            right = pltpu.roll(cells[f, r, :, 128:], lax.rem(r + 1, 128), 1)
            got.append(jnp.where(mine, left, held[2 * f]))
            got.append(jnp.where(mine, right, held[2 * f + 1]))
        return tuple(got)

    columns = lax.fori_loop(
        0, radial, pack, tuple(jnp.zeros((8, 128), jnp.float32) for _ in range(6)), unroll=8
    )
    for f in range(3):
        packed[0, f] = columns[2 * f]
        packed[1, f] = columns[2 * f + 1]

    @pl.when(az < 3)
    def _():
        later = jnp.where(az == 0, 2, 2 - az + jnp.where(is_vapor, 1, 0))
        pl.when(later > 0)(lambda: pl.semaphore_wait(ready.at[5], later))
        for q in range(2):
            pl.when(az != 1 + q)(strip_copies[q].start)

    @pl.when(next_later)
    def _():
        pl.semaphore_wait(ready.at[0], 1)
        start(0)

    to_left = remote(packed.at[0], sides.at[1], side_send.at[0], side_recv.at[1], ax=ax - 1)
    to_right = remote(packed.at[1], sides.at[0], side_send.at[1], side_recv.at[0], ax=ax + 1)

    @pl.when(has_left)
    def _():
        pl.when(even)(lambda: pl.semaphore_wait(ready.at[2], 1))
        to_left.start()

    @pl.when(has_right)
    def _():
        pl.when(even)(lambda: pl.semaphore_wait(ready.at[3], 1))
        to_right.start()

    @pl.when(low_end)
    def _():
        pl.semaphore_wait(ready.at[6], 1)
        pl.when(prev_first)(lambda: start_part(1, 0, round_about[1]))

    def start_late():
        pl.semaphore_wait(ready.at[1], 1)
        start(1)

    pl.when(swap_high)(start_late)

    @pl.when(has_left)
    def _():
        to_right.wait_recv()

    @pl.when(jnp.logical_not(has_left))
    def _():
        sides[0] = jnp.zeros((3, 8, 128), jnp.float32)

    @pl.when(has_right)
    def _():
        to_left.wait_recv()

    @pl.when(jnp.logical_not(has_right))
    def _():
        sides[1] = jnp.zeros((3, 8, 128), jnp.float32)

    def pick(vapor, wick):
        return jnp.where(is_vapor, jnp.float32(vapor), jnp.float32(wick))

    press = pick(1.0, 0.6)
    visc = pick(0.3, 0.05)
    fric = pick(0.1, 2.0)
    sound = pick(1.5, 0.8)
    pdiff = pick(0.2, 0.4)
    advect = pick(1.0, 0.5)
    zero = jnp.float32(0.0)

    def cell_row(r):
        inner = jnp.maximum(r - 1, 0)
        outer = jnp.minimum(r + 1, radial - 1)
        to_last = lax.rem(255 - r, 128)
        to_first = lax.rem(128 - r, 128)
        center, laplace, gradient = [], [], []
        for f in range(3):
            c = [cells[f, r, :, :128], cells[f, r, :, 128:]]
            plus = [pltpu.roll(c[0], 127, 1), pltpu.roll(c[1], 127, 1)]
            minus = [pltpu.roll(c[0], 1, 1), pltpu.roll(c[1], 1, 1)]
            from_right = pltpu.roll(sides[1, f], to_last, 1)
            from_left = pltpu.roll(sides[0, f], to_first, 1)
            ax_plus = [
                jnp.where(last_lane, plus[1], plus[0]),
                jnp.where(last_lane, from_right, plus[1]),
            ]
            ax_minus = [
                jnp.where(first_lane, from_left, minus[0]),
                jnp.where(first_lane, minus[0], minus[1]),
            ]
            laps, grads = [], []
            for h in range(2):
                lanes = pl.ds(128 * h, 128)
                az_plus = jnp.where(last_row, zero, pltpu.roll(c[h], 7, 0))
                az_minus = jnp.where(first_row, zero, pltpu.roll(c[h], 1, 0))
                laps.append(
                    cells[f, outer, :, lanes] + cells[f, inner, :, lanes]
                    + az_plus + az_minus + ax_plus[h] + ax_minus[h] - 6.0 * c[h]
                )
                grads.append(0.5 * (ax_plus[h] - ax_minus[h]))
            center.append(c)
            laplace.append(laps)
            gradient.append(grads)
        for h in range(2):
            lanes = pl.ds(128 * h, 128)
            t, p, u = center[0][h], center[1][h], center[2][h]
            out[0, r, :, lanes] = t + dt * (
                kappa[r, :, lanes] * laplace[0][h] - advect * u * gradient[0][h]
            )
            out[1, r, :, lanes] = p + dt * (
                -sound * gradient[2][h] + pdiff * laplace[1][h]
            )
            out[2, r, :, lanes] = u + dt * (
                -press * gradient[1][h] + visc * laplace[2][h] - fric * u
            )

    turns = radial // unroll
    at_end = jnp.logical_or(y == 0, y == 3)
    busy = jnp.logical_and(
        jnp.logical_and(at_end, az > 4), az < 15
    )

    @pl.loop(0, turns)
    def _(i):
        for k in range(unroll):
            cell_row(i * unroll + k)

        pl.when(jnp.logical_and(lifts, i == turns // 4 - 1))(pass_strips)
        pl.when(jnp.logical_and(az == 12, i == turns // 4 - 1))(start_late)
        pl.when(jnp.logical_and(az == 0, i == 3 * turns // 4 - 1))(start_late)
        quarter = lax.div(i + 1, turns // 4)

        @pl.when(lax.rem(i + 1, turns // 4) == 0)
        def _():
            pl.when(jnp.logical_and(busy, quarter < 4))(
                lambda: pass_on(quarter - 1, jnp.where(quarter < 3, quarter, quarter + 1))
            )
            pl.when(jnp.logical_and(az == 15, quarter == 3))(lambda: pass_on(0, 1))
            pl.when(jnp.logical_and(jnp.logical_and(inner, az > 8), quarter < 4))(
                lambda: pass_on(round_about[0] + quarter - 1, round_about[0] + quarter)
            )

    mine = jnp.where(y == 0, round_about[0], round_about[1])
    pl.when(at_end)(lambda: pass_on(jnp.where(busy, 4, (az == 15).astype(jnp.int32)), mine))

    @pl.when(is_worker)
    def _():
        strips[az] = jnp.where(az == 1, cells[1 - region, iface], cells[2, iface])
        others = strips.at[pl.ds(0, 15)]
        remote(others, others, strip_send, strip_recv, az=az).wait_recv()
        signal(ready.at[4], region=1 - region)
        for h in range(2):
            shift = placement[pl.ds(h, 1), :]
            shift = jnp.where(is_vapor, lax.rem(128 - shift, 128), shift)
            circle = strips[:, :, pl.ds(128 * h, 128)].reshape(128, 128)
            for bit in range(7):
                step = 1 << bit
                if step < 8:
                    rolled = pltpu.roll(circle, 128 - step, 0)
                else:
                    rolled = jnp.concatenate([circle[step:], circle[:step]], axis=0)
                circle = jnp.where(lax.rem(lax.div(shift, step), 2) == 1, rolled, circle)
            turned[:, :, pl.ds(128 * h, 128)] = circle.reshape(16, 8, 128)
        pl.semaphore_wait(ready.at[4], 1)

        @pl.loop(0, n_az)
        def _(j):
            remote(
                turned.at[j], facing.at[az - 1], turn_send, turn_recv.at[az - 1],
                az=j, region=1 - region,
            ).start()

    pl.when(jnp.logical_and(inner, az == 1))(lambda: pass_on(round_about[1], chunks))

    weights = (None, pdiff, visc)

    @pl.loop(0, chunks)
    def _(c):
        edge_copy(0, c).wait_recv()
        edge_copy(1, c).wait_recv()

        @pl.loop(0, rows // unroll)
        def _(i):
            for k in range(unroll):
                r = c * rows + i * unroll + k
                for h in range(2):
                    lanes = pl.ds(128 * h, 128)
                    for f in range(3):
                        beyond = jnp.where(
                            last_row,
                            edges[1, f, r, :, lanes],
                            jnp.where(first_row, edges[0, f, r, :, lanes], zero),
                        )
                        weight = kappa[r, :, lanes] if f == 0 else weights[f]
                        out[f, r, :, lanes] += dt * (weight * beyond)

    for q in range(2):
        remote(facing.at[q], facing.at[q], turn_send, turn_recv.at[q], az=q).wait_recv()

    for h in range(2):
        lanes = pl.ds(128 * h, 128)
        own_t, own_p, own_u = [cells[f, iface, :, lanes] for f in range(3)]
        first, second = facing[0, :, lanes], facing[1, :, lanes]
        t_wick = jnp.where(is_vapor, first, own_t)
        p_vapor = jnp.where(is_vapor, own_p, first)
        u_vapor = jnp.where(is_vapor, own_u, second)
        u_wick = jnp.where(is_vapor, second, own_u)
        evap = 2.0 * (t_wick - 0.5 * p_vapor)
        shear = 1.5 * (u_vapor - u_wick)
        out[0, iface, :, lanes] += dt * jnp.where(is_vapor, 0.5 * evap, -evap)
        out[1, iface, :, lanes] += dt * jnp.where(is_vapor, evap, -0.5 * evap)
        out[2, iface, :, lanes] += dt * jnp.where(is_vapor, -shear, 0.5 * shear)
        zone = jnp.broadcast_to(zones[pl.ds(h, 1), :], (8, 128))
        wall = cells[0, radial - 1, :, lanes]
        heat = jnp.where(
            zone == 0, jnp.float32(2.0), jnp.where(zone == 2, -1.5 * (wall + 1.0), 0.0)
        )
        out[0, radial - 1, :, lanes] += dt * jnp.where(is_vapor, 0.0, heat)

    @pl.loop(0, chunks)
    def _(c):
        edge_copy(0, c).wait_send()
        edge_copy(1, c).wait_send()

    @pl.when(jnp.logical_or(inner, jnp.logical_and(region == 1, at_end)))
    def _():
        @pl.loop(jnp.where(at_end, 0, 5), jnp.where(at_end, mine, chunks))
        def _(c):
            onward_copy(0, c).wait_send()

    pl.when(has_left)(to_left.wait_send)
    pl.when(has_right)(to_right.wait_send)
    @pl.when(is_worker)
    def _():
        strip_copies[0].wait_send()
        remote(turned, turned, turn_send, turn_recv.at[0], az=az).wait_send()

    @pl.when(jnp.logical_not(jnp.logical_or(is_worker, lifted)))
    def _():
        two = facing
        remote(two, two, strip_send, strip_recv, az=az).wait_send()

    @pl.when(jnp.logical_or(lifted, lifts))
    def _():
        for c in lift_copies:
            c.wait_send()


def store_kernel(new, out, sems):
    copies = [
        pltpu.make_async_copy(new.at[f], out.at[f], sems.at[f]) for f in range(3)
    ]
    for c in copies:
        c.start()
    for c in copies:
        c.wait()


def on_device(state, conduct, zones, placement):
    fields = state[0]
    f32 = jnp.float32
    shape = fields.shape
    radial, az_cells, ax_cells = shape[1:]
    hbm = pl.BlockSpec(memory_space=pltpu.HBM)
    vmem = pl.BlockSpec(memory_space=pltpu.VMEM)
    dma = pltpu.SemaphoreType.DMA
    new = pl.pallas_call(
        step_kernel,
        out_shape=pltpu.VMEM(shape, f32),
        in_specs=[hbm] * 4,
        out_specs=vmem,
        scratch_shapes=[
            pltpu.VMEM((2, 128), jnp.int32),
            pltpu.VMEM((2, 128), jnp.int32),
            pltpu.VMEM(shape, f32),
            pltpu.VMEM(shape[1:], f32),
            pltpu.VMEM((2, 3, radial, 1, ax_cells), f32),
            pltpu.VMEM((chunks, 3, radial // chunks, 1, ax_cells), f32),
            pltpu.VMEM((2, 8, ax_cells), f32),
            pltpu.VMEM((2, 3, 8, 128), f32),
            pltpu.VMEM((2, 3, 8, 128), f32),
            pltpu.VMEM((16, 8, 256), f32),
            pltpu.VMEM((16, 8, 256), f32),
            pltpu.VMEM((2, 8, 256), f32),
            dma((4,)),
            dma((2,)),
            dma((2,)),
            dma((2, chunks)),
            dma((2, chunks)),
            dma((chunks,)),
            dma((chunks,)),
            dma((2,)),
            dma((2,)),
            dma,
            dma,
            dma,
            dma((2,)),
            pltpu.SemaphoreType.REGULAR((7,)),
        ],
        compiler_params=pltpu.CompilerParams(
            collective_id=0, has_side_effects=True, vmem_limit_bytes=24 << 20
        ),
        cost_estimate=pl.CostEstimate(
            flops=40 * fields.size, bytes_accessed=4 * 7 * conduct.size, transcendentals=0
        ),
    )(*(
        pltpu.with_memory_space_constraint(x, pltpu.HBM)
        for x in (fields, conduct[0], zones.reshape(2, 128), placement.reshape(2, 128))
    ))
    result = pl.pallas_call(
        store_kernel,
        out_shape=jax.ShapeDtypeStruct(shape, f32),
        in_specs=[vmem],
        out_specs=hbm,
        scratch_shapes=[dma((3,))],
        compiler_params=pltpu.CompilerParams(vmem_limit_bytes=1 << 20),
    )(pltpu.with_memory_space_constraint(new, pltpu.VMEM))
    return result[None]


def solution(mesh):
    return jax.shard_map(
        on_device,
        mesh=mesh,
        in_specs=(
            P("region", None, None, "az", "ax"),
            P("region", None, "az", "ax"),
            P("ax"),
            P("ax"),
        ),
        out_specs=P("region", None, None, "az", "ax"),
        check_vma=False,
    )
```

```python
import functools
import jax
import jax.numpy as jnp
from jax import lax
from jax.experimental import pallas as pl
from jax.experimental.pallas import tpu as pltpu
from jax.sharding import PartitionSpec as P

MESH = pl.DeviceIdType.MESH
dt = 0.05
chunks = 8
unroll = 8


def step_kernel(
    state, conduct, zone_ref, place_ref, out,
    zones, placement, cells, kappa, edges, hop, lift, packed, packed_in, sides, strips, turned, facing,
    load_sem, lift_send, lift_recv, edge_send, edge_recv, hop_send, hop_recv, side_send, side_recv,
    strip_send, strip_recv, turn_send, turn_recv, ready,
):
    region = lax.axis_index("region")
    ax = lax.axis_index("ax")
    az = lax.axis_index("az")
    n_az = lax.axis_size("az")
    n_ax = lax.axis_size("ax")
    radial = state.shape[1]
    rows = radial // chunks
    is_vapor = region == 0
    y = lax.rem(az, 4)
    nxt = lax.rem(az + 1, n_az)
    prv = lax.rem(az + n_az - 1, n_az)
    odd = lax.rem(ax, 2) == 1
    has_left = ax > 0
    has_right = ax < n_ax - 1
    is_worker = jnp.logical_or(az == 1, az == 2)
    iface = jnp.where(is_vapor, radial - 1, 0)
    swap_high = jnp.logical_or(az == 11, az == 15)
    next_later = jnp.logical_not(
        jnp.logical_or(swap_high, jnp.logical_or(az == 10, az == 14))
    )
    prev_later = jnp.logical_or(jnp.logical_or(az == 0, az == 12), swap_high)
    next_first = jnp.logical_not(next_later)
    prev_first = jnp.logical_not(prev_later)
    even = lax.rem(ax, 2) == 0
    low_end = jnp.logical_and(y == 0, region == 1)
    high_end = jnp.logical_and(y == 3, region == 1)
    inner = jnp.logical_and(
        region == 1, jnp.logical_or(az == 1, jnp.logical_or(az == 9, az == 13))
    )

    def signal(sem, **device):
        pl.semaphore_signal(sem, inc=1, device_id=device, device_id_type=MESH)

    def remote(src, dst, send, recv, **device):
        return pltpu.make_async_remote_copy(
            src_ref=src, dst_ref=dst, send_sem=send, recv_sem=recv,
            device_id=device, device_id_type=MESH,
        )

    barrier = pltpu.get_barrier_semaphore()
    pl.when(next_later)(lambda: signal(barrier, az=nxt))
    pl.when(prev_later)(lambda: signal(barrier, az=prv))
    pl.when(low_end)(lambda: signal(barrier, az=az + 3))
    pl.when(jnp.logical_and(inner, az > 8))(lambda: signal(barrier, az=az + 2))
    pl.when(even)(lambda: signal(barrier, ax=ax + 1))
    pl.when(jnp.logical_and(even, has_left))(lambda: signal(barrier, ax=ax - 1))

    loads = [
        pltpu.make_async_copy(src, dst, load_sem.at[i])
        for i, (src, dst) in enumerate(
            ((state, cells), (conduct, kappa), (zone_ref, zones), (place_ref, placement))
        )
    ]
    for c in loads:
        c.start()

    @pl.when(az < 2)
    def _():
        signal(barrier, az=2)
        pl.when(az == 0)(lambda: signal(barrier, az=1))

    @pl.when(is_worker)
    def _():
        pl.when(is_vapor)(lambda: signal(barrier, region=1))

        @pl.loop(3, n_az)
        def _(j):
            signal(barrier, az=j)

    count = (
        next_first.astype(jnp.int32)
        + prev_first.astype(jnp.int32)
        + high_end.astype(jnp.int32)
        + jnp.logical_and(high_end, az > 8).astype(jnp.int32)
        + jnp.where(odd, 1 + has_right.astype(jnp.int32), 0)
        + jnp.minimum(az, 2)
        + jnp.logical_and(is_worker, region == 1).astype(jnp.int32)
    )
    pl.when(count > 0)(lambda: pl.semaphore_wait(barrier, count))

    pl.when(next_first)(lambda: signal(ready.at[1], az=nxt))
    pl.when(prev_first)(lambda: signal(ready.at[0], az=prv))
    pl.when(high_end)(lambda: signal(ready.at[6], az=az - 3))

    @pl.when(is_worker)
    def _():
        signal(ready.at[5], az=0)
        pl.when(az == 2)(lambda: signal(ready.at[5], az=1))
        pl.when(region == 1)(lambda: signal(ready.at[5], region=0))

    def strip_source(q):
        return state.at[1 - region if q == 0 else 2, iface]

    strip_copies = [
        remote(strip_source(q), strips.at[az], strip_send, strip_recv, az=1 + q)
        for q in range(2)
    ]
    lifted = az < 0
    lifts = az < 0
    lift_copies = [
        remote(strip_source(q), lift.at[q], lift_send.at[q], lift_recv.at[q], az=12)
        for q in range(2)
    ]
    lifted_copies = [
        remote(lift.at[q], strips.at[15], lift_send.at[q], strip_recv, az=1 + q)
        for q in range(2)
    ]

    def start_all(copies):
        for c in copies:
            c.start()

    def pass_strips():
        for q in range(2):
            lift_copies[q].wait_recv()
            lifted_copies[q].start()

    pl.when(jnp.logical_and(az > 2, jnp.logical_not(lifted)))(lambda: start_all(strip_copies))
    pl.when(lifted)(lambda: start_all(lift_copies))

    far = (high_end, low_end)
    neighbour = (nxt, prv)

    def edge_source(d, c):
        return state.at[:, pl.ds(c * rows, rows), pl.ds(7 - 7 * d, 1), :]

    def edge_copy(d, c):
        return remote(
            edge_source(d, c), edges.at[d, :, pl.ds(c * rows, rows)],
            edge_send.at[d], edge_recv.at[d, c], az=neighbour[d],
        )

    round_about = (
        jnp.where(az < 8, 7, 5),
        jnp.where(az < 4, 7, jnp.where(az < 12, 5, 6)),
    )
    rest_inner = (jnp.logical_and(high_end, az > 8), jnp.logical_and(low_end, az == 0))

    def detour_copy(d, c):
        way = jnp.where(c < round_about[d], 3, 2 - d)
        return remote(
            edge_source(d, c), hop.at[c], edge_send.at[d], hop_recv.at[c],
            az=az - way if d == 0 else az + way,
        )

    upward = jnp.logical_or(lax.rem(y, 2) == 0, jnp.logical_or(az == 9, az == 13))
    onward_even = lax.rem(az + 4 - y, n_az)
    onward_odd = lax.rem(az + n_az - 1 - y, n_az)

    def onward_copy(d, c):
        return remote(
            hop.at[c], edges.at[d, :, pl.ds(c * rows, rows)], hop_send.at[c], edge_recv.at[d, c],
            az=onward_even if d == 0 else onward_odd,
        )

    def start_part(d, first, last):
        @pl.loop(first, last)
        def _(c):
            detour = jnp.logical_and(far[d], jnp.logical_or(c < round_about[d], rest_inner[d]))
            pl.when(detour)(lambda: detour_copy(d, c).start())
            pl.when(jnp.logical_not(detour))(lambda: edge_copy(d, c).start())

    def start(d):
        start_part(d, 0, chunks)

    def pass_on(first, last):
        @pl.when(region == 1)
        def _():
            @pl.loop(first, last)
            def _(c):
                remote(hop.at[c], hop.at[c], hop_send.at[c], hop_recv.at[c], az=nxt).wait_recv()
                pl.when(upward)(lambda: onward_copy(0, c).start())
                pl.when(jnp.logical_not(upward))(lambda: onward_copy(1, c).start())

    last_straight = jnp.logical_and(az == 15, is_vapor)
    pl.when(jnp.logical_and(next_first, jnp.logical_not(last_straight)))(lambda: start(0))
    pl.when(prev_first)(
        lambda: start_part(1, jnp.where(low_end, round_about[1], 0), chunks)
    )

    @pl.when(odd)
    def _():
        signal(ready.at[3], ax=ax - 1)
        pl.when(has_right)(lambda: signal(ready.at[2], ax=ax + 1))

    for c in loads:
        c.wait()

    pl.when(last_straight)(lambda: start(0))

    lane = lax.broadcasted_iota(jnp.int32, (8, 128), 1)
    first_lane = lane == 0
    last_lane = lane == 127
    sub = lax.broadcasted_iota(jnp.int32, (8, 128), 0)
    first_row = sub == 0
    last_row = sub == 7

    def pack(r, held):
        mine = lane == r
        before = lane == lax.rem(r + 127, 128)
        got = []
        for f in range(3):
            left = pltpu.roll(cells[f, r, :, :128], lax.rem(r + 127, 128), 1)
            right = pltpu.roll(cells[f, r, :, 128:], lax.rem(r + 1, 128), 1)
            got.append(jnp.where(before, left, held[2 * f]))
            got.append(jnp.where(mine, right, held[2 * f + 1]))
        return tuple(got)

    columns = lax.fori_loop(
        0, radial, pack, tuple(jnp.zeros((8, 128), jnp.float32) for _ in range(6)), unroll=8
    )
    for f in range(3):
        packed[0, f] = columns[2 * f]
        packed[1, f] = columns[2 * f + 1]

    to_left = remote(packed.at[0], sides.at[1], side_send.at[0], side_recv.at[1], ax=ax - 1)
    to_right = remote(packed.at[1], sides.at[0], side_send.at[1], side_recv.at[0], ax=ax + 1)

    @pl.when(has_left)
    def _():
        pl.when(even)(lambda: pl.semaphore_wait(ready.at[2], 1))
        to_left.start()

    @pl.when(has_right)
    def _():
        pl.when(even)(lambda: pl.semaphore_wait(ready.at[3], 1))
        to_right.start()

    @pl.when(az < 3)
    def _():
        later = jnp.where(az == 0, 2, 2 - az + jnp.where(is_vapor, 1, 0))
        pl.when(later > 0)(lambda: pl.semaphore_wait(ready.at[5], later))
        for q in range(2):
            pl.when(az != 1 + q)(strip_copies[q].start)

    @pl.when(next_later)
    def _():
        pl.semaphore_wait(ready.at[0], 1)
        start(0)

    @pl.when(low_end)
    def _():
        pl.semaphore_wait(ready.at[6], 1)
        pl.when(prev_first)(lambda: start_part(1, 0, round_about[1]))

    def start_late():
        pl.semaphore_wait(ready.at[1], 1)
        start(1)

    pl.when(swap_high)(start_late)

    @pl.when(has_left)
    def _():
        to_right.wait_recv()

    @pl.when(jnp.logical_not(has_left))
    def _():
        sides[0] = jnp.zeros((3, 8, 128), jnp.float32)

    @pl.when(has_right)
    def _():
        to_left.wait_recv()

    @pl.when(jnp.logical_not(has_right))
    def _():
        sides[1] = jnp.zeros((3, 8, 128), jnp.float32)

    in_even = lax.rem(lane, 2) == 0
    for f in range(3):
        from_left, from_right = sides[0, f], sides[1, f]
        packed_in[0, f] = jnp.where(in_even, from_left, from_right)
        packed_in[1, f] = jnp.where(in_even, from_right, from_left)

    def pick(vapor, wick):
        return jnp.where(is_vapor, jnp.float32(vapor), jnp.float32(wick))

    press = pick(1.0, 0.6)
    visc = pick(0.3, 0.05)
    fric = pick(0.1, 2.0)
    sound = pick(1.5, 0.8)
    pdiff = pick(0.2, 0.4)
    advect = pick(1.0, 0.5)
    zero = jnp.float32(0.0)

    def cell_row(r, parity):
        inner = jnp.maximum(r - 1, 0)
        outer = jnp.minimum(r + 1, radial - 1)
        to_first = lax.rem(128 - r, 128)
        center, laplace, gradient = [], [], []
        for f in range(3):
            c = [cells[f, r, :, :128], cells[f, r, :, 128:]]
            plus = [pltpu.roll(c[0], 127, 1), pltpu.roll(c[1], 127, 1)]
            minus = [pltpu.roll(c[0], 1, 1), pltpu.roll(c[1], 1, 1)]
            beside = pltpu.roll(packed_in[parity, f], to_first, 1)
            ax_plus = [
                jnp.where(last_lane, plus[1], plus[0]),
                jnp.where(last_lane, beside, plus[1]),
            ]
            ax_minus = [
                jnp.where(first_lane, beside, minus[0]),
                jnp.where(first_lane, minus[0], minus[1]),
            ]
            laps, grads = [], []
            for h in range(2):
                lanes = pl.ds(128 * h, 128)
                az_plus = jnp.where(last_row, zero, pltpu.roll(c[h], 7, 0))
                az_minus = jnp.where(first_row, zero, pltpu.roll(c[h], 1, 0))
                laps.append(
                    cells[f, outer, :, lanes] + cells[f, inner, :, lanes]
                    + az_plus + az_minus + ax_plus[h] + ax_minus[h] - 6.0 * c[h]
                )
                grads.append(0.5 * (ax_plus[h] - ax_minus[h]))
            center.append(c)
            laplace.append(laps)
            gradient.append(grads)
        for h in range(2):
            lanes = pl.ds(128 * h, 128)
            t, p, u = center[0][h], center[1][h], center[2][h]
            out[0, r, :, lanes] = t + dt * (
                kappa[r, :, lanes] * laplace[0][h] - advect * u * gradient[0][h]
            )
            out[1, r, :, lanes] = p + dt * (
                -sound * gradient[2][h] + pdiff * laplace[1][h]
            )
            out[2, r, :, lanes] = u + dt * (
                -press * gradient[1][h] + visc * laplace[2][h] - fric * u
            )

    turns = radial // unroll
    at_end = jnp.logical_or(y == 0, y == 3)
    busy = jnp.logical_and(
        jnp.logical_and(at_end, az > 4), az < 15
    )

    @pl.loop(0, turns)
    def _(i):
        for k in range(unroll):
            cell_row(i * unroll + k, k % 2)

        pl.when(jnp.logical_and(lifts, i == turns // 4 - 1))(pass_strips)
        pl.when(jnp.logical_and(az == 12, i == turns // 4 - 1))(start_late)
        pl.when(jnp.logical_and(az == 0, i == 3 * turns // 4 - 1))(start_late)
        quarter = lax.div(i + 1, turns // 4)

        @pl.when(lax.rem(i + 1, turns // 4) == 0)
        def _():
            pl.when(jnp.logical_and(busy, quarter < 4))(
                lambda: pass_on(quarter - 1, jnp.where(quarter < 3, quarter, quarter + 1))
            )
            pl.when(jnp.logical_and(az == 15, quarter == 3))(lambda: pass_on(0, 1))
            pl.when(jnp.logical_and(jnp.logical_and(inner, az > 8), quarter < 4))(
                lambda: pass_on(round_about[0] + quarter - 1, round_about[0] + quarter)
            )

    mine = jnp.where(y == 0, round_about[0], round_about[1])
    pl.when(at_end)(lambda: pass_on(jnp.where(busy, 4, (az == 15).astype(jnp.int32)), mine))

    @pl.when(is_worker)
    def _():
        strips[az] = jnp.where(az == 1, cells[1 - region, iface], cells[2, iface])
        others = strips.at[pl.ds(0, 15)]
        remote(others, others, strip_send, strip_recv, az=az).wait_recv()
        signal(ready.at[4], region=1 - region)
        for h in range(2):
            shift = placement[pl.ds(h, 1), :]
            shift = jnp.where(is_vapor, lax.rem(128 - shift, 128), shift)
            circle = strips[:, :, pl.ds(128 * h, 128)].reshape(128, 128)
            for bit in range(7):
                step = 1 << bit
                if step < 8:
                    rolled = pltpu.roll(circle, 128 - step, 0)
                else:
                    rolled = jnp.concatenate([circle[step:], circle[:step]], axis=0)
                circle = jnp.where(lax.rem(lax.div(shift, step), 2) == 1, rolled, circle)
            turned[:, :, pl.ds(128 * h, 128)] = circle.reshape(16, 8, 128)
        pl.semaphore_wait(ready.at[4], 1)

        @pl.loop(0, n_az)
        def _(j):
            remote(
                turned.at[j], facing.at[az - 1], turn_send, turn_recv.at[az - 1],
                az=j, region=1 - region,
            ).start()

    pl.when(jnp.logical_and(inner, az == 1))(lambda: pass_on(round_about[1], chunks))

    weights = (None, pdiff, visc)

    @pl.loop(0, chunks)
    def _(c):
        edge_copy(0, c).wait_recv()
        edge_copy(1, c).wait_recv()

        @pl.loop(0, rows // unroll)
        def _(i):
            for k in range(unroll):
                r = c * rows + i * unroll + k
                for h in range(2):
                    lanes = pl.ds(128 * h, 128)
                    for f in range(3):
                        beyond = jnp.where(
                            last_row,
                            edges[1, f, r, :, lanes],
                            jnp.where(first_row, edges[0, f, r, :, lanes], zero),
                        )
                        weight = kappa[r, :, lanes] if f == 0 else weights[f]
                        out[f, r, :, lanes] += dt * (weight * beyond)

    for q in range(2):
        remote(facing.at[q], facing.at[q], turn_send, turn_recv.at[q], az=q).wait_recv()

    for h in range(2):
        lanes = pl.ds(128 * h, 128)
        own_t, own_p, own_u = [cells[f, iface, :, lanes] for f in range(3)]
        first, second = facing[0, :, lanes], facing[1, :, lanes]
        t_wick = jnp.where(is_vapor, first, own_t)
        p_vapor = jnp.where(is_vapor, own_p, first)
        u_vapor = jnp.where(is_vapor, own_u, second)
        u_wick = jnp.where(is_vapor, second, own_u)
        evap = 2.0 * (t_wick - 0.5 * p_vapor)
        shear = 1.5 * (u_vapor - u_wick)
        out[0, iface, :, lanes] += dt * jnp.where(is_vapor, 0.5 * evap, -evap)
        out[1, iface, :, lanes] += dt * jnp.where(is_vapor, evap, -0.5 * evap)
        out[2, iface, :, lanes] += dt * jnp.where(is_vapor, -shear, 0.5 * shear)
        zone = jnp.broadcast_to(zones[pl.ds(h, 1), :], (8, 128))
        wall = cells[0, radial - 1, :, lanes]
        heat = jnp.where(
            zone == 0, jnp.float32(2.0), jnp.where(zone == 2, -1.5 * (wall + 1.0), 0.0)
        )
        out[0, radial - 1, :, lanes] += dt * jnp.where(is_vapor, 0.0, heat)

    for d in range(2):
        remote(edges.at[d], edges.at[d], edge_send.at[d], edge_recv.at[d, 0], az=nxt).wait_send()

    @pl.when(jnp.logical_or(inner, jnp.logical_and(region == 1, at_end)))
    def _():
        @pl.loop(jnp.where(at_end, 0, jnp.where(az == 1, round_about[1], round_about[0])), jnp.where(at_end, mine, chunks))
        def _(c):
            onward_copy(0, c).wait_send()

    pl.when(has_left)(to_left.wait_send)
    pl.when(has_right)(to_right.wait_send)
    @pl.when(is_worker)
    def _():
        strip_copies[0].wait_send()
        remote(turned, turned, turn_send, turn_recv.at[0], az=az).wait_send()

    @pl.when(jnp.logical_not(jnp.logical_or(is_worker, lifted)))
    def _():
        two = facing
        remote(two, two, strip_send, strip_recv, az=az).wait_send()

    @pl.when(jnp.logical_or(lifted, lifts))
    def _():
        for c in lift_copies:
            c.wait_send()


def store_kernel(new, out, sems):
    copies = [
        pltpu.make_async_copy(new.at[f], out.at[f], sems.at[f]) for f in range(3)
    ]
    for c in copies:
        c.start()
    for c in copies:
        c.wait()


def on_device(state, conduct, zones, placement):
    fields = state[0]
    f32 = jnp.float32
    shape = fields.shape
    radial, az_cells, ax_cells = shape[1:]
    hbm = pl.BlockSpec(memory_space=pltpu.HBM)
    vmem = pl.BlockSpec(memory_space=pltpu.VMEM)
    dma = pltpu.SemaphoreType.DMA
    new = pl.pallas_call(
        step_kernel,
        out_shape=pltpu.VMEM(shape, f32),
        in_specs=[hbm] * 4,
        out_specs=vmem,
        scratch_shapes=[
            pltpu.VMEM((2, 128), jnp.int32),
            pltpu.VMEM((2, 128), jnp.int32),
            pltpu.VMEM(shape, f32),
            pltpu.VMEM(shape[1:], f32),
            pltpu.VMEM((2, 3, radial, 1, ax_cells), f32),
            pltpu.VMEM((chunks, 3, radial // chunks, 1, ax_cells), f32),
            pltpu.VMEM((2, 8, ax_cells), f32),
            pltpu.VMEM((2, 3, 8, 128), f32),
            pltpu.VMEM((2, 3, 8, 128), f32),
            pltpu.VMEM((2, 3, 8, 128), f32),
            pltpu.VMEM((16, 8, 256), f32),
            pltpu.VMEM((16, 8, 256), f32),
            pltpu.VMEM((2, 8, 256), f32),
            dma((4,)),
            dma((2,)),
            dma((2,)),
            dma((2,)),
            dma((2, chunks)),
            dma((chunks,)),
            dma((chunks,)),
            dma((2,)),
            dma((2,)),
            dma,
            dma,
            dma,
            dma((2,)),
            pltpu.SemaphoreType.REGULAR((7,)),
        ],
        compiler_params=pltpu.CompilerParams(
            collective_id=0, has_side_effects=True, vmem_limit_bytes=24 << 20
        ),
        cost_estimate=pl.CostEstimate(
            flops=40 * fields.size, bytes_accessed=4 * 7 * conduct.size, transcendentals=0
        ),
    )(*(
        pltpu.with_memory_space_constraint(x, pltpu.HBM)
        for x in (fields, conduct[0], zones.reshape(2, 128), placement.reshape(2, 128))
    ))
    result = pl.pallas_call(
        store_kernel,
        out_shape=jax.ShapeDtypeStruct(shape, f32),
        in_specs=[vmem],
        out_specs=hbm,
        scratch_shapes=[dma((3,))],
        compiler_params=pltpu.CompilerParams(vmem_limit_bytes=1 << 20),
    )(pltpu.with_memory_space_constraint(new, pltpu.VMEM))
    return result[None]


def solution(mesh):
    return jax.shard_map(
        on_device,
        mesh=mesh,
        in_specs=(
            P("region", None, None, "az", "ax"),
            P("region", None, "az", "ax"),
            P("ax"),
            P("ax"),
        ),
        out_specs=P("region", None, None, "az", "ax"),
        check_vma=False,
    )
```

```python
import functools
import jax
import jax.numpy as jnp
from jax import lax
from jax.experimental import pallas as pl
from jax.experimental.pallas import tpu as pltpu
from jax.sharding import PartitionSpec as P

MESH = pl.DeviceIdType.MESH
dt = 0.05
chunks = 8
unroll = 8


def step_kernel(
    state, conduct, zone_ref, place_ref, out,
    zones, placement, cells, kappa, edges, hop, packed, packed_in, sides, strips, turned, facing,
    load_sem, edge_send, edge_recv, hop_send, hop_recv, side_send, side_recv,
    strip_send, strip_recv, turn_send, turn_recv, ready,
):
    region = lax.axis_index("region")
    ax = lax.axis_index("ax")
    az = lax.axis_index("az")
    n_az = lax.axis_size("az")
    n_ax = lax.axis_size("ax")
    radial = state.shape[1]
    rows = radial // chunks
    is_vapor = region == 0
    y = lax.rem(az, 4)
    nxt = lax.rem(az + 1, n_az)
    prv = lax.rem(az + n_az - 1, n_az)
    odd = lax.rem(ax, 2) == 1
    has_left = ax > 0
    has_right = ax < n_ax - 1
    is_worker = jnp.logical_or(az == 1, az == 2)
    iface = jnp.where(is_vapor, radial - 1, 0)
    swap_high = jnp.logical_or(az == 11, az == 15)
    next_later = jnp.logical_not(
        jnp.logical_or(swap_high, jnp.logical_or(az == 10, az == 14))
    )
    prev_later = jnp.logical_or(jnp.logical_or(az == 0, az == 12), swap_high)
    next_first = jnp.logical_not(next_later)
    prev_first = jnp.logical_not(prev_later)
    even = lax.rem(ax, 2) == 0
    low_end = jnp.logical_and(y == 0, region == 1)
    high_end = jnp.logical_and(y == 3, region == 1)
    inner = jnp.logical_and(
        region == 1, jnp.logical_or(az == 1, jnp.logical_or(az == 9, az == 13))
    )

    def signal(sem, **device):
        pl.semaphore_signal(sem, inc=1, device_id=device, device_id_type=MESH)

    def remote(src, dst, send, recv, **device):
        return pltpu.make_async_remote_copy(
            src_ref=src, dst_ref=dst, send_sem=send, recv_sem=recv,
            device_id=device, device_id_type=MESH,
        )

    barrier = pltpu.get_barrier_semaphore()
    pl.when(next_later)(lambda: signal(barrier, az=nxt))
    pl.when(prev_later)(lambda: signal(barrier, az=prv))
    pl.when(low_end)(lambda: signal(barrier, az=az + 3))
    pl.when(jnp.logical_and(inner, az > 8))(lambda: signal(barrier, az=az + 2))
    pl.when(even)(lambda: signal(barrier, ax=ax + 1))
    pl.when(jnp.logical_and(even, has_left))(lambda: signal(barrier, ax=ax - 1))

    loads = [
        pltpu.make_async_copy(src, dst, load_sem.at[i])
        for i, (src, dst) in enumerate(
            ((state, cells), (conduct, kappa), (zone_ref, zones), (place_ref, placement))
        )
    ]
    for c in loads:
        c.start()

    @pl.when(az < 2)
    def _():
        signal(barrier, az=2)
        pl.when(az == 0)(lambda: signal(barrier, az=1))

    @pl.when(is_worker)
    def _():
        pl.when(is_vapor)(lambda: signal(barrier, region=1))

        @pl.loop(3, n_az)
        def _(j):
            signal(barrier, az=j)

    count = (
        next_first.astype(jnp.int32)
        + prev_first.astype(jnp.int32)
        + high_end.astype(jnp.int32)
        + jnp.logical_and(high_end, az > 8).astype(jnp.int32)
        + jnp.where(odd, 1 + has_right.astype(jnp.int32), 0)
        + jnp.minimum(az, 2)
        + jnp.logical_and(is_worker, region == 1).astype(jnp.int32)
    )
    pl.when(count > 0)(lambda: pl.semaphore_wait(barrier, count))

    pl.when(next_first)(lambda: signal(ready.at[1], az=nxt))
    pl.when(prev_first)(lambda: signal(ready.at[0], az=prv))
    pl.when(high_end)(lambda: signal(ready.at[6], az=az - 3))

    @pl.when(is_worker)
    def _():
        signal(ready.at[5], az=0)
        pl.when(az == 2)(lambda: signal(ready.at[5], az=1))
        pl.when(region == 1)(lambda: signal(ready.at[5], region=0))

    def strip_source(q):
        return state.at[1 - region if q == 0 else 2, iface]

    strip_copies = [
        remote(strip_source(q), strips.at[az], strip_send, strip_recv, az=1 + q)
        for q in range(2)
    ]
    def start_all(copies):
        for c in copies:
            c.start()

    pl.when(az > 2)(lambda: start_all(strip_copies))

    far = (high_end, low_end)
    neighbour = (nxt, prv)

    def edge_source(d, c):
        return state.at[:, pl.ds(c * rows, rows), pl.ds(7 - 7 * d, 1), :]

    def edge_copy(d, c):
        return remote(
            edge_source(d, c), edges.at[d, :, pl.ds(c * rows, rows)],
            edge_send.at[d], edge_recv.at[d, c], az=neighbour[d],
        )

    round_about = (
        jnp.where(az < 8, jnp.where(odd, 5, 8), 5),
        jnp.where(az < 4, 7, jnp.where(az < 12, 5, 6)),
    )
    rest_inner = (jnp.logical_and(high_end, az > 8), jnp.logical_and(low_end, az == 0))

    def detour_copy(d, c):
        way = jnp.where(c < round_about[d], 3, 2 - d)
        return remote(
            edge_source(d, c), hop.at[c], edge_send.at[d], hop_recv.at[c],
            az=az - way if d == 0 else az + way,
        )

    upward = jnp.logical_or(lax.rem(y, 2) == 0, jnp.logical_or(az == 9, az == 13))
    onward_even = lax.rem(az + 4 - y, n_az)
    onward_odd = lax.rem(az + n_az - 1 - y, n_az)

    def onward_copy(d, c):
        return remote(
            hop.at[c], edges.at[d, :, pl.ds(c * rows, rows)], hop_send.at[c], edge_recv.at[d, c],
            az=onward_even if d == 0 else onward_odd,
        )

    def start_part(d, first, last):
        @pl.loop(first, last)
        def _(c):
            detour = jnp.logical_and(far[d], jnp.logical_or(c < round_about[d], rest_inner[d]))
            pl.when(detour)(lambda: detour_copy(d, c).start())
            pl.when(jnp.logical_not(detour))(lambda: edge_copy(d, c).start())

    def start(d):
        start_part(d, 0, chunks)

    def pass_on(first, last):
        @pl.when(region == 1)
        def _():
            @pl.loop(first, last)
            def _(c):
                remote(hop.at[c], hop.at[c], hop_send.at[c], hop_recv.at[c], az=nxt).wait_recv()
                pl.when(upward)(lambda: onward_copy(0, c).start())
                pl.when(jnp.logical_not(upward))(lambda: onward_copy(1, c).start())

    last_straight = jnp.logical_and(az == 15, is_vapor)
    pl.when(jnp.logical_and(next_first, jnp.logical_not(last_straight)))(lambda: start(0))
    pl.when(prev_first)(
        lambda: start_part(1, jnp.where(low_end, round_about[1], 0), chunks)
    )

    @pl.when(odd)
    def _():
        signal(ready.at[3], ax=ax - 1)
        pl.when(has_right)(lambda: signal(ready.at[2], ax=ax + 1))

    for c in loads:
        c.wait()

    pl.when(last_straight)(lambda: start(0))

    lane = lax.broadcasted_iota(jnp.int32, (8, 128), 1)
    first_lane = lane == 0
    last_lane = lane == 127
    sub = lax.broadcasted_iota(jnp.int32, (8, 128), 0)
    first_row = sub == 0
    last_row = sub == 7

    def pack(r, held):
        mine = lane == r
        before = lane == lax.rem(r + 127, 128)
        got = []
        for f in range(3):
            left = pltpu.roll(cells[f, r, :, :128], lax.rem(r + 127, 128), 1)
            right = pltpu.roll(cells[f, r, :, 128:], lax.rem(r + 1, 128), 1)
            got.append(jnp.where(before, left, held[2 * f]))
            got.append(jnp.where(mine, right, held[2 * f + 1]))
        return tuple(got)

    columns = lax.fori_loop(
        0, radial, pack, tuple(jnp.zeros((8, 128), jnp.float32) for _ in range(6)), unroll=8
    )
    for f in range(3):
        packed[0, f] = columns[2 * f]
        packed[1, f] = columns[2 * f + 1]

    to_left = remote(packed.at[0], sides.at[1], side_send.at[0], side_recv.at[1], ax=ax - 1)
    to_right = remote(packed.at[1], sides.at[0], side_send.at[1], side_recv.at[0], ax=ax + 1)

    @pl.when(has_left)
    def _():
        pl.when(even)(lambda: pl.semaphore_wait(ready.at[2], 1))
        to_left.start()

    @pl.when(has_right)
    def _():
        pl.when(even)(lambda: pl.semaphore_wait(ready.at[3], 1))
        to_right.start()

    @pl.when(az < 3)
    def _():
        later = jnp.where(az == 0, 2, 2 - az + jnp.where(is_vapor, 1, 0))
        pl.when(later > 0)(lambda: pl.semaphore_wait(ready.at[5], later))
        for q in range(2):
            pl.when(az != 1 + q)(strip_copies[q].start)

    @pl.when(next_later)
    def _():
        pl.semaphore_wait(ready.at[0], 1)
        start(0)

    @pl.when(low_end)
    def _():
        pl.semaphore_wait(ready.at[6], 1)
        pl.when(prev_first)(lambda: start_part(1, 0, round_about[1]))

    def start_late():
        pl.semaphore_wait(ready.at[1], 1)
        start(1)

    pl.when(swap_high)(start_late)

    @pl.when(has_left)
    def _():
        to_right.wait_recv()

    @pl.when(jnp.logical_not(has_left))
    def _():
        sides[0] = jnp.zeros((3, 8, 128), jnp.float32)

    @pl.when(has_right)
    def _():
        to_left.wait_recv()

    @pl.when(jnp.logical_not(has_right))
    def _():
        sides[1] = jnp.zeros((3, 8, 128), jnp.float32)

    in_even = lax.rem(lane, 2) == 0
    for f in range(3):
        from_left, from_right = sides[0, f], sides[1, f]
        packed_in[0, f] = jnp.where(in_even, from_left, from_right)
        packed_in[1, f] = jnp.where(in_even, from_right, from_left)

    def pick(vapor, wick):
        return jnp.where(is_vapor, jnp.float32(vapor), jnp.float32(wick))

    press = pick(1.0, 0.6)
    visc = pick(0.3, 0.05)
    fric = pick(0.1, 2.0)
    sound = pick(1.5, 0.8)
    pdiff = pick(0.2, 0.4)
    advect = pick(1.0, 0.5)
    zero = jnp.float32(0.0)

    def cell_row(r, parity):
        inner = jnp.maximum(r - 1, 0)
        outer = jnp.minimum(r + 1, radial - 1)
        to_first = lax.rem(128 - r, 128)
        center, laplace, gradient = [], [], []
        for f in range(3):
            c = [cells[f, r, :, :128], cells[f, r, :, 128:]]
            plus = [pltpu.roll(c[0], 127, 1), pltpu.roll(c[1], 127, 1)]
            minus = [pltpu.roll(c[0], 1, 1), pltpu.roll(c[1], 1, 1)]
            beside = pltpu.roll(packed_in[parity, f], to_first, 1)
            ax_plus = [
                jnp.where(last_lane, plus[1], plus[0]),
                jnp.where(last_lane, beside, plus[1]),
            ]
            ax_minus = [
                jnp.where(first_lane, beside, minus[0]),
                jnp.where(first_lane, minus[0], minus[1]),
            ]
            laps, grads = [], []
            for h in range(2):
                lanes = pl.ds(128 * h, 128)
                az_plus = jnp.where(last_row, zero, pltpu.roll(c[h], 7, 0))
                az_minus = jnp.where(first_row, zero, pltpu.roll(c[h], 1, 0))
                laps.append(
                    cells[f, outer, :, lanes] + cells[f, inner, :, lanes]
                    + az_plus + az_minus + ax_plus[h] + ax_minus[h] - 6.0 * c[h]
                )
                grads.append(0.5 * (ax_plus[h] - ax_minus[h]))
            center.append(c)
            laplace.append(laps)
            gradient.append(grads)
        for h in range(2):
            lanes = pl.ds(128 * h, 128)
            t, p, u = center[0][h], center[1][h], center[2][h]
            out[0, r, :, lanes] = t + dt * (
                kappa[r, :, lanes] * laplace[0][h] - advect * u * gradient[0][h]
            )
            out[1, r, :, lanes] = p + dt * (
                -sound * gradient[2][h] + pdiff * laplace[1][h]
            )
            out[2, r, :, lanes] = u + dt * (
                -press * gradient[1][h] + visc * laplace[2][h] - fric * u
            )

    turns = radial // unroll
    at_end = jnp.logical_or(y == 0, y == 3)
    busy = jnp.logical_and(
        jnp.logical_and(at_end, az > 4), az < 15
    )

    @pl.loop(0, turns)
    def _(i):
        for k in range(unroll):
            cell_row(i * unroll + k, k % 2)

        pl.when(jnp.logical_and(az == 12, i == turns // 4 - 1))(start_late)
        pl.when(jnp.logical_and(az == 0, i == 3 * turns // 4 - 1))(start_late)
        quarter = lax.div(i + 1, turns // 4)

        @pl.when(lax.rem(i + 1, turns // 4) == 0)
        def _():
            pl.when(jnp.logical_and(busy, quarter < 4))(
                lambda: pass_on(quarter - 1, jnp.where(quarter < 3, quarter, quarter + 1))
            )
            pl.when(jnp.logical_and(az == 15, quarter == 3))(lambda: pass_on(0, 1))
            pl.when(jnp.logical_and(jnp.logical_and(inner, az > 8), quarter < 4))(
                lambda: pass_on(round_about[0] + quarter - 1, round_about[0] + quarter)
            )

    mine = jnp.where(y == 0, round_about[0], round_about[1])
    pl.when(at_end)(lambda: pass_on(jnp.where(busy, 4, (az == 15).astype(jnp.int32)), mine))

    @pl.when(is_worker)
    def _():
        strips[az] = jnp.where(az == 1, cells[1 - region, iface], cells[2, iface])
        others = strips.at[pl.ds(0, 15)]
        remote(others, others, strip_send, strip_recv, az=az).wait_recv()
        signal(ready.at[4], region=1 - region)
        for h in range(2):
            shift = placement[pl.ds(h, 1), :]
            shift = jnp.where(is_vapor, lax.rem(128 - shift, 128), shift)
            circle = strips[:, :, pl.ds(128 * h, 128)].reshape(128, 128)
            for bit in range(7):
                step = 1 << bit
                if step < 8:
                    rolled = pltpu.roll(circle, 128 - step, 0)
                else:
                    rolled = jnp.concatenate([circle[step:], circle[:step]], axis=0)
                circle = jnp.where(lax.rem(lax.div(shift, step), 2) == 1, rolled, circle)
            turned[:, :, pl.ds(128 * h, 128)] = circle.reshape(16, 8, 128)
        pl.semaphore_wait(ready.at[4], 1)

        @pl.loop(0, n_az)
        def _(j):
            remote(
                turned.at[j], facing.at[az - 1], turn_send, turn_recv.at[az - 1],
                az=j, region=1 - region,
            ).start()

    pl.when(jnp.logical_and(inner, az == 1))(lambda: pass_on(round_about[1], chunks))

    weights = (None, pdiff, visc)

    @pl.loop(0, chunks)
    def _(c):
        edge_copy(0, c).wait_recv()
        edge_copy(1, c).wait_recv()

        @pl.loop(0, rows // unroll)
        def _(i):
            for k in range(unroll):
                r = c * rows + i * unroll + k
                for h in range(2):
                    lanes = pl.ds(128 * h, 128)
                    for f in range(3):
                        beyond = jnp.where(
                            last_row,
                            edges[1, f, r, :, lanes],
                            jnp.where(first_row, edges[0, f, r, :, lanes], zero),
                        )
                        weight = kappa[r, :, lanes] if f == 0 else weights[f]
                        out[f, r, :, lanes] += dt * (weight * beyond)

    for q in range(2):
        remote(facing.at[q], facing.at[q], turn_send, turn_recv.at[q], az=q).wait_recv()

    for h in range(2):
        lanes = pl.ds(128 * h, 128)
        own_t, own_p, own_u = [cells[f, iface, :, lanes] for f in range(3)]
        first, second = facing[0, :, lanes], facing[1, :, lanes]
        t_wick = jnp.where(is_vapor, first, own_t)
        p_vapor = jnp.where(is_vapor, own_p, first)
        u_vapor = jnp.where(is_vapor, own_u, second)
        u_wick = jnp.where(is_vapor, second, own_u)
        evap = 2.0 * (t_wick - 0.5 * p_vapor)
        shear = 1.5 * (u_vapor - u_wick)
        out[0, iface, :, lanes] += dt * jnp.where(is_vapor, 0.5 * evap, -evap)
        out[1, iface, :, lanes] += dt * jnp.where(is_vapor, evap, -0.5 * evap)
        out[2, iface, :, lanes] += dt * jnp.where(is_vapor, -shear, 0.5 * shear)
        zone = jnp.broadcast_to(zones[pl.ds(h, 1), :], (8, 128))
        wall = cells[0, radial - 1, :, lanes]
        heat = jnp.where(
            zone == 0, jnp.float32(2.0), jnp.where(zone == 2, -1.5 * (wall + 1.0), 0.0)
        )
        out[0, radial - 1, :, lanes] += dt * jnp.where(is_vapor, 0.0, heat)

    for d in range(2):
        remote(edges.at[d], edges.at[d], edge_send.at[d], edge_recv.at[d, 0], az=nxt).wait_send()

    @pl.when(jnp.logical_or(inner, jnp.logical_and(region == 1, at_end)))
    def _():
        @pl.loop(jnp.where(at_end, 0, jnp.where(az == 1, round_about[1], round_about[0])), jnp.where(at_end, mine, chunks))
        def _(c):
            onward_copy(0, c).wait_send()

    pl.when(has_left)(to_left.wait_send)
    pl.when(has_right)(to_right.wait_send)
    @pl.when(is_worker)
    def _():
        strip_copies[0].wait_send()
        remote(turned, turned, turn_send, turn_recv.at[0], az=az).wait_send()

    @pl.when(jnp.logical_not(is_worker))
    def _():
        two = facing
        remote(two, two, strip_send, strip_recv, az=az).wait_send()


def store_kernel(new, out, sems):
    copies = [
        pltpu.make_async_copy(new.at[f], out.at[f], sems.at[f]) for f in range(3)
    ]
    for c in copies:
        c.start()
    for c in copies:
        c.wait()


def on_device(state, conduct, zones, placement):
    fields = state[0]
    f32 = jnp.float32
    shape = fields.shape
    radial, az_cells, ax_cells = shape[1:]
    hbm = pl.BlockSpec(memory_space=pltpu.HBM)
    vmem = pl.BlockSpec(memory_space=pltpu.VMEM)
    dma = pltpu.SemaphoreType.DMA
    new = pl.pallas_call(
        step_kernel,
        out_shape=pltpu.VMEM(shape, f32),
        in_specs=[hbm] * 4,
        out_specs=vmem,
        scratch_shapes=[
            pltpu.VMEM((2, 128), jnp.int32),
            pltpu.VMEM((2, 128), jnp.int32),
            pltpu.VMEM(shape, f32),
            pltpu.VMEM(shape[1:], f32),
            pltpu.VMEM((2, 3, radial, 1, ax_cells), f32),
            pltpu.VMEM((chunks, 3, radial // chunks, 1, ax_cells), f32),
            pltpu.VMEM((2, 3, 8, 128), f32),
            pltpu.VMEM((2, 3, 8, 128), f32),
            pltpu.VMEM((2, 3, 8, 128), f32),
            pltpu.VMEM((16, 8, 256), f32),
            pltpu.VMEM((16, 8, 256), f32),
            pltpu.VMEM((2, 8, 256), f32),
            dma((4,)),
            dma((2,)),
            dma((2, chunks)),
            dma((chunks,)),
            dma((chunks,)),
            dma((2,)),
            dma((2,)),
            dma,
            dma,
            dma,
            dma((2,)),
            pltpu.SemaphoreType.REGULAR((7,)),
        ],
        compiler_params=pltpu.CompilerParams(
            collective_id=0, has_side_effects=True, vmem_limit_bytes=24 << 20
        ),
        cost_estimate=pl.CostEstimate(
            flops=40 * fields.size, bytes_accessed=4 * 7 * conduct.size, transcendentals=0
        ),
    )(*(
        pltpu.with_memory_space_constraint(x, pltpu.HBM)
        for x in (fields, conduct[0], zones.reshape(2, 128), placement.reshape(2, 128))
    ))
    result = pl.pallas_call(
        store_kernel,
        out_shape=jax.ShapeDtypeStruct(shape, f32),
        in_specs=[vmem],
        out_specs=hbm,
        scratch_shapes=[dma((3,))],
        compiler_params=pltpu.CompilerParams(vmem_limit_bytes=1 << 20),
    )(pltpu.with_memory_space_constraint(new, pltpu.VMEM))
    return result[None]


def solution(mesh):
    return jax.shard_map(
        on_device,
        mesh=mesh,
        in_specs=(
            P("region", None, None, "az", "ax"),
            P("region", None, "az", "ax"),
            P("ax"),
            P("ax"),
        ),
        out_specs=P("region", None, None, "az", "ax"),
        check_vma=False,
    )
```

```python
import functools
import jax
import jax.numpy as jnp
from jax import lax
from jax.experimental import pallas as pl
from jax.experimental.pallas import tpu as pltpu
from jax.sharding import PartitionSpec as P

MESH = pl.DeviceIdType.MESH
dt = 0.05
chunks = 8
unroll = 8


def step_kernel(
    state, conduct, zone_ref, place_ref, out,
    zones, placement, cells, kappa, edges, hop, packed, packed_in, sides, strips, turned, facing,
    load_sem, edge_send, edge_recv, hop_send, hop_recv, side_send, side_recv,
    strip_send, strip_recv, turn_send, turn_recv, ready,
):
    region = lax.axis_index("region")
    ax = lax.axis_index("ax")
    az = lax.axis_index("az")
    n_az = lax.axis_size("az")
    n_ax = lax.axis_size("ax")
    radial = state.shape[1]
    rows = radial // chunks
    is_vapor = region == 0
    y = lax.rem(az, 4)
    nxt = lax.rem(az + 1, n_az)
    prv = lax.rem(az + n_az - 1, n_az)
    odd = lax.rem(ax, 2) == 1
    has_left = ax > 0
    has_right = ax < n_ax - 1
    is_worker = jnp.logical_or(az == 1, az == 2)
    iface = jnp.where(is_vapor, radial - 1, 0)
    swap_high = jnp.logical_or(az == 11, az == 15)
    next_later = jnp.logical_not(
        jnp.logical_or(swap_high, jnp.logical_or(az == 10, az == 14))
    )
    prev_later = jnp.logical_or(jnp.logical_or(az == 0, az == 12), swap_high)
    next_first = jnp.logical_not(next_later)
    prev_first = jnp.logical_not(prev_later)
    even = lax.rem(ax, 2) == 0
    low_end = jnp.logical_and(y == 0, region == 1)
    high_end = jnp.logical_and(y == 3, region == 1)
    inner = jnp.logical_and(
        region == 1, jnp.logical_or(az == 1, jnp.logical_or(az == 9, az == 13))
    )

    def signal(sem, **device):
        pl.semaphore_signal(sem, inc=1, device_id=device, device_id_type=MESH)

    def remote(src, dst, send, recv, **device):
        return pltpu.make_async_remote_copy(
            src_ref=src, dst_ref=dst, send_sem=send, recv_sem=recv,
            device_id=device, device_id_type=MESH,
        )

    barrier = pltpu.get_barrier_semaphore()
    pl.when(next_later)(lambda: signal(barrier, az=nxt))
    pl.when(prev_later)(lambda: signal(barrier, az=prv))
    pl.when(low_end)(lambda: signal(barrier, az=az + 3))
    pl.when(jnp.logical_and(inner, az > 8))(lambda: signal(barrier, az=az + 2))
    pl.when(even)(lambda: signal(barrier, ax=ax + 1))
    pl.when(jnp.logical_and(odd, has_right))(lambda: signal(barrier, ax=ax + 1))

    loads = [
        pltpu.make_async_copy(src, dst, load_sem.at[i])
        for i, (src, dst) in enumerate(
            ((state, cells), (conduct, kappa), (zone_ref, zones), (place_ref, placement))
        )
    ]
    for c in loads:
        c.start()

    @pl.when(az < 2)
    def _():
        signal(barrier, az=2)
        pl.when(az == 0)(lambda: signal(barrier, az=1))

    @pl.when(is_worker)
    def _():
        pl.when(is_vapor)(lambda: signal(barrier, region=1))

        @pl.loop(3, n_az)
        def _(j):
            signal(barrier, az=j)

    count = (
        next_first.astype(jnp.int32)
        + prev_first.astype(jnp.int32)
        + high_end.astype(jnp.int32)
        + jnp.logical_and(high_end, az > 8).astype(jnp.int32)
        + has_left.astype(jnp.int32)
        + jnp.minimum(az, 2)
        + jnp.logical_and(is_worker, region == 1).astype(jnp.int32)
    )
    pl.when(count > 0)(lambda: pl.semaphore_wait(barrier, count))

    pl.when(next_first)(lambda: signal(ready.at[1], az=nxt))
    pl.when(prev_first)(lambda: signal(ready.at[0], az=prv))
    pl.when(high_end)(lambda: signal(ready.at[6], az=az - 3))

    @pl.when(is_worker)
    def _():
        signal(ready.at[5], az=0)
        pl.when(az == 2)(lambda: signal(ready.at[5], az=1))
        pl.when(region == 1)(lambda: signal(ready.at[5], region=0))

    def strip_source(q):
        return state.at[1 - region if q == 0 else 2, iface]

    strip_copies = [
        remote(strip_source(q), strips.at[az], strip_send, strip_recv, az=1 + q)
        for q in range(2)
    ]
    def start_all(copies):
        for c in copies:
            c.start()

    pl.when(az > 2)(lambda: start_all(strip_copies))

    far = (high_end, low_end)
    neighbour = (nxt, prv)

    def edge_source(d, c):
        return state.at[:, pl.ds(c * rows, rows), pl.ds(7 - 7 * d, 1), :]

    def edge_copy(d, c):
        return remote(
            edge_source(d, c), edges.at[d, :, pl.ds(c * rows, rows)],
            edge_send.at[d], edge_recv.at[d, c], az=neighbour[d],
        )

    round_about = (
        jnp.where(az < 8, jnp.where(odd, 5, 8), 5),
        jnp.where(az < 4, 7, jnp.where(az < 12, 5, 6)),
    )
    rest_inner = (jnp.logical_and(high_end, az > 8), jnp.logical_and(low_end, az == 0))

    def detour_copy(d, c):
        way = jnp.where(c < round_about[d], 3, 2 - d)
        return remote(
            edge_source(d, c), hop.at[c], edge_send.at[d], hop_recv.at[c],
            az=az - way if d == 0 else az + way,
        )

    upward = jnp.logical_or(lax.rem(y, 2) == 0, jnp.logical_or(az == 9, az == 13))
    onward_even = lax.rem(az + 4 - y, n_az)
    onward_odd = lax.rem(az + n_az - 1 - y, n_az)

    def onward_copy(d, c):
        return remote(
            hop.at[c], edges.at[d, :, pl.ds(c * rows, rows)], hop_send.at[c], edge_recv.at[d, c],
            az=onward_even if d == 0 else onward_odd,
        )

    def start_part(d, first, last):
        @pl.loop(first, last)
        def _(c):
            detour = jnp.logical_and(far[d], jnp.logical_or(c < round_about[d], rest_inner[d]))
            pl.when(detour)(lambda: detour_copy(d, c).start())
            pl.when(jnp.logical_not(detour))(lambda: edge_copy(d, c).start())

    def start(d):
        start_part(d, 0, chunks)

    def pass_on(first, last):
        @pl.when(region == 1)
        def _():
            @pl.loop(first, last)
            def _(c):
                remote(hop.at[c], hop.at[c], hop_send.at[c], hop_recv.at[c], az=nxt).wait_recv()
                pl.when(upward)(lambda: onward_copy(0, c).start())
                pl.when(jnp.logical_not(upward))(lambda: onward_copy(1, c).start())

    last_straight = jnp.logical_and(az == 15, is_vapor)
    pl.when(jnp.logical_and(next_first, jnp.logical_not(last_straight)))(lambda: start(0))
    pl.when(prev_first)(
        lambda: start_part(1, jnp.where(low_end, round_about[1], 0), chunks)
    )

    pl.when(has_left)(lambda: signal(ready.at[3], ax=ax - 1))

    for c in loads:
        c.wait()

    pl.when(last_straight)(lambda: start(0))

    lane = lax.broadcasted_iota(jnp.int32, (8, 128), 1)
    first_lane = lane == 0
    last_lane = lane == 127
    sub = lax.broadcasted_iota(jnp.int32, (8, 128), 0)
    first_row = sub == 0
    last_row = sub == 7

    def pack(r, held):
        mine = lane == r
        before = lane == lax.rem(r + 127, 128)
        got = []
        for f in range(3):
            left = pltpu.roll(cells[f, r, :, :128], lax.rem(r + 127, 128), 1)
            right = pltpu.roll(cells[f, r, :, 128:], lax.rem(r + 1, 128), 1)
            got.append(jnp.where(before, left, held[2 * f]))
            got.append(jnp.where(mine, right, held[2 * f + 1]))
        return tuple(got)

    columns = lax.fori_loop(
        0, radial, pack, tuple(jnp.zeros((8, 128), jnp.float32) for _ in range(6)), unroll=8
    )
    for f in range(3):
        packed[0, f] = columns[2 * f]
        packed[1, f] = columns[2 * f + 1]

    to_left = remote(packed.at[0], sides.at[1], side_send.at[0], side_recv.at[1], ax=ax - 1)
    to_right = remote(packed.at[1], sides.at[0], side_send.at[1], side_recv.at[0], ax=ax + 1)

    @pl.when(has_left)
    def _():
        to_left.start()

    @pl.when(has_right)
    def _():
        pl.semaphore_wait(ready.at[3], 1)
        to_right.start()

    @pl.when(az < 3)
    def _():
        later = jnp.where(az == 0, 2, 2 - az + jnp.where(is_vapor, 1, 0))
        pl.when(later > 0)(lambda: pl.semaphore_wait(ready.at[5], later))
        for q in range(2):
            pl.when(az != 1 + q)(strip_copies[q].start)

    @pl.when(next_later)
    def _():
        pl.semaphore_wait(ready.at[0], 1)
        start(0)

    @pl.when(low_end)
    def _():
        pl.semaphore_wait(ready.at[6], 1)
        pl.when(prev_first)(lambda: start_part(1, 0, round_about[1]))

    def start_late():
        pl.semaphore_wait(ready.at[1], 1)
        start(1)

    pl.when(swap_high)(start_late)

    @pl.when(has_left)
    def _():
        to_right.wait_recv()

    @pl.when(jnp.logical_not(has_left))
    def _():
        sides[0] = jnp.zeros((3, 8, 128), jnp.float32)

    @pl.when(has_right)
    def _():
        to_left.wait_recv()

    @pl.when(jnp.logical_not(has_right))
    def _():
        sides[1] = jnp.zeros((3, 8, 128), jnp.float32)

    in_even = lax.rem(lane, 2) == 0
    for f in range(3):
        from_left, from_right = sides[0, f], sides[1, f]
        packed_in[0, f] = jnp.where(in_even, from_left, from_right)
        packed_in[1, f] = jnp.where(in_even, from_right, from_left)

    def pick(vapor, wick):
        return jnp.where(is_vapor, jnp.float32(vapor), jnp.float32(wick))

    press = pick(1.0, 0.6)
    visc = pick(0.3, 0.05)
    fric = pick(0.1, 2.0)
    sound = pick(1.5, 0.8)
    pdiff = pick(0.2, 0.4)
    advect = pick(1.0, 0.5)
    zero = jnp.float32(0.0)

    def cell_row(r, parity):
        inner = jnp.maximum(r - 1, 0)
        outer = jnp.minimum(r + 1, radial - 1)
        to_first = lax.rem(128 - r, 128)
        center, laplace, gradient = [], [], []
        for f in range(3):
            c = [cells[f, r, :, :128], cells[f, r, :, 128:]]
            plus = [pltpu.roll(c[0], 127, 1), pltpu.roll(c[1], 127, 1)]
            minus = [pltpu.roll(c[0], 1, 1), pltpu.roll(c[1], 1, 1)]
            beside = pltpu.roll(packed_in[parity, f], to_first, 1)
            ax_plus = [
                jnp.where(last_lane, plus[1], plus[0]),
                jnp.where(last_lane, beside, plus[1]),
            ]
            ax_minus = [
                jnp.where(first_lane, beside, minus[0]),
                jnp.where(first_lane, minus[0], minus[1]),
            ]
            laps, grads = [], []
            for h in range(2):
                lanes = pl.ds(128 * h, 128)
                az_plus = jnp.where(last_row, zero, pltpu.roll(c[h], 7, 0))
                az_minus = jnp.where(first_row, zero, pltpu.roll(c[h], 1, 0))
                laps.append(
                    cells[f, outer, :, lanes] + cells[f, inner, :, lanes]
                    + az_plus + az_minus + ax_plus[h] + ax_minus[h] - 6.0 * c[h]
                )
                grads.append(0.5 * (ax_plus[h] - ax_minus[h]))
            center.append(c)
            laplace.append(laps)
            gradient.append(grads)
        for h in range(2):
            lanes = pl.ds(128 * h, 128)
            t, p, u = center[0][h], center[1][h], center[2][h]
            out[0, r, :, lanes] = t + dt * (
                kappa[r, :, lanes] * laplace[0][h] - advect * u * gradient[0][h]
            )
            out[1, r, :, lanes] = p + dt * (
                -sound * gradient[2][h] + pdiff * laplace[1][h]
            )
            out[2, r, :, lanes] = u + dt * (
                -press * gradient[1][h] + visc * laplace[2][h] - fric * u
            )

    turns = radial // unroll
    at_end = jnp.logical_or(y == 0, y == 3)
    busy = jnp.logical_and(
        jnp.logical_and(at_end, az > 4), az < 15
    )

    @pl.loop(0, turns)
    def _(i):
        for k in range(unroll):
            cell_row(i * unroll + k, k % 2)

        pl.when(jnp.logical_and(az == 12, i == turns // 4 - 1))(start_late)
        pl.when(jnp.logical_and(az == 0, i == 3 * turns // 4 - 1))(start_late)
        quarter = lax.div(i + 1, turns // 4)

        @pl.when(lax.rem(i + 1, turns // 4) == 0)
        def _():
            pl.when(jnp.logical_and(busy, quarter < 4))(
                lambda: pass_on(quarter - 1, jnp.where(quarter < 3, quarter, quarter + 1))
            )
            pl.when(jnp.logical_and(az == 15, quarter == 3))(lambda: pass_on(0, 1))
            pl.when(jnp.logical_and(jnp.logical_and(inner, az > 8), quarter < 4))(
                lambda: pass_on(round_about[0] + quarter - 1, round_about[0] + quarter)
            )

    mine = jnp.where(y == 0, round_about[0], round_about[1])
    pl.when(at_end)(lambda: pass_on(jnp.where(busy, 4, (az == 15).astype(jnp.int32)), mine))

    @pl.when(is_worker)
    def _():
        strips[az] = jnp.where(az == 1, cells[1 - region, iface], cells[2, iface])
        others = strips.at[pl.ds(0, 15)]
        remote(others, others, strip_send, strip_recv, az=az).wait_recv()
        signal(ready.at[4], region=1 - region)
        for h in range(2):
            shift = placement[pl.ds(h, 1), :]
            shift = jnp.where(is_vapor, lax.rem(128 - shift, 128), shift)
            circle = strips[:, :, pl.ds(128 * h, 128)].reshape(128, 128)
            for bit in range(7):
                step = 1 << bit
                if step < 8:
                    rolled = pltpu.roll(circle, 128 - step, 0)
                else:
                    rolled = jnp.concatenate([circle[step:], circle[:step]], axis=0)
                circle = jnp.where(lax.rem(lax.div(shift, step), 2) == 1, rolled, circle)
            turned[:, :, pl.ds(128 * h, 128)] = circle.reshape(16, 8, 128)
        pl.semaphore_wait(ready.at[4], 1)

        @pl.loop(0, n_az)
        def _(j):
            remote(
                turned.at[j], facing.at[az - 1], turn_send, turn_recv.at[az - 1],
                az=j, region=1 - region,
            ).start()

    pl.when(jnp.logical_and(inner, az == 1))(lambda: pass_on(round_about[1], chunks))

    weights = (None, pdiff, visc)

    @pl.loop(0, chunks)
    def _(c):
        edge_copy(0, c).wait_recv()
        edge_copy(1, c).wait_recv()

        @pl.loop(0, rows // unroll)
        def _(i):
            for k in range(unroll):
                r = c * rows + i * unroll + k
                for h in range(2):
                    lanes = pl.ds(128 * h, 128)
                    for f in range(3):
                        beyond = jnp.where(
                            last_row,
                            edges[1, f, r, :, lanes],
                            jnp.where(first_row, edges[0, f, r, :, lanes], zero),
                        )
                        weight = kappa[r, :, lanes] if f == 0 else weights[f]
                        out[f, r, :, lanes] += dt * (weight * beyond)

    for q in range(2):
        remote(facing.at[q], facing.at[q], turn_send, turn_recv.at[q], az=q).wait_recv()

    for h in range(2):
        lanes = pl.ds(128 * h, 128)
        own_t, own_p, own_u = [cells[f, iface, :, lanes] for f in range(3)]
        first, second = facing[0, :, lanes], facing[1, :, lanes]
        t_wick = jnp.where(is_vapor, first, own_t)
        p_vapor = jnp.where(is_vapor, own_p, first)
        u_vapor = jnp.where(is_vapor, own_u, second)
        u_wick = jnp.where(is_vapor, second, own_u)
        evap = 2.0 * (t_wick - 0.5 * p_vapor)
        shear = 1.5 * (u_vapor - u_wick)
        out[0, iface, :, lanes] += dt * jnp.where(is_vapor, 0.5 * evap, -evap)
        out[1, iface, :, lanes] += dt * jnp.where(is_vapor, evap, -0.5 * evap)
        out[2, iface, :, lanes] += dt * jnp.where(is_vapor, -shear, 0.5 * shear)
        zone = jnp.broadcast_to(zones[pl.ds(h, 1), :], (8, 128))
        wall = cells[0, radial - 1, :, lanes]
        heat = jnp.where(
            zone == 0, jnp.float32(2.0), jnp.where(zone == 2, -1.5 * (wall + 1.0), 0.0)
        )
        out[0, radial - 1, :, lanes] += dt * jnp.where(is_vapor, 0.0, heat)

    for d in range(2):
        remote(edges.at[d], edges.at[d], edge_send.at[d], edge_recv.at[d, 0], az=nxt).wait_send()

    @pl.when(jnp.logical_or(inner, jnp.logical_and(region == 1, at_end)))
    def _():
        @pl.loop(jnp.where(at_end, 0, jnp.where(az == 1, round_about[1], round_about[0])), jnp.where(at_end, mine, chunks))
        def _(c):
            onward_copy(0, c).wait_send()

    pl.when(has_left)(to_left.wait_send)
    pl.when(has_right)(to_right.wait_send)
    @pl.when(is_worker)
    def _():
        strip_copies[0].wait_send()
        remote(turned, turned, turn_send, turn_recv.at[0], az=az).wait_send()

    @pl.when(jnp.logical_not(is_worker))
    def _():
        two = facing
        remote(two, two, strip_send, strip_recv, az=az).wait_send()


def store_kernel(new, out, sems):
    copies = [
        pltpu.make_async_copy(new.at[f], out.at[f], sems.at[f]) for f in range(3)
    ]
    for c in copies:
        c.start()
    for c in copies:
        c.wait()


def on_device(state, conduct, zones, placement):
    fields = state[0]
    f32 = jnp.float32
    shape = fields.shape
    radial, az_cells, ax_cells = shape[1:]
    hbm = pl.BlockSpec(memory_space=pltpu.HBM)
    vmem = pl.BlockSpec(memory_space=pltpu.VMEM)
    dma = pltpu.SemaphoreType.DMA
    new = pl.pallas_call(
        step_kernel,
        out_shape=pltpu.VMEM(shape, f32),
        in_specs=[hbm] * 4,
        out_specs=vmem,
        scratch_shapes=[
            pltpu.VMEM((2, 128), jnp.int32),
            pltpu.VMEM((2, 128), jnp.int32),
            pltpu.VMEM(shape, f32),
            pltpu.VMEM(shape[1:], f32),
            pltpu.VMEM((2, 3, radial, 1, ax_cells), f32),
            pltpu.VMEM((chunks, 3, radial // chunks, 1, ax_cells), f32),
            pltpu.VMEM((2, 3, 8, 128), f32),
            pltpu.VMEM((2, 3, 8, 128), f32),
            pltpu.VMEM((2, 3, 8, 128), f32),
            pltpu.VMEM((16, 8, 256), f32),
            pltpu.VMEM((16, 8, 256), f32),
            pltpu.VMEM((2, 8, 256), f32),
            dma((4,)),
            dma((2,)),
            dma((2, chunks)),
            dma((chunks,)),
            dma((chunks,)),
            dma((2,)),
            dma((2,)),
            dma,
            dma,
            dma,
            dma((2,)),
            pltpu.SemaphoreType.REGULAR((7,)),
        ],
        compiler_params=pltpu.CompilerParams(
            collective_id=0, has_side_effects=True, vmem_limit_bytes=24 << 20
        ),
        cost_estimate=pl.CostEstimate(
            flops=40 * fields.size, bytes_accessed=4 * 7 * conduct.size, transcendentals=0
        ),
    )(*(
        pltpu.with_memory_space_constraint(x, pltpu.HBM)
        for x in (fields, conduct[0], zones.reshape(2, 128), placement.reshape(2, 128))
    ))
    result = pl.pallas_call(
        store_kernel,
        out_shape=jax.ShapeDtypeStruct(shape, f32),
        in_specs=[vmem],
        out_specs=hbm,
        scratch_shapes=[dma((3,))],
        compiler_params=pltpu.CompilerParams(vmem_limit_bytes=1 << 20),
    )(pltpu.with_memory_space_constraint(new, pltpu.VMEM))
    return result[None]


def solution(mesh):
    return jax.shard_map(
        on_device,
        mesh=mesh,
        in_specs=(
            P("region", None, None, "az", "ax"),
            P("region", None, "az", "ax"),
            P("ax"),
            P("ax"),
        ),
        out_specs=P("region", None, None, "az", "ax"),
        check_vma=False,
    )
```

```python
import functools
import jax
import jax.numpy as jnp
from jax import lax
from jax.experimental import pallas as pl
from jax.experimental.pallas import tpu as pltpu
from jax.sharding import PartitionSpec as P

MESH = pl.DeviceIdType.MESH
dt = 0.05
chunks = 8
unroll = 8


def step_kernel(
    state, conduct, zone_ref, place_ref, out,
    zones, placement, cells, kappa, edges, hop, packed, packed_in, sides, strips, turned, facing,
    load_sem, edge_send, edge_recv, hop_send, hop_recv, side_send, side_recv,
    strip_send, strip_recv, turn_send, turn_recv, ready,
):
    region = lax.axis_index("region")
    ax = lax.axis_index("ax")
    az = lax.axis_index("az")
    n_az = lax.axis_size("az")
    n_ax = lax.axis_size("ax")
    radial = state.shape[1]
    rows = radial // chunks
    is_vapor = region == 0
    y = lax.rem(az, 4)
    nxt = lax.rem(az + 1, n_az)
    prv = lax.rem(az + n_az - 1, n_az)
    odd = lax.rem(ax, 2) == 1
    has_left = ax > 0
    has_right = ax < n_ax - 1
    is_worker = jnp.logical_or(az == 1, az == 2)
    iface = jnp.where(is_vapor, radial - 1, 0)
    swap_high = jnp.logical_or(az == 11, az == 15)
    next_later = jnp.logical_not(
        jnp.logical_or(swap_high, jnp.logical_or(az == 10, az == 14))
    )
    prev_later = jnp.logical_or(jnp.logical_or(az == 0, az == 12), swap_high)
    next_first = jnp.logical_not(next_later)
    prev_first = jnp.logical_not(prev_later)
    even = lax.rem(ax, 2) == 0
    low_end = jnp.logical_and(y == 0, region == 1)
    high_end = jnp.logical_and(y == 3, region == 1)
    inner = jnp.logical_and(
        region == 1, jnp.logical_or(az == 1, jnp.logical_or(az == 9, az == 13))
    )

    def signal(sem, **device):
        pl.semaphore_signal(sem, inc=1, device_id=device, device_id_type=MESH)

    def remote(src, dst, send, recv, **device):
        return pltpu.make_async_remote_copy(
            src_ref=src, dst_ref=dst, send_sem=send, recv_sem=recv,
            device_id=device, device_id_type=MESH,
        )

    barrier = pltpu.get_barrier_semaphore()
    pl.when(next_later)(lambda: signal(barrier, az=nxt))
    pl.when(prev_later)(lambda: signal(barrier, az=prv))
    pl.when(low_end)(lambda: signal(barrier, az=az + 3))
    pl.when(jnp.logical_and(inner, az > 8))(lambda: signal(barrier, az=az + 2))
    pl.when(even)(lambda: signal(barrier, ax=ax + 1))
    pl.when(jnp.logical_and(odd, has_right))(lambda: signal(barrier, ax=ax + 1))

    loads = [
        pltpu.make_async_copy(src, dst, load_sem.at[i])
        for i, (src, dst) in enumerate(
            ((state, cells), (conduct, kappa), (zone_ref, zones), (place_ref, placement))
        )
    ]
    for c in loads:
        c.start()

    @pl.when(az < 2)
    def _():
        signal(barrier, az=2)
        pl.when(az == 0)(lambda: signal(barrier, az=1))

    @pl.when(is_worker)
    def _():
        pl.when(is_vapor)(lambda: signal(barrier, region=1))

        @pl.loop(3, n_az)
        def _(j):
            signal(barrier, az=j)

    count = (
        next_first.astype(jnp.int32)
        + prev_first.astype(jnp.int32)
        + high_end.astype(jnp.int32)
        + jnp.logical_and(high_end, az > 8).astype(jnp.int32)
        + has_left.astype(jnp.int32)
        + jnp.minimum(az, 2)
        + jnp.logical_and(is_worker, region == 1).astype(jnp.int32)
    )
    pl.when(count > 0)(lambda: pl.semaphore_wait(barrier, count))

    pl.when(next_first)(lambda: signal(ready.at[1], az=nxt))
    pl.when(prev_first)(lambda: signal(ready.at[0], az=prv))
    pl.when(high_end)(lambda: signal(ready.at[6], az=az - 3))

    @pl.when(is_worker)
    def _():
        signal(ready.at[5], az=0)
        pl.when(az == 2)(lambda: signal(ready.at[5], az=1))
        pl.when(region == 1)(lambda: signal(ready.at[5], region=0))

    def strip_source(q):
        return state.at[1 - region if q == 0 else 2, iface]

    strip_copies = [
        remote(strip_source(q), strips.at[az], strip_send, strip_recv, az=1 + q)
        for q in range(2)
    ]
    def start_all(copies):
        for c in copies:
            c.start()

    pl.when(az > 2)(lambda: start_all(strip_copies))

    far = (high_end, low_end)
    neighbour = (nxt, prv)

    def edge_source(d, c):
        return state.at[:, pl.ds(c * rows, rows), pl.ds(7 - 7 * d, 1), :]

    def edge_copy(d, c):
        return remote(
            edge_source(d, c), edges.at[d, :, pl.ds(c * rows, rows)],
            edge_send.at[d], edge_recv.at[d, c], az=neighbour[d],
        )

    round_about = (
        jnp.where(az < 8, jnp.where(odd, 3, 8), 5),
        jnp.where(az < 4, 7, jnp.where(az < 12, 5, 6)),
    )
    rest_inner = (jnp.logical_and(high_end, az > 8), jnp.logical_and(low_end, az == 0))

    def detour_copy(d, c):
        way = jnp.where(c < round_about[d], 3, 2 - d)
        return remote(
            edge_source(d, c), hop.at[c], edge_send.at[d], hop_recv.at[c],
            az=az - way if d == 0 else az + way,
        )

    upward = jnp.logical_or(lax.rem(y, 2) == 0, jnp.logical_or(az == 9, az == 13))
    onward_even = lax.rem(az + 4 - y, n_az)
    onward_odd = lax.rem(az + n_az - 1 - y, n_az)

    def onward_copy(d, c):
        return remote(
            hop.at[c], edges.at[d, :, pl.ds(c * rows, rows)], hop_send.at[c], edge_recv.at[d, c],
            az=onward_even if d == 0 else onward_odd,
        )

    def start_part(d, first, last):
        @pl.loop(first, last)
        def _(c):
            detour = jnp.logical_and(far[d], jnp.logical_or(c < round_about[d], rest_inner[d]))
            pl.when(detour)(lambda: detour_copy(d, c).start())
            pl.when(jnp.logical_not(detour))(lambda: edge_copy(d, c).start())

    def start(d):
        start_part(d, 0, chunks)

    def pass_on(first, last):
        @pl.when(region == 1)
        def _():
            @pl.loop(first, last)
            def _(c):
                remote(hop.at[c], hop.at[c], hop_send.at[c], hop_recv.at[c], az=nxt).wait_recv()
                pl.when(upward)(lambda: onward_copy(0, c).start())
                pl.when(jnp.logical_not(upward))(lambda: onward_copy(1, c).start())

    last_straight = jnp.logical_and(az == 15, is_vapor)
    pl.when(jnp.logical_and(next_first, jnp.logical_not(last_straight)))(lambda: start(0))
    pl.when(prev_first)(
        lambda: start_part(1, jnp.where(low_end, round_about[1], 0), chunks)
    )

    pl.when(has_left)(lambda: signal(ready.at[3], ax=ax - 1))

    for c in loads:
        c.wait()

    pl.when(last_straight)(lambda: start(0))

    lane = lax.broadcasted_iota(jnp.int32, (8, 128), 1)
    first_lane = lane == 0
    last_lane = lane == 127
    sub = lax.broadcasted_iota(jnp.int32, (8, 128), 0)
    first_row = sub == 0
    last_row = sub == 7

    def pack(r, held):
        mine = lane == r
        before = lane == lax.rem(r + 127, 128)
        got = []
        for f in range(3):
            left = pltpu.roll(cells[f, r, :, :128], lax.rem(r + 127, 128), 1)
            right = pltpu.roll(cells[f, r, :, 128:], lax.rem(r + 1, 128), 1)
            got.append(jnp.where(before, left, held[2 * f]))
            got.append(jnp.where(mine, right, held[2 * f + 1]))
        return tuple(got)

    columns = lax.fori_loop(
        0, radial, pack, tuple(jnp.zeros((8, 128), jnp.float32) for _ in range(6)), unroll=8
    )
    for f in range(3):
        packed[0, f] = columns[2 * f]
        packed[1, f] = columns[2 * f + 1]

    to_left = remote(packed.at[0], sides.at[1], side_send.at[0], side_recv.at[1], ax=ax - 1)
    to_right = remote(packed.at[1], sides.at[0], side_send.at[1], side_recv.at[0], ax=ax + 1)

    @pl.when(has_left)
    def _():
        to_left.start()

    @pl.when(has_right)
    def _():
        pl.semaphore_wait(ready.at[3], 1)
        to_right.start()

    @pl.when(az < 3)
    def _():
        later = jnp.where(az == 0, 2, 2 - az + jnp.where(is_vapor, 1, 0))
        pl.when(later > 0)(lambda: pl.semaphore_wait(ready.at[5], later))
        for q in range(2):
            pl.when(az != 1 + q)(strip_copies[q].start)

    @pl.when(next_later)
    def _():
        pl.semaphore_wait(ready.at[0], 1)
        start(0)

    @pl.when(low_end)
    def _():
        pl.semaphore_wait(ready.at[6], 1)
        pl.when(prev_first)(lambda: start_part(1, 0, round_about[1]))

    def start_late():
        pl.semaphore_wait(ready.at[1], 1)
        start(1)

    pl.when(swap_high)(start_late)

    @pl.when(has_left)
    def _():
        to_right.wait_recv()

    @pl.when(jnp.logical_not(has_left))
    def _():
        sides[0] = jnp.zeros((3, 8, 128), jnp.float32)

    @pl.when(has_right)
    def _():
        to_left.wait_recv()

    @pl.when(jnp.logical_not(has_right))
    def _():
        sides[1] = jnp.zeros((3, 8, 128), jnp.float32)

    in_even = lax.rem(lane, 2) == 0
    for f in range(3):
        from_left, from_right = sides[0, f], sides[1, f]
        packed_in[0, f] = jnp.where(in_even, from_left, from_right)
        packed_in[1, f] = jnp.where(in_even, from_right, from_left)

    def pick(vapor, wick):
        return jnp.where(is_vapor, jnp.float32(vapor), jnp.float32(wick))

    press = pick(1.0, 0.6)
    visc = pick(0.3, 0.05)
    fric = pick(0.1, 2.0)
    sound = pick(1.5, 0.8)
    pdiff = pick(0.2, 0.4)
    advect = pick(1.0, 0.5)
    zero = jnp.float32(0.0)

    def cell_row(r, parity):
        inner = jnp.maximum(r - 1, 0)
        outer = jnp.minimum(r + 1, radial - 1)
        to_first = lax.rem(128 - r, 128)
        center, laplace, gradient = [], [], []
        for f in range(3):
            c = [cells[f, r, :, :128], cells[f, r, :, 128:]]
            plus = [pltpu.roll(c[0], 127, 1), pltpu.roll(c[1], 127, 1)]
            minus = [pltpu.roll(c[0], 1, 1), pltpu.roll(c[1], 1, 1)]
            beside = pltpu.roll(packed_in[parity, f], to_first, 1)
            ax_plus = [
                jnp.where(last_lane, plus[1], plus[0]),
                jnp.where(last_lane, beside, plus[1]),
            ]
            ax_minus = [
                jnp.where(first_lane, beside, minus[0]),
                jnp.where(first_lane, minus[0], minus[1]),
            ]
            laps, grads = [], []
            for h in range(2):
                lanes = pl.ds(128 * h, 128)
                az_plus = jnp.where(last_row, zero, pltpu.roll(c[h], 7, 0))
                az_minus = jnp.where(first_row, zero, pltpu.roll(c[h], 1, 0))
                laps.append(
                    cells[f, outer, :, lanes] + cells[f, inner, :, lanes]
                    + az_plus + az_minus + ax_plus[h] + ax_minus[h] - 6.0 * c[h]
                )
                grads.append(0.5 * (ax_plus[h] - ax_minus[h]))
            center.append(c)
            laplace.append(laps)
            gradient.append(grads)
        for h in range(2):
            lanes = pl.ds(128 * h, 128)
            t, p, u = center[0][h], center[1][h], center[2][h]
            out[0, r, :, lanes] = t + dt * (
                kappa[r, :, lanes] * laplace[0][h] - advect * u * gradient[0][h]
            )
            out[1, r, :, lanes] = p + dt * (
                -sound * gradient[2][h] + pdiff * laplace[1][h]
            )
            out[2, r, :, lanes] = u + dt * (
                -press * gradient[1][h] + visc * laplace[2][h] - fric * u
            )

    turns = radial // unroll
    at_end = jnp.logical_or(y == 0, y == 3)
    busy = jnp.logical_and(
        jnp.logical_and(at_end, az > 4), az < 15
    )

    @pl.loop(0, turns)
    def _(i):
        for k in range(unroll):
            cell_row(i * unroll + k, k % 2)

        pl.when(jnp.logical_and(az == 12, i == turns // 4 - 1))(start_late)
        pl.when(jnp.logical_and(az == 0, i == 3 * turns // 4 - 1))(start_late)
        quarter = lax.div(i + 1, turns // 4)

        @pl.when(lax.rem(i + 1, turns // 4) == 0)
        def _():
            pl.when(jnp.logical_and(busy, quarter < 4))(
                lambda: pass_on(quarter - 1, jnp.where(quarter < 3, quarter, quarter + 1))
            )
            pl.when(jnp.logical_and(az == 15, quarter == 3))(lambda: pass_on(0, 1))
            pl.when(jnp.logical_and(jnp.logical_and(inner, az > 8), quarter < 4))(
                lambda: pass_on(round_about[0] + quarter - 1, round_about[0] + quarter)
            )

    mine = jnp.where(y == 0, round_about[0], round_about[1])
    pl.when(at_end)(lambda: pass_on(jnp.where(busy, 4, (az == 15).astype(jnp.int32)), mine))

    @pl.when(is_worker)
    def _():
        strips[az] = jnp.where(az == 1, cells[1 - region, iface], cells[2, iface])
        others = strips.at[pl.ds(0, 15)]
        remote(others, others, strip_send, strip_recv, az=az).wait_recv()
        signal(ready.at[4], region=1 - region)
        for h in range(2):
            shift = placement[pl.ds(h, 1), :]
            shift = jnp.where(is_vapor, lax.rem(128 - shift, 128), shift)
            circle = strips[:, :, pl.ds(128 * h, 128)].reshape(128, 128)
            for bit in range(7):
                step = 1 << bit
                if step < 8:
                    rolled = pltpu.roll(circle, 128 - step, 0)
                else:
                    rolled = jnp.concatenate([circle[step:], circle[:step]], axis=0)
                circle = jnp.where(lax.rem(lax.div(shift, step), 2) == 1, rolled, circle)
            turned[:, :, pl.ds(128 * h, 128)] = circle.reshape(16, 8, 128)
        pl.semaphore_wait(ready.at[4], 1)

        @pl.loop(0, n_az)
        def _(j):
            remote(
                turned.at[j], facing.at[az - 1], turn_send, turn_recv.at[az - 1],
                az=j, region=1 - region,
            ).start()

    pl.when(jnp.logical_and(inner, az == 1))(lambda: pass_on(round_about[1], chunks))

    weights = (None, pdiff, visc)

    @pl.loop(0, chunks)
    def _(c):
        edge_copy(0, c).wait_recv()
        edge_copy(1, c).wait_recv()

        @pl.loop(0, rows // unroll)
        def _(i):
            for k in range(unroll):
                r = c * rows + i * unroll + k
                for h in range(2):
                    lanes = pl.ds(128 * h, 128)
                    for f in range(3):
                        beyond = jnp.where(
                            last_row,
                            edges[1, f, r, :, lanes],
                            jnp.where(first_row, edges[0, f, r, :, lanes], zero),
                        )
                        weight = kappa[r, :, lanes] if f == 0 else weights[f]
                        out[f, r, :, lanes] += dt * (weight * beyond)

    for q in range(2):
        remote(facing.at[q], facing.at[q], turn_send, turn_recv.at[q], az=q).wait_recv()

    for h in range(2):
        lanes = pl.ds(128 * h, 128)
        own_t, own_p, own_u = [cells[f, iface, :, lanes] for f in range(3)]
        first, second = facing[0, :, lanes], facing[1, :, lanes]
        t_wick = jnp.where(is_vapor, first, own_t)
        p_vapor = jnp.where(is_vapor, own_p, first)
        u_vapor = jnp.where(is_vapor, own_u, second)
        u_wick = jnp.where(is_vapor, second, own_u)
        evap = 2.0 * (t_wick - 0.5 * p_vapor)
        shear = 1.5 * (u_vapor - u_wick)
        out[0, iface, :, lanes] += dt * jnp.where(is_vapor, 0.5 * evap, -evap)
        out[1, iface, :, lanes] += dt * jnp.where(is_vapor, evap, -0.5 * evap)
        out[2, iface, :, lanes] += dt * jnp.where(is_vapor, -shear, 0.5 * shear)
        zone = jnp.broadcast_to(zones[pl.ds(h, 1), :], (8, 128))
        wall = cells[0, radial - 1, :, lanes]
        heat = jnp.where(
            zone == 0, jnp.float32(2.0), jnp.where(zone == 2, -1.5 * (wall + 1.0), 0.0)
        )
        out[0, radial - 1, :, lanes] += dt * jnp.where(is_vapor, 0.0, heat)

    for d in range(2):
        remote(edges.at[d], edges.at[d], edge_send.at[d], edge_recv.at[d, 0], az=nxt).wait_send()

    @pl.when(jnp.logical_or(inner, jnp.logical_and(region == 1, at_end)))
    def _():
        @pl.loop(jnp.where(at_end, 0, jnp.where(az == 1, round_about[1], round_about[0])), jnp.where(at_end, mine, chunks))
        def _(c):
            onward_copy(0, c).wait_send()

    pl.when(has_left)(to_left.wait_send)
    pl.when(has_right)(to_right.wait_send)
    @pl.when(is_worker)
    def _():
        strip_copies[0].wait_send()
        remote(turned, turned, turn_send, turn_recv.at[0], az=az).wait_send()

    @pl.when(jnp.logical_not(is_worker))
    def _():
        two = facing
        remote(two, two, strip_send, strip_recv, az=az).wait_send()


def store_kernel(new, out, sems):
    copies = [
        pltpu.make_async_copy(new.at[f], out.at[f], sems.at[f]) for f in range(3)
    ]
    for c in copies:
        c.start()
    for c in copies:
        c.wait()


def on_device(state, conduct, zones, placement):
    fields = state[0]
    f32 = jnp.float32
    shape = fields.shape
    radial, az_cells, ax_cells = shape[1:]
    hbm = pl.BlockSpec(memory_space=pltpu.HBM)
    vmem = pl.BlockSpec(memory_space=pltpu.VMEM)
    dma = pltpu.SemaphoreType.DMA
    new = pl.pallas_call(
        step_kernel,
        out_shape=pltpu.VMEM(shape, f32),
        in_specs=[hbm] * 4,
        out_specs=vmem,
        scratch_shapes=[
            pltpu.VMEM((2, 128), jnp.int32),
            pltpu.VMEM((2, 128), jnp.int32),
            pltpu.VMEM(shape, f32),
            pltpu.VMEM(shape[1:], f32),
            pltpu.VMEM((2, 3, radial, 1, ax_cells), f32),
            pltpu.VMEM((chunks, 3, radial // chunks, 1, ax_cells), f32),
            pltpu.VMEM((2, 3, 8, 128), f32),
            pltpu.VMEM((2, 3, 8, 128), f32),
            pltpu.VMEM((2, 3, 8, 128), f32),
            pltpu.VMEM((16, 8, 256), f32),
            pltpu.VMEM((16, 8, 256), f32),
            pltpu.VMEM((2, 8, 256), f32),
            dma((4,)),
            dma((2,)),
            dma((2, chunks)),
            dma((chunks,)),
            dma((chunks,)),
            dma((2,)),
            dma((2,)),
            dma,
            dma,
            dma,
            dma((2,)),
            pltpu.SemaphoreType.REGULAR((7,)),
        ],
        compiler_params=pltpu.CompilerParams(
            collective_id=0, has_side_effects=True, vmem_limit_bytes=24 << 20
        ),
        cost_estimate=pl.CostEstimate(
            flops=40 * fields.size, bytes_accessed=4 * 7 * conduct.size, transcendentals=0
        ),
    )(*(
        pltpu.with_memory_space_constraint(x, pltpu.HBM)
        for x in (fields, conduct[0], zones.reshape(2, 128), placement.reshape(2, 128))
    ))
    result = pl.pallas_call(
        store_kernel,
        out_shape=jax.ShapeDtypeStruct(shape, f32),
        in_specs=[vmem],
        out_specs=hbm,
        scratch_shapes=[dma((3,))],
        compiler_params=pltpu.CompilerParams(vmem_limit_bytes=1 << 20),
    )(pltpu.with_memory_space_constraint(new, pltpu.VMEM))
    return result[None]


def solution(mesh):
    return jax.shard_map(
        on_device,
        mesh=mesh,
        in_specs=(
            P("region", None, None, "az", "ax"),
            P("region", None, "az", "ax"),
            P("ax"),
            P("ax"),
        ),
        out_specs=P("region", None, None, "az", "ax"),
        check_vma=False,
    )
```
